256 devices in a mesh: seq: 32 (over x_hi, z, core), tp: 8 (over y, x_lo).
Axes of the slice: x: 4 (x_hi: 2, x_lo: 2; x = x_hi * 2 + x_lo), y: 4, z: 8, core: 2. Of those that a mesh axis runs over, the one named last changes fastest.
Arguments:
- projected: bfloat16 [3, 4096, 8192], P(None, 'tp', 'seq'), may hold values from -12 to 12
- filter_taps: bfloat16 [4096, 8192], P('tp', 'seq'), may hold values from -2.5 to 2.5
- short_weight: float32 [3, 4096, 3], P(None, 'tp'), may hold values from -3 to 3
- skip_bias: float32 [4096], P('tp'), may hold values from -3 to 3
- norm_gain: float32 [4096], replicated, may hold values from 0.1 to 1.9
- gate_weight: bfloat16 [5632, 4096], P(('seq', 'tp')), may hold values from -0.09375 to 0.09375
- up_weight: bfloat16 [5632, 4096], P(('seq', 'tp')), may hold values from -0.09375 to 0.09375
- down_weight: bfloat16 [5632, 4096], P(('seq', 'tp')), may hold values from -0.078125 to 0.078125
Outputs:
- mixed: bfloat16 [4096, 8192], P('tp', 'seq')
The draws below stay inside these ranges and needn't reach their ends.
All inputs are finite; a program needn't handle non-finite values.
Results may differ from the reference program's by a relative error of at most 0.018.
Values may be sent and summed in bfloat16 or wider, within the bound.
No kernel may reach another device: no remote copies, remote signals or barrier semaphores. Data moves between devices by JAX's collectives and lax.ppermute only.
A program may use at most 128 MiB of HBM per device.

```python
import math
import jax
import jax.numpy as jnp
from jax import lax

MODEL_CHANNELS = 4096
FF = 5632
SEQUENCE_LENGTH = 8192


def draw_projected(key, part):
    key = jax.random.fold_in(key, 5)
    noise_key, scale_key = jax.random.split(key)
    noise_values = jnp.clip(jax.random.normal(noise_key, (3, MODEL_CHANNELS, SEQUENCE_LENGTH), jnp.float32), -4.0, 4.0)
    row_scale = jnp.exp(jax.random.uniform(scale_key, (SEQUENCE_LENGTH,), jnp.float32, math.log(0.3), math.log(3.0)))
    scales = jnp.concatenate([row_scale[None, :], jnp.ones((2, SEQUENCE_LENGTH), jnp.float32)], axis=0)
    return (noise_values * scales[:, None, :]).astype(jnp.bfloat16)


def draw_filter_taps(key, part):
    key = jax.random.fold_in(key, 7)
    split_keys = jax.random.split(key, 7)
    position_grid = jnp.arange(SEQUENCE_LENGTH, dtype=jnp.float32)[None, :]
    slow_share = 0.5
    noise_values = jnp.clip(jax.random.normal(split_keys[0], (MODEL_CHANNELS, SEQUENCE_LENGTH), jnp.float32), -4.0, 4.0)
    slow_mask = jax.random.uniform(split_keys[1], (MODEL_CHANNELS,), jnp.float32) < slow_share
    slow_rate = jnp.exp(jax.random.uniform(split_keys[2], (MODEL_CHANNELS,), jnp.float32, math.log(0.25), math.log(2.0))) / SEQUENCE_LENGTH
    fast_rate = jnp.exp(jax.random.uniform(split_keys[3], (MODEL_CHANNELS,), jnp.float32, math.log(2.0 / SEQUENCE_LENGTH), math.log(1.0 / 30.0)))
    decay_rate = jnp.where(slow_mask, slow_rate, fast_rate)
    spike_position = jax.random.randint(split_keys[4], (MODEL_CHANNELS, 4), 1, SEQUENCE_LENGTH).astype(jnp.float32)
    spike_mask = jax.random.uniform(split_keys[5], (MODEL_CHANNELS, 4), jnp.float32, 0.5, 0.8)
    decay_profile = jnp.exp(-decay_rate[:, None] * position_grid)
    for spike_index in range(4):
        decay_profile = decay_profile * jnp.where(position_grid >= spike_position[:, spike_index:spike_index + 1], spike_mask[:, spike_index:spike_index + 1], 1.0)
    energy = jnp.expm1(-2.0 * decay_rate * SEQUENCE_LENGTH) / jnp.expm1(-2.0 * decay_rate)
    channel_scale = jnp.exp(jax.random.uniform(split_keys[6], (MODEL_CHANNELS,), jnp.float32, math.log(0.5), math.log(2.0)))
    return (noise_values * decay_profile * (channel_scale / jnp.sqrt(energy))[:, None]).astype(jnp.bfloat16)


def shard_levels(stream_key, shape, shards, low, top_value):
    gain = 1.0
    for position, blocks in shards:
        steps = jax.random.uniform(jax.random.fold_in(jax.random.fold_in(stream_key, 6), position), (blocks,), jnp.float32, low / len(shards), top_value / len(shards))
        gain = gain * jnp.repeat(jnp.exp(steps), shape[position] // blocks).reshape((-1,) + (1,) * (len(shape) - 1 - position))
    return gain


def scatter_about(key, shape, scale, most, shards=(), kind=jnp.bfloat16):
    entries = scale * jax.random.normal(key, shape, jnp.float32)
    if shards:
        entries = entries * shard_levels(key, shape, shards, -0.22, 0.18)
    return jnp.clip(entries, -most, most).astype(kind)


def setup_inputs(seed: int = 0) -> dict:
    arg_keys = jax.random.split(jax.random.key(seed), 9)
    return {
        "projected": draw_projected(jax.random.fold_in(arg_keys[8], 71), 0),
        "filter_taps": draw_filter_taps(jax.random.fold_in(arg_keys[8], 71), 0),
        "short_weight": scatter_about(arg_keys[2], (3, MODEL_CHANNELS, 3), 0.6, 3.0, ((1, 8),), jnp.float32),
        "skip_bias": scatter_about(arg_keys[3], (MODEL_CHANNELS,), 0.7, 3.0, ((0, 8),), jnp.float32),
        "norm_gain": jnp.clip(1.0 + 0.18 * jax.random.normal(arg_keys[4], (MODEL_CHANNELS,), jnp.float32), 0.1, 1.9),
        "gate_weight": scatter_about(arg_keys[5], (FF, MODEL_CHANNELS), MODEL_CHANNELS ** -0.5, 0.09375, ((0, 256),)),
        "up_weight": scatter_about(arg_keys[6], (FF, MODEL_CHANNELS), MODEL_CHANNELS ** -0.5, 0.09375, ((0, 256),)),
        "down_weight": scatter_about(arg_keys[7], (FF, MODEL_CHANNELS), FF ** -0.5, 0.078125, ((0, 256),)),
    }


EPSILON = 1e-06

def short_filter(signal, weights):
    extent = signal.shape[2]
    padded = jnp.pad(signal, ((0, 0), (0, 0), (2, 0)))
    return weights[:, :, 0:1] * padded[:, :, 2:] + weights[:, :, 1:2] * padded[:, :, 1:extent + 1] + weights[:, :, 2:3] * padded[:, :, 0:extent]

def reference(projected, filter_taps, short_weight, skip_bias, norm_gain, gate_weight, up_weight, down_weight):
    model_width = projected.shape[1]
    seq_len = projected.shape[2]
    channel_block = math.gcd(model_width, 256)

    def mix_block(block_index):
        begin_at = (block_index * channel_block).astype(jnp.int32)
        projections = lax.dynamic_slice_in_dim(projected, begin_at, channel_block, 1).astype(jnp.float32)
        weights = lax.dynamic_slice_in_dim(short_weight, begin_at, channel_block, 1)
        filter_rows = lax.dynamic_slice_in_dim(filter_taps, begin_at, channel_block, 0).astype(jnp.float32)
        bias_part = lax.dynamic_slice_in_dim(skip_bias, begin_at, channel_block, 0)
        shorts = short_filter(projections, weights)
        gated_low = (shorts[1] * shorts[2]).astype(jnp.bfloat16)
        gated_term = lax.optimization_barrier(gated_low).astype(jnp.float32)
        length_two = 2 * seq_len
        spectrum = jnp.fft.rfft(gated_term, n=length_two, axis=1) * jnp.fft.rfft(filter_rows, n=length_two, axis=1)
        long_part = jnp.fft.irfft(spectrum, n=length_two, axis=1)[:, :seq_len]
        mixed_term = lax.optimization_barrier((long_part + bias_part[:, None] * gated_term).astype(jnp.bfloat16))
        return (shorts[0] * mixed_term.astype(jnp.float32)).astype(jnp.bfloat16)
    hyena_out = lax.map(mix_block, jnp.arange(model_width // channel_block, dtype=jnp.int32)).reshape(model_width, seq_len)
    hyena_wide = hyena_out.astype(jnp.float32)
    mean_square = lax.optimization_barrier(jnp.mean(hyena_wide * hyena_wide, axis=0))
    normed = (hyena_wide * lax.rsqrt(mean_square + EPSILON)[None, :] * norm_gain[:, None]).astype(jnp.bfloat16)
    token_span = math.gcd(seq_len, 2048)

    def feed_block(block_index):
        begin_at = (block_index * token_span).astype(jnp.int32)
        columns = lax.dynamic_slice_in_dim(normed, begin_at, token_span, 1)
        gate_sum = jnp.dot(gate_weight, columns, preferred_element_type=jnp.float32)
        up_sum = jnp.dot(up_weight, columns, preferred_element_type=jnp.float32)
        hidden = (jax.nn.silu(gate_sum) * up_sum).astype(jnp.bfloat16)
        return jnp.dot(down_weight.T, hidden, preferred_element_type=jnp.float32)
    feed_out = lax.map(feed_block, jnp.arange(seq_len // token_span, dtype=jnp.int32))
    feed_out = jnp.transpose(feed_out, (1, 0, 2)).reshape(model_width, seq_len)
    return (hyena_wide + feed_out).astype(jnp.bfloat16)
```

```python
import math

import jax
import jax.numpy as jnp
from jax import lax
from jax.sharding import Mesh
from jax.sharding import PartitionSpec as P

EPSILON = 1e-06
HIGHEST = lax.Precision.HIGHEST
SEQ = ("xh", "z", "core")
TP = ("y", "xl")


def short_filter(signal, weights, leading):
    extent = signal.shape[2]
    padded = jnp.concatenate([leading, signal], axis=2)
    return (
        weights[:, :, 0:1] * padded[:, :, 2:]
        + weights[:, :, 1:2] * padded[:, :, 1 : extent + 1]
        + weights[:, :, 2:3] * padded[:, :, 0:extent]
    )


def fourier_tables(half_rows, columns):
    full_rows = 2 * half_rows
    length_total = full_rows * columns
    row_freq = jnp.arange(full_rows, dtype=jnp.int32)[:, None]
    row_place = jnp.arange(half_rows, dtype=jnp.int32)[None, :]
    column_place = jnp.arange(columns, dtype=jnp.int32)
    row_angle = (row_freq * row_place % full_rows).astype(jnp.float32) * (2.0 * math.pi / full_rows)
    column_angle = (column_place[:, None] * column_place[None, :] % columns).astype(jnp.float32) * (
        2.0 * math.pi / columns
    )
    twist_angle = (row_freq * column_place[None, :]).astype(jnp.float32) * (
        2.0 * math.pi / length_total
    )
    return (
        jnp.cos(row_angle),
        jnp.sin(row_angle),
        jnp.cos(column_angle),
        jnp.sin(column_angle),
        jnp.cos(twist_angle),
        jnp.sin(twist_angle),
    )


def apply_rows(factor_table, signal):
    return jnp.einsum("kn,bnm->bkm", factor_table, signal, precision=HIGHEST)


def apply_columns(signal, factor_table):
    return jnp.einsum("bkn,nj->bkj", signal, factor_table, precision=HIGHEST)


def long_mixing(gated_term, filter_rows, bias_part):
    channels, seq_len = gated_term.shape
    columns = math.gcd(seq_len, 128)
    half_rows = seq_len // columns
    row_cosine, row_sine, column_cosine, column_sine, twist_cosine, twist_sine = fourier_tables(
        half_rows, columns
    )
    signals = (
        jnp.concatenate([gated_term, filter_rows], axis=0)
        .astype(jnp.float32)
        .reshape(2 * channels, half_rows, columns)
    )
    first_real = apply_rows(row_cosine, signals)
    first_imag = -apply_rows(row_sine, signals)
    turned_real = first_real * twist_cosine + first_imag * twist_sine
    turned_imag = first_imag * twist_cosine - first_real * twist_sine
    spectrum_real = apply_columns(turned_real, column_cosine) + apply_columns(
        turned_imag, column_sine
    )
    spectrum_imag = apply_columns(turned_imag, column_cosine) - apply_columns(
        turned_real, column_sine
    )
    product_real = (
        spectrum_real[:channels] * spectrum_real[channels:]
        - spectrum_imag[:channels] * spectrum_imag[channels:]
    )
    product_imag = (
        spectrum_real[:channels] * spectrum_imag[channels:]
        + spectrum_imag[:channels] * spectrum_real[channels:]
    )
    back_real = apply_columns(product_real, column_cosine) - apply_columns(
        product_imag, column_sine
    )
    back_imag = apply_columns(product_imag, column_cosine) + apply_columns(
        product_real, column_sine
    )
    untwist_real = back_real * twist_cosine - back_imag * twist_sine
    untwist_imag = back_imag * twist_cosine + back_real * twist_sine
    result = (
        jnp.einsum("kn,bkm->bnm", row_cosine, untwist_real, precision=HIGHEST)
        - jnp.einsum("kn,bkm->bnm", row_sine, untwist_imag, precision=HIGHEST)
    ) / (2.0 * seq_len)
    long_part = result.reshape(channels, seq_len)
    return (long_part + bias_part[:, None] * gated_term.astype(jnp.float32)).astype(jnp.bfloat16)


def gather_weights(gate_weight, up_weight, down_weight):
    rows, width = gate_weight.shape
    pair_pad = -(2 * rows) % 16
    mine = jnp.concatenate([gate_weight, up_weight, down_weight], axis=0)
    theirs = lax.ppermute(mine, "xh", [(0, 1), (1, 0)])
    blank = jnp.zeros((pair_pad, width), mine.dtype)
    pieces = []
    for part in range(3):
        span = slice(part * rows, (part + 1) * rows)
        pieces += [mine[span], theirs[span], blank]
    first = jnp.concatenate(pieces[:6], axis=0)
    second = jnp.concatenate(pieces[6:], axis=0)
    gate_up = lax.all_gather(first, ("z", "core"), axis=0, tiled=True)
    down = lax.all_gather(second, ("z", "core"), axis=0, tiled=True)
    return gate_up, down, 2 * rows + pair_pad


def per_device(
    projected, filter_taps, short_weight, skip_bias, norm_gain, gate_weight, up_weight, down_weight
):
    groups = lax.axis_size(SEQ)
    members = lax.axis_size(TP)
    local_width, block_len = filter_taps.shape
    per_group = local_width // groups
    seq_len = groups * block_len
    offset = lax.axis_index(SEQ) * per_group
    bias_part = lax.dynamic_slice_in_dim(skip_bias, offset, per_group, 0)
    channel_weights = lax.dynamic_slice_in_dim(short_weight, offset, per_group, 1)

    sent = jnp.concatenate([projected[1:], filter_taps[None]], axis=0)
    sent = sent.reshape(3, groups, per_group, block_len).transpose(1, 0, 2, 3)
    here = lax.all_to_all(sent, SEQ, split_axis=0, concat_axis=0, tiled=True)

    edge = lax.ppermute(
        projected[0, :, block_len - 2 :].T, SEQ, [(i, i + 1) for i in range(groups - 1)]
    ).T
    query = short_filter(
        projected[:1].astype(jnp.float32), short_weight[:1], edge[None].astype(jnp.float32)
    )[0]

    gate_up, down, pair = gather_weights(gate_weight, up_weight, down_weight)

    here = here.transpose(1, 2, 0, 3).reshape(3, per_group, seq_len)
    shorts = short_filter(
        here[:2].astype(jnp.float32), channel_weights[1:], jnp.zeros((2, per_group, 2), jnp.float32)
    )
    gated_term = (shorts[0] * shorts[1]).astype(jnp.bfloat16)
    mixed_term = long_mixing(gated_term, here[2], bias_part)
    returned = mixed_term.reshape(per_group, groups, block_len).transpose(1, 0, 2)
    returned = lax.all_to_all(returned, SEQ, split_axis=0, concat_axis=0, tiled=True)
    hyena = (query * returned.reshape(local_width, block_len).astype(jnp.float32)).astype(
        jnp.bfloat16
    )

    copies = jnp.broadcast_to(hyena[None], (members, local_width, block_len))
    whole = lax.all_to_all(copies, TP, split_axis=0, concat_axis=0, tiled=True)
    whole = whole.reshape(members * local_width, block_len)
    wide = whole.astype(jnp.float32)
    mean_square = jnp.mean(wide * wide, axis=0)
    normed = (wide * lax.rsqrt(mean_square + EPSILON)[None, :] * norm_gain[:, None]).astype(
        jnp.bfloat16
    )
    sums = jnp.dot(gate_up, normed, preferred_element_type=jnp.float32)
    sums = sums.reshape(-1, 2, pair, block_len)
    hidden = (jax.nn.silu(sums[:, 0]) * sums[:, 1]).astype(jnp.bfloat16)
    partial_sum = lax.dot_general(
        down,
        hidden.reshape(-1, block_len),
        (((0,), (0,)), ((), ())),
        preferred_element_type=jnp.float32,
    ).astype(jnp.bfloat16)
    shares = lax.all_to_all(
        partial_sum.reshape(members, local_width, block_len),
        TP,
        split_axis=0,
        concat_axis=0,
        tiled=True,
    )
    feed_out = jnp.sum(shares.astype(jnp.float32), axis=0)
    return (hyena.astype(jnp.float32) + feed_out).astype(jnp.bfloat16)


def solution(mesh):
    fine = Mesh(mesh.devices.reshape(2, 8, 2, 4, 2), SEQ + TP)
    placed = (
        P(None, TP, SEQ),
        P(TP, SEQ),
        P(None, TP, None),
        P(TP),
        P(),
        P(SEQ + TP, None),
        P(SEQ + TP, None),
        P(SEQ + TP, None),
    )
    return jax.shard_map(
        per_device, mesh=fine, in_specs=placed, out_specs=P(TP, SEQ), check_vma=False
    )
```

```python
import math

import jax
import jax.numpy as jnp
from jax import lax
from jax.sharding import Mesh
from jax.sharding import PartitionSpec as P

EPSILON = 1e-06
HIGHEST = lax.Precision.HIGHEST
SEQ = ("xh", "z", "core")
TP = ("y", "xl")


def short_filter(signal, weights, leading):
    extent = signal.shape[2]
    padded = jnp.concatenate([leading, signal], axis=2)
    return (
        weights[:, :, 0:1] * padded[:, :, 2:]
        + weights[:, :, 1:2] * padded[:, :, 1 : extent + 1]
        + weights[:, :, 2:3] * padded[:, :, 0:extent]
    )


def fourier_tables(half_rows, columns):
    full_rows = 2 * half_rows
    length_total = full_rows * columns
    row_freq = jnp.arange(full_rows, dtype=jnp.int32)[:, None]
    row_place = jnp.arange(half_rows, dtype=jnp.int32)[None, :]
    column_place = jnp.arange(columns, dtype=jnp.int32)
    row_angle = (row_freq * row_place % full_rows).astype(jnp.float32) * (2.0 * math.pi / full_rows)
    column_angle = (column_place[:, None] * column_place[None, :] % columns).astype(jnp.float32) * (
        2.0 * math.pi / columns
    )
    twist_angle = (row_freq * column_place[None, :]).astype(jnp.float32) * (
        2.0 * math.pi / length_total
    )
    return (
        jnp.cos(row_angle),
        jnp.sin(row_angle),
        jnp.cos(column_angle),
        jnp.sin(column_angle),
        jnp.cos(twist_angle),
        jnp.sin(twist_angle),
    )


def apply_rows(factor_table, signal):
    return jnp.einsum("kn,bnm->bkm", factor_table, signal, precision=HIGHEST)


def apply_columns(signal, factor_table):
    return jnp.einsum("bkn,nj->bkj", signal, factor_table, precision=HIGHEST)


def long_mixing(gated_term, filter_rows, bias_part):
    channels, seq_len = gated_term.shape
    columns = math.gcd(seq_len, 128)
    half_rows = seq_len // columns
    row_cosine, row_sine, column_cosine, column_sine, twist_cosine, twist_sine = fourier_tables(
        half_rows, columns
    )
    signals = (
        jnp.concatenate([gated_term, filter_rows], axis=0)
        .astype(jnp.float32)
        .reshape(2 * channels, half_rows, columns)
    )
    first_real = apply_rows(row_cosine, signals)
    first_imag = -apply_rows(row_sine, signals)
    turned_real = first_real * twist_cosine + first_imag * twist_sine
    turned_imag = first_imag * twist_cosine - first_real * twist_sine
    spectrum_real = apply_columns(turned_real, column_cosine) + apply_columns(
        turned_imag, column_sine
    )
    spectrum_imag = apply_columns(turned_imag, column_cosine) - apply_columns(
        turned_real, column_sine
    )
    product_real = (
        spectrum_real[:channels] * spectrum_real[channels:]
        - spectrum_imag[:channels] * spectrum_imag[channels:]
    )
    product_imag = (
        spectrum_real[:channels] * spectrum_imag[channels:]
        + spectrum_imag[:channels] * spectrum_real[channels:]
    )
    back_real = apply_columns(product_real, column_cosine) - apply_columns(
        product_imag, column_sine
    )
    back_imag = apply_columns(product_imag, column_cosine) + apply_columns(
        product_real, column_sine
    )
    untwist_real = back_real * twist_cosine - back_imag * twist_sine
    untwist_imag = back_imag * twist_cosine + back_real * twist_sine
    result = (
        jnp.einsum("kn,bkm->bnm", row_cosine, untwist_real, precision=HIGHEST)
        - jnp.einsum("kn,bkm->bnm", row_sine, untwist_imag, precision=HIGHEST)
    ) / (2.0 * seq_len)
    long_part = result.reshape(channels, seq_len)
    return (long_part + bias_part[:, None] * gated_term.astype(jnp.float32)).astype(jnp.bfloat16)


def padded_rows(weight):
    rows = weight.shape[0]
    return jnp.pad(weight, ((0, -rows % 8), (0, 0)))


def swap(values, axis):
    return lax.ppermute(values, axis, [(0, 1), (1, 0)])


def spread_down(own):
    half = own.shape[0] // 2
    core = lax.axis_index("core")
    near = swap(lax.dynamic_slice_in_dim(own, core * half, half, 0), "xh")
    return near, swap(near, "core")


def down_product(weight, hidden):
    return lax.dot_general(
        weight, hidden, (((0,), (0,)), ((), ())), preferred_element_type=jnp.float32
    )


def per_device(
    projected, filter_taps, short_weight, skip_bias, norm_gain, gate_weight, up_weight, down_weight
):
    groups = lax.axis_size(SEQ)
    members = lax.axis_size(TP)
    local_width, block_len = filter_taps.shape
    per_group = local_width // groups
    seq_len = groups * block_len
    offset = lax.axis_index(SEQ) * per_group
    bias_part = lax.dynamic_slice_in_dim(skip_bias, offset, per_group, 0)
    channel_weights = lax.dynamic_slice_in_dim(short_weight, offset, per_group, 1)

    sent = jnp.concatenate([projected[1:], filter_taps[None]], axis=0)
    sent = sent.reshape(3, groups, per_group, block_len).transpose(1, 0, 2, 3)
    here = lax.all_to_all(sent, SEQ, split_axis=0, concat_axis=0, tiled=True)

    edge = lax.ppermute(
        projected[0, :, block_len - 2 :].T, SEQ, [(i, i + 1) for i in range(groups - 1)]
    ).T
    query = short_filter(
        projected[:1].astype(jnp.float32), short_weight[:1], edge[None].astype(jnp.float32)
    )[0]

    own_pair = jnp.concatenate([padded_rows(gate_weight), padded_rows(up_weight)], axis=0)
    other_pair = swap(own_pair, "xh")
    down_own = lax.all_gather(padded_rows(down_weight), ("z", "core"), axis=0, tiled=True)
    here, own_pair, other_pair = lax.optimization_barrier((here, own_pair, other_pair))
    gate_up = lax.all_gather(
        jnp.concatenate([own_pair, other_pair], axis=0), ("z", "core"), axis=0, tiled=True
    )

    here = here.transpose(1, 2, 0, 3).reshape(3, per_group, seq_len)
    shorts = short_filter(
        here[:2].astype(jnp.float32), channel_weights[1:], jnp.zeros((2, per_group, 2), jnp.float32)
    )
    gated_term = (shorts[0] * shorts[1]).astype(jnp.bfloat16)
    mixed_term = long_mixing(gated_term, here[2], bias_part)
    returned = mixed_term.reshape(per_group, groups, block_len).transpose(1, 0, 2)
    returned, down_own = lax.optimization_barrier((returned, down_own))
    down_near, down_far = spread_down(down_own)
    returned = lax.all_to_all(returned, SEQ, split_axis=0, concat_axis=0, tiled=True)
    hyena = (query * returned.reshape(local_width, block_len).astype(jnp.float32)).astype(
        jnp.bfloat16
    )

    copies = jnp.broadcast_to(hyena[None], (members, local_width, block_len))
    whole = lax.all_to_all(copies, TP, split_axis=0, concat_axis=0, tiled=True)
    whole = whole.reshape(members * local_width, block_len)
    wide = whole.astype(jnp.float32)
    mean_square = jnp.mean(wide * wide, axis=0)
    normed = (wide * lax.rsqrt(mean_square + EPSILON)[None, :] * norm_gain[:, None]).astype(
        jnp.bfloat16
    )
    sums = jnp.dot(gate_up, normed, preferred_element_type=jnp.float32)
    sums = sums.reshape(-1, 2, 2, own_pair.shape[0] // 2, block_len)
    hidden = (jax.nn.silu(sums[:, :, 0]) * sums[:, :, 1]).astype(jnp.bfloat16)
    hidden_own = hidden[:, 0].reshape(-1, block_len)
    hidden_other = hidden[:, 1].reshape(-1, block_len)
    half = down_near.shape[0]
    core = lax.axis_index("core")
    hidden_near = lax.dynamic_slice_in_dim(hidden_other, core * half, half, 0)
    hidden_far = lax.dynamic_slice_in_dim(hidden_other, (1 - core) * half, half, 0)
    partial_sum = (
        down_product(down_own, hidden_own)
        + down_product(down_near, hidden_near)
        + down_product(down_far, hidden_far)
    ).astype(jnp.bfloat16)
    shares = lax.all_to_all(
        partial_sum.reshape(members, local_width, block_len),
        TP,
        split_axis=0,
        concat_axis=0,
        tiled=True,
    )
    feed_out = jnp.sum(shares.astype(jnp.float32), axis=0)
    return (hyena.astype(jnp.float32) + feed_out).astype(jnp.bfloat16)


def solution(mesh):
    fine = Mesh(mesh.devices.reshape(2, 8, 2, 4, 2), SEQ + TP)
    placed = (
        P(None, TP, SEQ),
        P(TP, SEQ),
        P(None, TP, None),
        P(TP),
        P(),
        P(SEQ + TP, None),
        P(SEQ + TP, None),
        P(SEQ + TP, None),
    )
    return jax.shard_map(
        per_device, mesh=fine, in_specs=placed, out_specs=P(TP, SEQ), check_vma=False
    )
```

```python
import jax
import jax.numpy as jnp
from jax import lax
from jax.experimental import pallas as pl
from jax.experimental.pallas import tpu as pltpu
from jax.sharding import Mesh
from jax.sharding import PartitionSpec as P

EPSILON = 1e-06
LANES = 128
SEQ = ("xh", "z", "core")
TP = ("y", "xl")


def short_filter(signal, weights, leading):
    extent = signal.shape[2]
    padded = jnp.concatenate([leading, signal], axis=2)
    return (
        weights[:, :, 0:1] * padded[:, :, 2:]
        + weights[:, :, 1:2] * padded[:, :, 1 : extent + 1]
        + weights[:, :, 2:3] * padded[:, :, 0:extent]
    )


def build_table(taps_ref, channel, table_ref):
    seq_len = taps_ref.shape[2]
    base = jnp.broadcast_to(taps_ref[channel].astype(jnp.float32), (8, seq_len))
    base = pltpu.roll(base, 0, 1, stride=1, stride_axis=0)
    lane = lax.broadcasted_iota(jnp.int32, (8, seq_len), 1)
    row = lax.broadcasted_iota(jnp.int32, (8, seq_len), 0)
    base = jnp.where(lane >= row, base, 0.0)
    for pair in range(LANES // 16):
        parts = []
        for shift in (16 * pair, 16 * pair + 8):
            moved = pltpu.roll(base, shift, 1) if shift else base
            parts.append(jnp.where(lane >= shift, moved, 0.0) if shift else moved)
        table_ref[16 * pair : 16 * pair + 16, :] = jnp.concatenate(parts, axis=0).astype(jnp.bfloat16)

def apply_table(gated_ref, bias_ref, channel, table_ref, out_ref):
    rows = gated_ref.shape[1]
    gated = gated_ref[channel].astype(jnp.float32)
    tiles = rows // 8
    left = []
    for skip in range(tiles):
        keep = rows - 8 * skip
        left.append(jnp.concatenate([gated[:keep, :LANES], gated[:keep, LANES:]], axis=0).astype(jnp.bfloat16))
    zero = jnp.zeros((8, LANES), jnp.float32)
    total = [[zero] * tiles, [zero] * tiles]
    row = lax.broadcasted_iota(jnp.int32, (rows, LANES), 0)
    carried = [zero] * tiles
    for rho in range(8):
        sums = [carried, [zero] * tiles]
        carried = [zero] * tiles
        for skip in range(tiles):
            step = 8 * skip + rho
            keep = rows - 8 * skip
            part = jnp.dot(left[skip], table_ref[:, 2 * LANES * step : 2 * LANES * (step + 1)], preferred_element_type=jnp.float32)
            for lane_half in range(2):
                for row_half in range(2):
                    move = (2 * step + lane_half + row_half) // 2
                    if move >= rows: continue
                    side = (lane_half + row_half) % 2
                    target = sums[side] if move == step else carried
                    first = move // 8
                    for tile in range(tiles - first):
                        start = row_half * keep + 8 * tile
                        target[tile + first] = target[tile + first] + part[start:start + 8, lane_half * LANES:(lane_half + 1) * LANES]
        for side in range(2):
            if rho == 0:
                moved = sums[side]
            else:
                moved = jnp.concatenate(sums[side], axis=0)
                moved = jnp.where(row >= rho, pltpu.roll(moved, rho, 0), 0.0)
                moved = [moved[8*t:8*t+8] for t in range(tiles)]
            total[side] = [a + b for a, b in zip(total[side], moved)]
    total[0] = [a + b for a, b in zip(total[0], carried)]
    whole = jnp.concatenate([jnp.concatenate(total[0], axis=0), jnp.concatenate(total[1], axis=0)], axis=1)
    out_ref[channel] = (whole + bias_ref[channel] * gated).astype(jnp.bfloat16)

def conv_kernel(bias_ref, gated_ref, taps_ref, out_ref, even_ref, odd_ref):
    channels = gated_ref.shape[0]
    build_table(taps_ref, 0, even_ref)
    def body(step, carry):
        channel = 2 * step
        build_table(taps_ref, channel + 1, odd_ref)
        apply_table(gated_ref, bias_ref, channel, even_ref, out_ref)
        build_table(taps_ref, lax.rem(channel + 2, channels), even_ref)
        apply_table(gated_ref, bias_ref, channel + 1, odd_ref, out_ref)
        return carry
    lax.fori_loop(0, channels // 2, body, 0)

def long_mixing(gated, taps, bias):
    channels, rows, width = gated.shape
    seq_len = rows * width
    return pl.pallas_call(conv_kernel,
        out_shape=jax.ShapeDtypeStruct(gated.shape, jnp.bfloat16),
        in_specs=[pl.BlockSpec(memory_space=pltpu.SMEM), pl.BlockSpec(memory_space=pltpu.VMEM), pl.BlockSpec(memory_space=pltpu.VMEM)],
        out_specs=pl.BlockSpec(memory_space=pltpu.VMEM),
        scratch_shapes=[pltpu.VMEM((LANES, seq_len), jnp.bfloat16)]*2,
        compiler_params=pltpu.CompilerParams(vmem_limit_bytes=24*1024*1024),
        cost_estimate=pl.CostEstimate(flops=2*channels*seq_len*seq_len, bytes_accessed=6*channels*seq_len, transcendentals=0),
        name="long_mixing")(bias, gated, taps.reshape(channels, 1, seq_len))


def padded_rows(weight):
    rows = weight.shape[0]
    return jnp.pad(weight, ((0, -rows % 8), (0, 0)))


def swap(values, axis):
    return lax.ppermute(values, axis, [(0, 1), (1, 0)])


def spread_part(own, part, parts):
    size = own.shape[0] // (2 * parts)
    core = lax.axis_index("core")
    return lax.dynamic_slice_in_dim(own, (core * parts + part) * size, size, 0)


def down_product(weight, hidden):
    return lax.dot_general(
        weight, hidden, (((0,), (0,)), ((), ())), preferred_element_type=jnp.float32
    )


def per_device(
    projected, filter_taps, short_weight, skip_bias, norm_gain, gate_weight, up_weight, down_weight
):
    groups = lax.axis_size(SEQ)
    members = lax.axis_size(TP)
    local_width, block_len = filter_taps.shape
    per_group = local_width // groups
    seq_len = groups * block_len
    offset = lax.axis_index(SEQ) * per_group
    bias_part = lax.dynamic_slice_in_dim(skip_bias, offset, per_group, 0)

    edge = lax.ppermute(
        projected[:, :, block_len - 2 :].transpose(0, 2, 1).reshape(6, local_width),
        SEQ,
        [(i, i + 1) for i in range(groups - 1)],
    )
    edge = edge.reshape(3, 2, local_width).transpose(0, 2, 1)
    shorts = short_filter(
        projected.astype(jnp.float32), short_weight, edge.astype(jnp.float32)
    )
    query = shorts[0]
    gated = (shorts[1] * shorts[2]).astype(jnp.bfloat16)
    sent = jnp.stack([gated, filter_taps]).reshape(2, groups, per_group, block_len)
    here = lax.all_to_all(
        sent.transpose(1, 0, 2, 3), SEQ, split_axis=0, concat_axis=0, tiled=True
    )

    own_pair = jnp.concatenate([padded_rows(gate_weight), padded_rows(up_weight)], axis=0)
    other_pair = swap(own_pair, "xh")
    down_own = lax.all_gather(padded_rows(down_weight), ("z", "core"), axis=0, tiled=True)
    here, own_pair, other_pair = lax.optimization_barrier((here, own_pair, other_pair))
    gate_up = lax.all_gather(
        jnp.concatenate([own_pair, other_pair], axis=0), ("z", "core"), axis=0, tiled=True
    )

    here = here.transpose(1, 2, 0, 3)
    mixed_term = long_mixing(here[0], here[1].reshape(per_group, seq_len), bias_part)
    returned = mixed_term.transpose(1, 0, 2)
    first, second = spread_part(down_own, 0, 2), spread_part(down_own, 1, 2)
    returned, first, second = lax.optimization_barrier((returned, first, second))
    near_first = swap(first, "xh")
    returned = lax.all_to_all(returned, SEQ, split_axis=0, concat_axis=0, tiled=True)
    hyena = (query * returned.reshape(local_width, block_len).astype(jnp.float32)).astype(
        jnp.bfloat16
    )

    hyena, near_first, second = lax.optimization_barrier((hyena, near_first, second))
    near_second = swap(second, "xh")
    copies = jnp.broadcast_to(hyena[None], (members, local_width, block_len))
    whole = lax.all_to_all(copies, TP, split_axis=0, concat_axis=0, tiled=True)
    whole = whole.reshape(members * local_width, block_len)
    wide = whole.astype(jnp.float32)
    mean_square = jnp.mean(wide * wide, axis=0)
    normed = (wide * lax.rsqrt(mean_square + EPSILON)[None, :] * norm_gain[:, None]).astype(
        jnp.bfloat16
    )
    sums = jnp.dot(gate_up, normed, preferred_element_type=jnp.float32)
    sums = sums.reshape(-1, 2, 2, own_pair.shape[0] // 2, block_len)
    hidden = (jax.nn.silu(sums[:, :, 0]) * sums[:, :, 1]).astype(jnp.bfloat16)
    hidden_own = hidden[:, 0].reshape(-1, block_len)
    hidden_other = hidden[:, 1].reshape(-1, block_len)
    partial_sum = down_product(down_own, hidden_own)
    core = lax.axis_index("core")
    for part, near in enumerate((near_first, near_second)):
        size = near.shape[0]
        for side, rows in ((core, near), (1 - core, swap(near, "core"))):
            chosen = lax.dynamic_slice_in_dim(hidden_other, (side * 2 + part) * size, size, 0)
            partial_sum += down_product(rows, chosen)
    partial_sum = partial_sum.astype(jnp.bfloat16)
    shares = lax.all_to_all(
        partial_sum.reshape(members, local_width, block_len),
        TP,
        split_axis=0,
        concat_axis=0,
        tiled=True,
    )
    feed_out = jnp.sum(shares.astype(jnp.float32), axis=0)
    return (hyena.astype(jnp.float32) + feed_out).astype(jnp.bfloat16)


def solution(mesh):
    fine = Mesh(mesh.devices.reshape(2, 8, 2, 4, 2), SEQ + TP)
    placed = (
        P(None, TP, SEQ),
        P(TP, SEQ),
        P(None, TP, None),
        P(TP),
        P(),
        P(SEQ + TP, None),
        P(SEQ + TP, None),
        P(SEQ + TP, None),
    )
    return jax.shard_map(
        per_device, mesh=fine, in_specs=placed, out_specs=P(TP, SEQ), check_vma=False
    )
```

```python
import jax
import jax.numpy as jnp
from jax import lax
from jax.experimental import pallas as pl
from jax.experimental.pallas import tpu as pltpu
from jax.sharding import Mesh
from jax.sharding import PartitionSpec as P

EPSILON = 1e-06
LANES = 128
SEQ = ("xh", "z", "core")
TP = ("y", "xl")


def short_filter(signal, weights, leading):
    extent = signal.shape[2]
    padded = jnp.concatenate([leading, signal], axis=2)
    return (
        weights[:, :, 0:1] * padded[:, :, 2:]
        + weights[:, :, 1:2] * padded[:, :, 1 : extent + 1]
        + weights[:, :, 2:3] * padded[:, :, 0:extent]
    )


def build_table(taps_ref, channel, table_ref):
    seq_len = taps_ref.shape[2]
    base = jnp.broadcast_to(taps_ref[channel].astype(jnp.float32), (8, seq_len))
    base = pltpu.roll(base, 0, 1, stride=1, stride_axis=0)
    lane = lax.broadcasted_iota(jnp.int32, (8, seq_len), 1)
    row = lax.broadcasted_iota(jnp.int32, (8, seq_len), 0)
    base = jnp.where(lane >= row, base, 0.0)
    for pair in range(LANES // 16):
        parts = []
        for shift in (16 * pair, 16 * pair + 8):
            moved = pltpu.roll(base, shift, 1) if shift else base
            parts.append(jnp.where(lane >= shift, moved, 0.0) if shift else moved)
        table_ref[16 * pair : 16 * pair + 16, :] = jnp.concatenate(parts, axis=0).astype(jnp.bfloat16)

def apply_table(gated_ref, bias_ref, channel, table_ref, out_ref):
    rows = gated_ref.shape[1]
    gated = gated_ref[channel].astype(jnp.float32)
    tiles = rows // 8
    left = []
    for skip in range(tiles):
        keep = rows - 8 * skip
        left.append(jnp.concatenate([gated[:keep, :LANES], gated[:keep, LANES:]], axis=0).astype(jnp.bfloat16))
    zero = jnp.zeros((8, LANES), jnp.float32)
    total = [[zero] * tiles, [zero] * tiles]
    row = lax.broadcasted_iota(jnp.int32, (rows, LANES), 0)
    carried = [zero] * tiles
    for rho in range(8):
        sums = [carried, [zero] * tiles]
        carried = [zero] * tiles
        for skip in range(tiles):
            step = 8 * skip + rho
            keep = rows - 8 * skip
            part = jnp.dot(left[skip], table_ref[:, 2 * LANES * step : 2 * LANES * (step + 1)], preferred_element_type=jnp.float32)
            for lane_half in range(2):
                for row_half in range(2):
                    move = (2 * step + lane_half + row_half) // 2
                    if move >= rows: continue
                    side = (lane_half + row_half) % 2
                    target = sums[side] if move == step else carried
                    first = move // 8
                    for tile in range(tiles - first):
                        start = row_half * keep + 8 * tile
                        target[tile + first] = target[tile + first] + part[start:start + 8, lane_half * LANES:(lane_half + 1) * LANES]
        for side in range(2):
            if rho == 0:
                moved = sums[side]
            else:
                moved = jnp.concatenate(sums[side], axis=0)
                moved = jnp.where(row >= rho, pltpu.roll(moved, rho, 0), 0.0)
                moved = [moved[8*t:8*t+8] for t in range(tiles)]
            total[side] = [a + b for a, b in zip(total[side], moved)]
    total[0] = [a + b for a, b in zip(total[0], carried)]
    whole = jnp.concatenate([jnp.concatenate(total[0], axis=0), jnp.concatenate(total[1], axis=0)], axis=1)
    out_ref[channel] = (whole + bias_ref[channel] * gated).astype(jnp.bfloat16)

def conv_kernel(bias_ref, gated_ref, taps_ref, out_ref, even_ref, odd_ref):
    channels = gated_ref.shape[0]
    build_table(taps_ref, 0, even_ref)
    def body(step, carry):
        channel = 2 * step
        build_table(taps_ref, channel + 1, odd_ref)
        apply_table(gated_ref, bias_ref, channel, even_ref, out_ref)
        build_table(taps_ref, lax.rem(channel + 2, channels), even_ref)
        apply_table(gated_ref, bias_ref, channel + 1, odd_ref, out_ref)
        return carry
    lax.fori_loop(0, channels // 2, body, 0)

def long_mixing(gated, taps, bias):
    channels, rows, width = gated.shape
    seq_len = rows * width
    return pl.pallas_call(conv_kernel,
        out_shape=jax.ShapeDtypeStruct(gated.shape, jnp.bfloat16),
        in_specs=[pl.BlockSpec(memory_space=pltpu.SMEM), pl.BlockSpec(memory_space=pltpu.VMEM), pl.BlockSpec(memory_space=pltpu.VMEM)],
        out_specs=pl.BlockSpec(memory_space=pltpu.VMEM),
        scratch_shapes=[pltpu.VMEM((LANES, seq_len), jnp.bfloat16)]*2,
        compiler_params=pltpu.CompilerParams(vmem_limit_bytes=24*1024*1024),
        cost_estimate=pl.CostEstimate(flops=8 * channels * seq_len * seq_len, bytes_accessed=6*channels*seq_len, transcendentals=0),
        name="long_mixing")(bias, gated, taps.reshape(channels, 1, seq_len))


def pack_kernel(gate_ref, up_ref, other_ref, out_ref):
    parts = [gate_ref[...], up_ref[...], other_ref[...]]
    whole = jnp.concatenate([part.astype(jnp.float32) for part in parts], axis=0)
    out_ref[...] = whole.astype(out_ref.dtype)


def pack_rows(gate, up, other):
    rows = gate.shape[0] + up.shape[0] + other.shape[0]
    return pl.pallas_call(
        pack_kernel,
        out_shape=jax.ShapeDtypeStruct((rows, gate.shape[1]), gate.dtype),
        name="pack_rows",
    )(gate, up, other)


def payload_kernel(query_ref, mixed_ref, gain_ref, hyena_ref, out_ref):
    rows = query_ref.shape[0]
    hyena = (query_ref[...] * mixed_ref[...].astype(jnp.float32)).astype(jnp.bfloat16)
    hyena_ref[...] = hyena
    wide = hyena.astype(jnp.float32)
    scaled = (wide * gain_ref[...]).astype(jnp.bfloat16)
    rest = jnp.sum(wide * wide, axis=0, keepdims=True)
    place = lax.broadcasted_iota(jnp.int32, (out_ref.shape[1] - rows, wide.shape[1]), 0)
    extra = jnp.zeros(place.shape, jnp.float32)
    for index in range(3):
        part = rest.astype(jnp.bfloat16).astype(jnp.float32)
        extra = jnp.where(place == index, part, extra)
        rest = rest - part
    for member in range(out_ref.shape[0]):
        out_ref[member, :rows, :] = scaled
        out_ref[member, rows:, :] = extra.astype(jnp.bfloat16)


def make_payload(query, mixed, gain, members):
    rows, width = query.shape
    return pl.pallas_call(
        payload_kernel,
        out_shape=(
            jax.ShapeDtypeStruct((rows, width), jnp.bfloat16),
            jax.ShapeDtypeStruct((members, rows + 16, width), jnp.bfloat16),
        ),
        name="make_payload",
    )(query, mixed, gain.reshape(rows, 1))


def feed_kernel(
    core_ref, sent_ref, weight_ref, own_ref, near_ref, far_ref, out_ref, x_ref, scale_ref, hidden_ref
):
    step = pl.program_id(0)
    first_steps = pl.num_programs(0) - sent_ref.shape[0] // out_ref.shape[0]
    members, rows = sent_ref.shape[0], out_ref.shape[2]
    block = own_ref.shape[0] // (weight_ref.shape[0] * first_steps)
    half = near_ref.shape[0]

    @pl.when(step == 0)
    def _():
        squares = jnp.zeros((1, x_ref.shape[1]), jnp.float32)
        for member in range(members):
            x_ref[member * rows : (member + 1) * rows, :] = sent_ref[member, :rows, :]
            extra = sent_ref[member, rows:, :].astype(jnp.float32)
            squares = squares + (extra[0:1] + extra[1:2] + extra[2:3])
        scale = lax.rsqrt(squares / (members * rows) + EPSILON)
        scale_ref[...] = jnp.broadcast_to(scale, scale_ref.shape)

    @pl.when(step < first_steps)
    def _():
        scale = scale_ref[0:1, :]
        for index in range(weight_ref.shape[0]):
            sums = jnp.dot(weight_ref[index], x_ref[...], preferred_element_type=jnp.float32)
            sums = sums * scale
            units = sums.shape[0] // 4
            for side in range(2):
                gate = sums[2 * side * units : (2 * side + 1) * units]
                up = sums[(2 * side + 1) * units : (2 * side + 2) * units]
                value = gate / (1.0 + jnp.exp(-gate)) * up
                blank = jnp.zeros((block - units, value.shape[1]), jnp.float32)
                start = pl.multiple_of((step * weight_ref.shape[0] + index) * block, 8)
                hidden_ref[side, pl.ds(start, block), :] = jnp.concatenate([value, blank], axis=0)

    @pl.when(step >= first_steps)
    def _():
        core = core_ref[0]
        near_start = pl.multiple_of(core * half, 8)
        far_start = pl.multiple_of((1 - core) * half, 8)
        pieces = (
            (hidden_ref[0], own_ref),
            (hidden_ref[1, pl.ds(near_start, half), :], near_ref),
            (hidden_ref[1, pl.ds(far_start, half), :], far_ref),
        )
        total = None
        for hidden, ref in pieces:
            part = lax.dot_general(
                hidden.astype(jnp.bfloat16),
                ref[...],
                (((0,), (0,)), ((), ())),
                preferred_element_type=jnp.float32,
            )
            total = part if total is None else total + part
        for member in range(out_ref.shape[0]):
            out_ref[member] = total[:, member * rows : (member + 1) * rows].astype(jnp.bfloat16)


def feed_forward(sent, weights, own, near, far, core):
    members, padded, width = sent.shape
    blocks, block_rows, channels = weights.shape
    rows = channels // members
    per_step, out_step = 2, 2
    first_steps = blocks // per_step

    def down_spec(rows_here):
        return pl.BlockSpec(
            (rows_here, out_step * rows), lambda i: (0, jnp.maximum(i - first_steps, 0))
        )

    return pl.pallas_call(
        feed_kernel,
        grid=(first_steps + members // out_step,),
        out_shape=jax.ShapeDtypeStruct((members, width, rows), jnp.bfloat16),
        in_specs=[
            pl.BlockSpec(memory_space=pltpu.SMEM),
            pl.BlockSpec(memory_space=pltpu.VMEM),
            pl.BlockSpec(
                (per_step, block_rows, channels), lambda i: (jnp.minimum(i, first_steps - 1), 0, 0)
            ),
            down_spec(own.shape[0]),
            down_spec(near.shape[0]),
            down_spec(far.shape[0]),
        ],
        out_specs=pl.BlockSpec(
            (out_step, width, rows), lambda i: (jnp.maximum(i - first_steps, 0), 0, 0)
        ),
        scratch_shapes=[
            pltpu.VMEM((channels, width), jnp.bfloat16),
            pltpu.VMEM((8, width), jnp.float32),
            pltpu.VMEM((2, own.shape[0], width), jnp.float32),
        ],
        compiler_params=pltpu.CompilerParams(vmem_limit_bytes=48 * 1024 * 1024),
        cost_estimate=pl.CostEstimate(flops=10**10, bytes_accessed=3 * 10**7, transcendentals=0),
        name="feed_forward",
    )(core, sent, weights, own, near, far)


def padded_rows(weight):
    rows = weight.shape[0]
    return jnp.pad(weight, ((0, -rows % 8), (0, 0)))


def swap(values, axis):
    return lax.ppermute(values, axis, [(0, 1), (1, 0)])


def per_device(
    projected, filter_taps, short_weight, skip_bias, norm_gain, gate_weight, up_weight, down_weight
):
    groups = lax.axis_size(SEQ)
    members = lax.axis_size(TP)
    local_width, block_len = filter_taps.shape
    per_group = local_width // groups
    seq_len = groups * block_len
    offset = lax.axis_index(SEQ) * per_group
    bias_part = lax.dynamic_slice_in_dim(skip_bias, offset, per_group, 0)

    edge = lax.ppermute(
        projected[:, :, block_len - 2 :].transpose(0, 2, 1).reshape(6, local_width),
        SEQ,
        [(i, i + 1) for i in range(groups - 1)],
    )
    edge = edge.reshape(3, 2, local_width).transpose(0, 2, 1)
    shorts = short_filter(
        projected.astype(jnp.float32), short_weight, edge.astype(jnp.float32)
    )
    query = shorts[0]
    gated = (shorts[1] * shorts[2]).astype(jnp.bfloat16)
    sent = jnp.stack([gated, filter_taps]).reshape(2, groups, per_group, block_len)
    here = lax.all_to_all(
        sent.transpose(1, 0, 2, 3), SEQ, split_axis=0, concat_axis=0, tiled=True
    )

    core = lax.axis_index("core")
    down_own = lax.all_gather(padded_rows(down_weight), ("z", "core"), axis=0, tiled=True)
    other_pair = swap(jnp.concatenate([gate_weight, up_weight], axis=0), "xh")
    here, other_pair = lax.optimization_barrier((here, other_pair))
    gate_up = lax.all_gather(
        pack_rows(gate_weight, up_weight, other_pair)[None], ("z", "core"), axis=0, tiled=True
    )

    half = down_own.shape[0] // 2
    down_half = lax.dynamic_slice_in_dim(down_own, core * half, half, 0)
    here, down_half = lax.optimization_barrier((here, down_half))
    down_near = swap(down_half, "xh")
    here = here.transpose(1, 2, 0, 3)
    mixed_term = long_mixing(here[0], here[1].reshape(per_group, seq_len), bias_part)
    returned = lax.all_to_all(
        mixed_term.transpose(1, 0, 2), SEQ, split_axis=0, concat_axis=0, tiled=True
    )
    gain = lax.dynamic_slice_in_dim(
        norm_gain, lax.axis_index(TP) * local_width, local_width, 0
    )
    hyena, payload = make_payload(query, returned.reshape(local_width, block_len), gain, members)
    payload, down_near = lax.optimization_barrier((payload, down_near))
    down_far = swap(down_near, "core")
    sent = lax.all_to_all(payload, TP, split_axis=0, concat_axis=0, tiled=True)
    partial_sum = feed_forward(sent, gate_up, down_own, down_near, down_far, core.reshape(1))
    shares = lax.all_to_all(partial_sum, TP, split_axis=0, concat_axis=0, tiled=True)
    feed_out = jnp.sum(shares.astype(jnp.float32), axis=0).T
    return (hyena.astype(jnp.float32) + feed_out).astype(jnp.bfloat16)


def solution(mesh):
    fine = Mesh(mesh.devices.reshape(2, 8, 2, 4, 2), SEQ + TP)
    placed = (
        P(None, TP, SEQ),
        P(TP, SEQ),
        P(None, TP, None),
        P(TP),
        P(),
        P(SEQ + TP, None),
        P(SEQ + TP, None),
        P(SEQ + TP, None),
    )
    return jax.shard_map(
        per_device, mesh=fine, in_specs=placed, out_specs=P(TP, SEQ), check_vma=False
    )
```

```python
import functools

import jax
import jax.numpy as jnp
from jax import lax
from jax.experimental import pallas as pl
from jax.experimental.pallas import tpu as pltpu
from jax.sharding import Mesh
from jax.sharding import PartitionSpec as P

EPSILON = 1e-06
LANES = 128
SEQ = ("xh", "z", "core")
TP = ("y", "xl")


def gate_kernel(projected_ref, taps_ref, weight_ref, edge_ref, sent_ref, query_ref):
    rows, width = taps_ref.shape
    groups = sent_ref.shape[0]
    weights = weight_ref[...].T
    edges = edge_ref[...].astype(jnp.float32).T
    lane = lax.broadcasted_iota(jnp.int32, (rows, width), 1)
    shorts = []
    for index in range(3):
        value = projected_ref[index].astype(jnp.float32)
        far, near = edges[:, 2 * index : 2 * index + 1], edges[:, 2 * index + 1 : 2 * index + 2]
        once = jnp.where(lane == 0, near, pltpu.roll(value, 1, 1))
        twice = jnp.where(lane == 0, far, jnp.where(lane == 1, near, pltpu.roll(value, 2, 1)))
        taps = [weights[:, 3 * index + tap : 3 * index + tap + 1] for tap in range(3)]
        shorts.append(taps[0] * value + taps[1] * once + taps[2] * twice)
    query_ref[...] = shorts[0]
    gated = (shorts[1] * shorts[2]).astype(jnp.bfloat16)
    sent_ref[:, 0] = gated.reshape(groups, rows // groups, width)
    sent_ref[:, 1] = taps_ref[...].reshape(groups, rows // groups, width)


def make_gated(projected, taps, short_weight, edge, groups):
    count, rows, width = projected.shape
    weights = short_weight.transpose(0, 2, 1).reshape(9, rows)
    return pl.pallas_call(
        gate_kernel,
        out_shape=(
            jax.ShapeDtypeStruct((groups, 2, rows // groups, width), jnp.bfloat16),
            jax.ShapeDtypeStruct((rows, width), jnp.float32),
        ),
        name="make_gated",
    )(projected, taps, jnp.pad(weights, ((0, 7), (0, 0))), edge)


def pack_first_kernel(split, gate_ref, up_ref, down_ref, first_ref, pair_ref):
    gate, up = gate_ref[...].astype(jnp.float32), up_ref[...].astype(jnp.float32)
    down = down_ref[...].astype(jnp.float32)
    first = jnp.concatenate([down, gate[split:], up[split:]], axis=0)
    first_ref[...] = first.astype(jnp.bfloat16)
    pair_ref[...] = jnp.concatenate([gate[:split], up[:split]], axis=0).astype(jnp.bfloat16)


def pack_first(gate, up, down):
    rows, width = gate.shape
    split = rows - (-rows % 16) // 2
    return pl.pallas_call(
        functools.partial(pack_first_kernel, split),
        out_shape=(
            jax.ShapeDtypeStruct((rows + 2 * (rows - split), width), gate.dtype),
            jax.ShapeDtypeStruct((2 * split, width), gate.dtype),
        ),
        name="pack_first",
    )(gate, up, down)


def pack_second_kernel(pair_ref, other_ref, out_ref):
    pair, other = pair_ref[...].astype(jnp.float32), other_ref[...].astype(jnp.float32)
    blank = jnp.zeros((out_ref.shape[0] - 2 * pair.shape[0], pair.shape[1]), jnp.float32)
    out_ref[...] = jnp.concatenate([pair, other, blank], axis=0).astype(jnp.bfloat16)


def pack_second(pair, other):
    rows = 2 * pair.shape[0]
    return pl.pallas_call(
        pack_second_kernel,
        out_shape=jax.ShapeDtypeStruct((rows + -rows % 8, pair.shape[1]), pair.dtype),
        name="pack_second",
    )(pair, other)


def build_table(taps_ref, channel, table_ref):
    seq_len = taps_ref.shape[2]
    base = jnp.broadcast_to(taps_ref[channel].astype(jnp.float32), (8, seq_len))
    base = pltpu.roll(base, 0, 1, stride=1, stride_axis=0)
    lane = lax.broadcasted_iota(jnp.int32, (8, seq_len), 1)
    row = lax.broadcasted_iota(jnp.int32, (8, seq_len), 0)
    base = jnp.where(lane >= row, base, 0.0)
    for pair in range(LANES // 16):
        parts = []
        for shift in (16 * pair, 16 * pair + 8):
            moved = pltpu.roll(base, shift, 1) if shift else base
            parts.append(jnp.where(lane >= shift, moved, 0.0) if shift else moved)
        table_ref[16 * pair : 16 * pair + 16, :] = jnp.concatenate(parts, axis=0).astype(jnp.bfloat16)

def apply_table(gated_ref, bias_ref, channel, table_ref, out_ref):
    rows = gated_ref.shape[1]
    gated = gated_ref[channel].astype(jnp.float32)
    tiles = rows // 8
    left = []
    for skip in range(tiles):
        keep = rows - 8 * skip
        left.append(jnp.concatenate([gated[:keep, :LANES], gated[:keep, LANES:]], axis=0).astype(jnp.bfloat16))
    zero = jnp.zeros((8, LANES), jnp.float32)
    total = [[zero] * tiles, [zero] * tiles]
    row = lax.broadcasted_iota(jnp.int32, (rows, LANES), 0)
    carried = [zero] * tiles
    for rho in range(8):
        sums = [carried, [zero] * tiles]
        carried = [zero] * tiles
        for skip in range(tiles):
            step = 8 * skip + rho
            keep = rows - 8 * skip
            part = jnp.dot(left[skip], table_ref[:, 2 * LANES * step : 2 * LANES * (step + 1)], preferred_element_type=jnp.float32)
            for lane_half in range(2):
                for row_half in range(2):
                    move = (2 * step + lane_half + row_half) // 2
                    if move >= rows: continue
                    side = (lane_half + row_half) % 2
                    target = sums[side] if move == step else carried
                    first = move // 8
                    for tile in range(tiles - first):
                        start = row_half * keep + 8 * tile
                        target[tile + first] = target[tile + first] + part[start:start + 8, lane_half * LANES:(lane_half + 1) * LANES]
        for side in range(2):
            if rho == 0:
                moved = sums[side]
            else:
                moved = jnp.concatenate(sums[side], axis=0)
                moved = jnp.where(row >= rho, pltpu.roll(moved, rho, 0), 0.0)
                moved = [moved[8*t:8*t+8] for t in range(tiles)]
            total[side] = [a + b for a, b in zip(total[side], moved)]
    total[0] = [a + b for a, b in zip(total[0], carried)]
    whole = jnp.concatenate([jnp.concatenate(total[0], axis=0), jnp.concatenate(total[1], axis=0)], axis=1)
    out_ref[channel] = (whole + bias_ref[channel] * gated).astype(jnp.bfloat16)

def conv_kernel(bias_ref, gated_ref, taps_ref, out_ref, even_ref, odd_ref):
    channels = gated_ref.shape[0]
    build_table(taps_ref, 0, even_ref)
    def body(step, carry):
        channel = 2 * step
        build_table(taps_ref, channel + 1, odd_ref)
        apply_table(gated_ref, bias_ref, channel, even_ref, out_ref)
        build_table(taps_ref, lax.rem(channel + 2, channels), even_ref)
        apply_table(gated_ref, bias_ref, channel + 1, odd_ref, out_ref)
        return carry
    lax.fori_loop(0, channels // 2, body, 0)

def long_mixing(gated, taps, bias):
    channels, rows, width = gated.shape
    seq_len = rows * width
    return pl.pallas_call(conv_kernel,
        out_shape=jax.ShapeDtypeStruct(gated.shape, jnp.bfloat16),
        in_specs=[pl.BlockSpec(memory_space=pltpu.SMEM), pl.BlockSpec(memory_space=pltpu.VMEM), pl.BlockSpec(memory_space=pltpu.VMEM)],
        out_specs=pl.BlockSpec(memory_space=pltpu.VMEM),
        scratch_shapes=[pltpu.VMEM((LANES, seq_len), jnp.bfloat16)]*2,
        compiler_params=pltpu.CompilerParams(vmem_limit_bytes=24*1024*1024),
        cost_estimate=pl.CostEstimate(flops=8 * channels * seq_len * seq_len, bytes_accessed=6*channels*seq_len, transcendentals=0),
        name="long_mixing")(bias, gated, taps.reshape(channels, 1, seq_len))


def payload_kernel(query_ref, mixed_ref, gain_ref, hyena_ref, out_ref):
    rows = query_ref.shape[0]
    hyena = (query_ref[...] * mixed_ref[...].astype(jnp.float32)).astype(jnp.bfloat16)
    hyena_ref[...] = hyena
    wide = hyena.astype(jnp.float32)
    scaled = (wide * gain_ref[...]).astype(jnp.bfloat16)
    rest = jnp.sum(wide * wide, axis=0, keepdims=True)
    place = lax.broadcasted_iota(jnp.int32, (out_ref.shape[1] - rows, wide.shape[1]), 0)
    extra = jnp.zeros(place.shape, jnp.float32)
    for index in range(3):
        part = rest.astype(jnp.bfloat16).astype(jnp.float32)
        extra = jnp.where(place == index, part, extra)
        rest = rest - part
    for member in range(out_ref.shape[0]):
        out_ref[member, :rows, :] = scaled
        out_ref[member, rows:, :] = extra.astype(jnp.bfloat16)


def make_payload(query, mixed, gain, members):
    rows, width = query.shape
    return pl.pallas_call(
        payload_kernel,
        out_shape=(
            jax.ShapeDtypeStruct((rows, width), jnp.bfloat16),
            jax.ShapeDtypeStruct((members, rows + 16, width), jnp.bfloat16),
        ),
        name="make_payload",
    )(query, mixed, gain.reshape(rows, 1))


def gated_product(gate, up):
    return gate / (1.0 + jnp.exp(-gate)) * up


def feed_kernel(
    sizes, core_ref, sent_ref, weight_ref, p0_ref, p1_ref, p2_ref, p3_ref, out_ref,
    x_ref, scale_ref, hidden_ref, flat_ref, piece_ref, piece_sem,
):
    units, split, block, per_step, first_steps = sizes
    step = pl.program_id(0)
    members, rows = sent_ref.shape[0], out_ref.shape[2]
    core = core_ref[0]
    copies = [
        pltpu.make_async_copy(ref, piece_ref.at[index], piece_sem.at[index])
        for index, ref in enumerate((p0_ref, p1_ref, p2_ref, p3_ref))
    ]

    @pl.when(step == 0)
    def _():
        for copy in copies:
            copy.start()
        squares = jnp.zeros((1, x_ref.shape[1]), jnp.float32)
        for member in range(members):
            x_ref[member * rows : (member + 1) * rows, :] = sent_ref[member, :rows, :]
            extra = sent_ref[member, rows:, :].astype(jnp.float32)
            squares = squares + (extra[0:1] + extra[1:2] + extra[2:3])
        scale = lax.rsqrt(squares / (members * rows) + EPSILON)
        scale_ref[...] = jnp.broadcast_to(scale, scale_ref.shape)

    @pl.when(step < first_steps)
    def _():
        scale = scale_ref[0:1, :]
        sums = jnp.dot(weight_ref[...], x_ref[...], preferred_element_type=jnp.float32) * scale
        height = weight_ref.shape[0] // per_step
        for index in range(per_step):
            part = sums[index * height : (index + 1) * height]
            for side in range(2):
                base = 2 * side * split
                value = gated_product(
                    part[base : base + split], part[base + split : base + 2 * split]
                )
                blank = jnp.zeros((block - split, value.shape[1]), jnp.float32)
                start = pl.multiple_of((step * (per_step // 2) + index // 2) * block, 8)
                hidden_ref[side, index % 2, pl.ds(start, block), :] = jnp.concatenate(
                    [value, blank], axis=0
                )

    @pl.when(step == first_steps)
    def _():
        for copy in copies:
            copy.wait()
        scale = scale_ref[0:1, :]
        count = piece_ref.shape[1] // block
        for index in range(4):
            tails = [
                piece_ref[index, z * block + block // 2 : (z + 1) * block, :] for z in range(count)
            ]
            sums = jnp.dot(
                jnp.concatenate(tails, axis=0), x_ref[...], preferred_element_type=jnp.float32
            )
            sums = sums * scale
            place = core if index % 2 == 0 else 1 - core
            for z in range(count):
                gate_at = z * (block // 2) + units - block // 2
                up_at = gate_at + units - split
                value = gated_product(sums[gate_at:up_at], sums[up_at : up_at + units - split])
                hidden_ref[index // 2, place, z * block + split : z * block + units, :] = value
            flat_ref[index] = hidden_ref[index // 2, place].T.astype(jnp.bfloat16)

    @pl.when(step >= first_steps)
    def _():
        wide = out_ref.shape[0] * rows
        start = pl.multiple_of((step - first_steps) * wide, LANES)
        total = None
        for index in range(4):
            part = jnp.dot(
                flat_ref[index],
                piece_ref[index, :, pl.ds(start, wide)],
                preferred_element_type=jnp.float32,
            )
            total = part if total is None else total + part
        for member in range(out_ref.shape[0]):
            out_ref[member] = total[:, member * rows : (member + 1) * rows].astype(jnp.bfloat16)


def feed_forward(sent, weights, pieces, core, units, split):
    members, padded, width = sent.shape
    channels = weights.shape[1]
    rows = channels // members
    length = pieces[0].shape[0]
    block = 2 * units - split + units - split
    blocks = 2 * length // block
    per_step, out_step = 4, 2
    first_steps = blocks // per_step
    anywhere = pl.BlockSpec(memory_space=pl.ANY)
    return pl.pallas_call(
        functools.partial(feed_kernel, (units, split, block, per_step, first_steps)),
        grid=(first_steps + members // out_step,),
        out_shape=jax.ShapeDtypeStruct((members, width, rows), jnp.bfloat16),
        in_specs=[
            pl.BlockSpec(memory_space=pltpu.SMEM),
            pl.BlockSpec(memory_space=pltpu.VMEM),
            pl.BlockSpec(
                (weights.shape[0] // first_steps, channels),
                lambda i: (jnp.minimum(i, first_steps - 1), 0),
            ),
            anywhere,
            anywhere,
            anywhere,
            anywhere,
        ],
        out_specs=pl.BlockSpec(
            (out_step, width, rows), lambda i: (jnp.maximum(i - first_steps, 0), 0, 0)
        ),
        scratch_shapes=[
            pltpu.VMEM((channels, width), jnp.bfloat16),
            pltpu.VMEM((8, width), jnp.float32),
            pltpu.VMEM((2, 2, length, width), jnp.float32),
            pltpu.VMEM((4, width, length), jnp.bfloat16),
            pltpu.VMEM((4, length, channels), jnp.bfloat16),
            pltpu.SemaphoreType.DMA((4,)),
        ],
        compiler_params=pltpu.CompilerParams(vmem_limit_bytes=48 * 1024 * 1024),
        cost_estimate=pl.CostEstimate(flops=10**10, bytes_accessed=3 * 10**7, transcendentals=0),
        name="feed_forward",
    )(core, sent, weights, *pieces)


def swap(values, axis):
    return lax.ppermute(values, axis, [(0, 1), (1, 0)])


def per_device(
    projected, filter_taps, short_weight, skip_bias, norm_gain, gate_weight, up_weight, down_weight
):
    groups = lax.axis_size(SEQ)
    members = lax.axis_size(TP)
    local_width, block_len = filter_taps.shape
    per_group = local_width // groups
    seq_len = groups * block_len
    offset = lax.axis_index(SEQ) * per_group
    bias_part = lax.dynamic_slice_in_dim(skip_bias, offset, per_group, 0)

    first, pair = pack_first(gate_weight, up_weight, down_weight)
    own_near = lax.all_gather(first, "z", axis=0, tiled=True)
    edge = projected[:, :, block_len - 2 :].transpose(0, 2, 1).reshape(6, local_width)
    edge = lax.ppermute(
        jnp.pad(edge, ((0, 2), (0, 0))), SEQ, [(i, i + 1) for i in range(groups - 1)]
    )
    sent, query = make_gated(projected, filter_taps, short_weight, edge, groups)
    here = lax.all_to_all(sent, SEQ, split_axis=0, concat_axis=0, tiled=True)

    core = lax.axis_index("core")
    other_pair = swap(pair, "xh")
    here, other_pair = lax.optimization_barrier((here, other_pair))
    gate_up = lax.all_gather(pack_second(pair, other_pair), ("z", "core"), axis=0, tiled=True)

    here, own_near = lax.optimization_barrier((here, own_near))
    own_far = swap(own_near, "core")
    near = swap(own_near, "xh")
    here = here.transpose(1, 2, 0, 3)
    mixed_term = long_mixing(here[0], here[1].reshape(per_group, seq_len), bias_part)
    returned = lax.all_to_all(
        mixed_term.transpose(1, 0, 2), SEQ, split_axis=0, concat_axis=0, tiled=True
    )
    gain = lax.dynamic_slice_in_dim(
        norm_gain, lax.axis_index(TP) * local_width, local_width, 0
    )
    hyena, payload = make_payload(query, returned.reshape(local_width, block_len), gain, members)
    payload, near = lax.optimization_barrier((payload, near))
    pieces = (own_near, own_far, near, swap(near, "core"))
    sent = lax.all_to_all(payload, TP, split_axis=0, concat_axis=0, tiled=True)
    units, split = gate_weight.shape[0], pair.shape[0] // 2
    partial_sum = feed_forward(sent, gate_up, pieces, core.reshape(1), units, split)
    shares = lax.all_to_all(partial_sum, TP, split_axis=0, concat_axis=0, tiled=True)
    feed_out = jnp.sum(shares.astype(jnp.float32), axis=0).T
    return (hyena.astype(jnp.float32) + feed_out).astype(jnp.bfloat16)


def solution(mesh):
    fine = Mesh(mesh.devices.reshape(2, 8, 2, 4, 2), SEQ + TP)
    placed = (
        P(None, TP, SEQ),
        P(TP, SEQ),
        P(None, TP, None),
        P(TP),
        P(),
        P(SEQ + TP, None),
        P(SEQ + TP, None),
        P(SEQ + TP, None),
    )
    return jax.shard_map(
        per_device, mesh=fine, in_specs=placed, out_specs=P(TP, SEQ), check_vma=False
    )
```

```python
import functools

import jax
import jax.numpy as jnp
from jax import lax
from jax.experimental import pallas as pl
from jax.experimental.pallas import tpu as pltpu
from jax.sharding import Mesh
from jax.sharding import PartitionSpec as P

EPSILON = 1e-06
LANES = 128
SEQ = ("xh", "z", "core")
TP = ("y", "xl")


def gate_kernel(projected_ref, taps_ref, weight_ref, edge_ref, sent_ref, query_ref):
    rows, width = taps_ref.shape
    groups = sent_ref.shape[0]
    weights = weight_ref[...].T
    edges = edge_ref[...].astype(jnp.float32).T
    lane = lax.broadcasted_iota(jnp.int32, (rows, width), 1)
    shorts = []
    for index in range(3):
        value = projected_ref[index].astype(jnp.float32)
        far, near = edges[:, 2 * index : 2 * index + 1], edges[:, 2 * index + 1 : 2 * index + 2]
        once = jnp.where(lane == 0, near, pltpu.roll(value, 1, 1))
        twice = jnp.where(lane == 0, far, jnp.where(lane == 1, near, pltpu.roll(value, 2, 1)))
        taps = [weights[:, 3 * index + tap : 3 * index + tap + 1] for tap in range(3)]
        shorts.append(taps[0] * value + taps[1] * once + taps[2] * twice)
    query_ref[...] = shorts[0]
    gated = (shorts[1] * shorts[2]).astype(jnp.bfloat16)
    sent_ref[:, 0] = gated.reshape(groups, rows // groups, width)
    sent_ref[:, 1] = taps_ref[...].reshape(groups, rows // groups, width)


def make_gated(projected, taps, short_weight, edge, groups):
    count, rows, width = projected.shape
    weights = short_weight.transpose(0, 2, 1).reshape(9, rows)
    return pl.pallas_call(
        gate_kernel,
        out_shape=(
            jax.ShapeDtypeStruct((groups, 2, rows // groups, width), jnp.bfloat16),
            jax.ShapeDtypeStruct((rows, width), jnp.float32),
        ),
        name="make_gated",
    )(projected, taps, jnp.pad(weights, ((0, 7), (0, 0))), edge)


def pack_first_kernel(gate_ref, up_ref, down_ref, first_ref, pair_ref):
    gate, up = gate_ref[...].astype(jnp.float32), up_ref[...].astype(jnp.float32)
    down = down_ref[...].astype(jnp.float32)
    blank = jnp.zeros((first_ref.shape[0] - down.shape[0], down.shape[1]), jnp.float32)
    first_ref[...] = jnp.concatenate([down, blank], axis=0).astype(jnp.bfloat16)
    pair_ref[...] = jnp.concatenate([gate, up], axis=0).astype(jnp.bfloat16)


def pack_first(gate, up, down):
    rows, width = gate.shape
    return pl.pallas_call(
        pack_first_kernel,
        out_shape=(
            jax.ShapeDtypeStruct((rows + -rows % 8, width), gate.dtype),
            jax.ShapeDtypeStruct((2 * rows, width), gate.dtype),
        ),
        name="pack_first",
    )(gate, up, down)


def pack_second_kernel(pair_ref, other_ref, out_ref):
    pair, other = pair_ref[...].astype(jnp.float32), other_ref[...].astype(jnp.float32)
    out_ref[...] = jnp.concatenate([pair, other], axis=0).astype(jnp.bfloat16)


def pack_second(pair, other):
    return pl.pallas_call(
        pack_second_kernel,
        out_shape=jax.ShapeDtypeStruct((2 * pair.shape[0], pair.shape[1]), pair.dtype),
        name="pack_second",
    )(pair, other)


def build_table(taps_ref, channel, table_ref):
    seq_len = taps_ref.shape[2]
    taps = jnp.broadcast_to(taps_ref[channel].astype(jnp.float32), (8, seq_len))
    base = jnp.concatenate([taps, jnp.zeros((8, LANES), jnp.float32)], axis=1)
    base = pltpu.roll(base, 0, 1, stride=1, stride_axis=0)
    for pair in range(LANES // 16):
        parts = []
        for shift in (16 * pair, 16 * pair + 8):
            moved = pltpu.roll(base, shift, 1) if shift else base
            parts.append(moved[:, :seq_len])
        table_ref[16 * pair : 16 * pair + 16, :] = jnp.concatenate(parts, axis=0).astype(
            jnp.bfloat16
        )


def apply_table(gated_ref, bias_ref, channel, table_ref, out_ref):
    rows = gated_ref.shape[1]
    gated = gated_ref[channel].astype(jnp.float32)
    tiles = rows // 8
    left = []
    for skip in range(tiles):
        keep = rows - 8 * skip
        left.append(jnp.concatenate([gated[:keep, :LANES], gated[:keep, LANES:]], axis=0).astype(jnp.bfloat16))
    zero = jnp.zeros((8, LANES), jnp.float32)
    total = [[zero] * tiles, [zero] * tiles]
    row = lax.broadcasted_iota(jnp.int32, (rows, LANES), 0)
    carried = [zero] * tiles
    for rho in range(8):
        sums = [carried, [zero] * tiles]
        carried = [zero] * tiles
        for skip in range(tiles):
            step = 8 * skip + rho
            keep = rows - 8 * skip
            part = jnp.dot(left[skip], table_ref[:, 2 * LANES * step : 2 * LANES * (step + 1)], preferred_element_type=jnp.float32)
            for lane_half in range(2):
                for row_half in range(2):
                    move = (2 * step + lane_half + row_half) // 2
                    if move >= rows: continue
                    side = (lane_half + row_half) % 2
                    target = sums[side] if move == step else carried
                    first = move // 8
                    for tile in range(tiles - first):
                        start = row_half * keep + 8 * tile
                        target[tile + first] = target[tile + first] + part[start:start + 8, lane_half * LANES:(lane_half + 1) * LANES]
        for side in range(2):
            if rho == 0:
                moved = sums[side]
            else:
                moved = jnp.concatenate(sums[side], axis=0)
                moved = jnp.where(row >= rho, pltpu.roll(moved, rho, 0), 0.0)
                moved = [moved[8*t:8*t+8] for t in range(tiles)]
            total[side] = [a + b for a, b in zip(total[side], moved)]
    total[0] = [a + b for a, b in zip(total[0], carried)]
    whole = jnp.concatenate([jnp.concatenate(total[0], axis=0), jnp.concatenate(total[1], axis=0)], axis=1)
    out_ref[channel] = (whole + bias_ref[channel] * gated).astype(jnp.bfloat16)

def conv_kernel(bias_ref, gated_ref, taps_ref, out_ref, even_ref, odd_ref):
    channels = gated_ref.shape[0]
    build_table(taps_ref, 0, even_ref)
    def body(step, carry):
        channel = 2 * step
        build_table(taps_ref, channel + 1, odd_ref)
        apply_table(gated_ref, bias_ref, channel, even_ref, out_ref)
        build_table(taps_ref, lax.rem(channel + 2, channels), even_ref)
        apply_table(gated_ref, bias_ref, channel + 1, odd_ref, out_ref)
        return carry
    lax.fori_loop(0, channels // 2, body, 0)

def long_mixing(gated, taps, bias):
    channels, rows, width = gated.shape
    seq_len = rows * width
    return pl.pallas_call(conv_kernel,
        out_shape=jax.ShapeDtypeStruct(gated.shape, jnp.bfloat16),
        in_specs=[pl.BlockSpec(memory_space=pltpu.SMEM), pl.BlockSpec(memory_space=pltpu.VMEM), pl.BlockSpec(memory_space=pltpu.VMEM)],
        out_specs=pl.BlockSpec(memory_space=pltpu.VMEM),
        scratch_shapes=[pltpu.VMEM((LANES, seq_len), jnp.bfloat16)]*2,
        compiler_params=pltpu.CompilerParams(vmem_limit_bytes=24*1024*1024),
        cost_estimate=pl.CostEstimate(flops=8 * channels * seq_len * seq_len, bytes_accessed=6*channels*seq_len, transcendentals=0),
        name="long_mixing")(bias, gated, taps.reshape(channels, 1, seq_len))


def payload_kernel(query_ref, mixed_ref, gain_ref, hyena_ref, out_ref):
    rows = query_ref.shape[0]
    hyena = (query_ref[...] * mixed_ref[...].astype(jnp.float32)).astype(jnp.bfloat16)
    hyena_ref[...] = hyena
    wide = hyena.astype(jnp.float32)
    scaled = (wide * gain_ref[...]).astype(jnp.bfloat16)
    rest = jnp.sum(wide * wide, axis=0, keepdims=True)
    place = lax.broadcasted_iota(jnp.int32, (out_ref.shape[1] - rows, wide.shape[1]), 0)
    extra = jnp.zeros(place.shape, jnp.float32)
    for index in range(3):
        part = rest.astype(jnp.bfloat16).astype(jnp.float32)
        extra = jnp.where(place == index, part, extra)
        rest = rest - part
    for member in range(out_ref.shape[0]):
        out_ref[member, :rows, :] = scaled
        out_ref[member, rows:, :] = extra.astype(jnp.bfloat16)


def make_payload(query, mixed, gain, members):
    rows, width = query.shape
    return pl.pallas_call(
        payload_kernel,
        out_shape=(
            jax.ShapeDtypeStruct((rows, width), jnp.bfloat16),
            jax.ShapeDtypeStruct((members, rows + 16, width), jnp.bfloat16),
        ),
        name="make_payload",
    )(query, mixed, gain.reshape(rows, 1))


def feed_kernel(
    sizes, core_ref, sent_ref, weight_ref, p0_ref, p1_ref, p2_ref, p3_ref, out_ref,
    x_ref, scale_ref, hidden_ref, flat_ref, piece_ref, piece_sem,
):
    units, block, per_step, first_steps = sizes
    step = pl.program_id(0)
    members, rows = sent_ref.shape[0], out_ref.shape[2]
    core = core_ref[0]
    length = p0_ref.shape[0]
    copies = []
    for index, ref in enumerate((p0_ref, p1_ref, p2_ref, p3_ref)):
        slot = 2 * (index // 2) + (core if index % 2 == 0 else 1 - core)
        target = piece_ref.at[pl.ds(pl.multiple_of(slot * length, 16), length), :]
        copies.append(pltpu.make_async_copy(ref, target, piece_sem.at[index]))

    @pl.when(step == 0)
    def _():
        for copy in copies:
            copy.start()
        squares = jnp.zeros((1, x_ref.shape[1]), jnp.float32)
        for member in range(members):
            x_ref[member * rows : (member + 1) * rows, :] = sent_ref[member, :rows, :]
            extra = sent_ref[member, rows:, :].astype(jnp.float32)
            squares = squares + (extra[0:1] + extra[1:2] + extra[2:3])
        scale = lax.rsqrt(squares / (members * rows) + EPSILON)
        scale_ref[...] = jnp.broadcast_to(scale, scale_ref.shape)

    @pl.when(step < first_steps)
    def _():
        scale = scale_ref[0:1, :]
        sums = jnp.dot(weight_ref[...], x_ref[...], preferred_element_type=jnp.float32) * scale
        height = weight_ref.shape[0] // per_step
        for index in range(per_step):
            part = sums[index * height : (index + 1) * height]
            for side in range(2):
                base = 2 * side * units
                gate, up = part[base : base + units], part[base + units : base + 2 * units]
                value = gate / (1.0 + jnp.exp(-gate)) * up
                blank = jnp.zeros((block - units, value.shape[1]), jnp.float32)
                start = (2 * side + index % 2) * length
                start += (step * (per_step // 2) + index // 2) * block
                hidden_ref[pl.ds(pl.multiple_of(start, 8), block), :] = jnp.concatenate(
                    [value, blank], axis=0
                )

    @pl.when(step == first_steps)
    def _():
        for copy in copies:
            copy.wait()
        flat_ref[...] = hidden_ref[...].T.astype(jnp.bfloat16)

    @pl.when(step >= first_steps)
    def _():
        wide = out_ref.shape[0] * rows
        start = pl.multiple_of((step - first_steps) * wide, LANES)
        total = jnp.dot(
            flat_ref[...], piece_ref[:, pl.ds(start, wide)], preferred_element_type=jnp.float32
        )
        for member in range(out_ref.shape[0]):
            out_ref[member] = total[:, member * rows : (member + 1) * rows].astype(jnp.bfloat16)


def feed_forward(sent, weights, pieces, core, units):
    members, padded, width = sent.shape
    channels = weights.shape[1]
    rows = channels // members
    length = pieces[0].shape[0]
    block = units + -units % 8
    blocks = 2 * length // block
    per_step, out_step = 4, 2
    first_steps = blocks // per_step
    anywhere = pl.BlockSpec(memory_space=pl.ANY)
    return pl.pallas_call(
        functools.partial(feed_kernel, (units, block, per_step, first_steps)),
        grid=(first_steps + members // out_step,),
        out_shape=jax.ShapeDtypeStruct((members, width, rows), jnp.bfloat16),
        in_specs=[
            pl.BlockSpec(memory_space=pltpu.SMEM),
            pl.BlockSpec(memory_space=pltpu.VMEM),
            pl.BlockSpec(
                (weights.shape[0] // first_steps, channels),
                lambda i: (jnp.minimum(i, first_steps - 1), 0),
            ),
            anywhere,
            anywhere,
            anywhere,
            anywhere,
        ],
        out_specs=pl.BlockSpec(
            (out_step, width, rows), lambda i: (jnp.maximum(i - first_steps, 0), 0, 0)
        ),
        scratch_shapes=[
            pltpu.VMEM((channels, width), jnp.bfloat16),
            pltpu.VMEM((8, width), jnp.float32),
            pltpu.VMEM((4 * length, width), jnp.float32),
            pltpu.VMEM((width, 4 * length), jnp.bfloat16),
            pltpu.VMEM((4 * length, channels), jnp.bfloat16),
            pltpu.SemaphoreType.DMA((4,)),
        ],
        compiler_params=pltpu.CompilerParams(vmem_limit_bytes=48 * 1024 * 1024),
        cost_estimate=pl.CostEstimate(flops=10**10, bytes_accessed=3 * 10**7, transcendentals=0),
        name="feed_forward",
    )(core, sent, weights, *pieces)


def swap(values, axis):
    return lax.ppermute(values, axis, [(0, 1), (1, 0)])


def per_device(
    projected, filter_taps, short_weight, skip_bias, norm_gain, gate_weight, up_weight, down_weight
):
    groups = lax.axis_size(SEQ)
    members = lax.axis_size(TP)
    local_width, block_len = filter_taps.shape
    per_group = local_width // groups
    seq_len = groups * block_len
    offset = lax.axis_index(SEQ) * per_group
    bias_part = lax.dynamic_slice_in_dim(skip_bias, offset, per_group, 0)

    first, pair = pack_first(gate_weight, up_weight, down_weight)
    own_near = lax.all_gather(first, "z", axis=0, tiled=True)
    edge = projected[:, :, block_len - 2 :].transpose(0, 2, 1).reshape(6, local_width)
    edge = lax.ppermute(
        jnp.pad(edge, ((0, 2), (0, 0))), SEQ, [(i, i + 1) for i in range(groups - 1)]
    )
    sent, query = make_gated(projected, filter_taps, short_weight, edge, groups)
    here = lax.all_to_all(sent, SEQ, split_axis=0, concat_axis=0, tiled=True)

    core = lax.axis_index("core")
    other_pair = swap(pair, "xh")
    here, other_pair = lax.optimization_barrier((here, other_pair))
    gate_up = lax.all_gather(pack_second(pair, other_pair), ("z", "core"), axis=0, tiled=True)

    here, own_near = lax.optimization_barrier((here, own_near))
    own_far = swap(own_near, "core")
    near = swap(own_near, "xh")
    here = here.transpose(1, 2, 0, 3)
    mixed_term = long_mixing(here[0], here[1].reshape(per_group, seq_len), bias_part)
    mixed_term, own_far = lax.optimization_barrier((mixed_term, own_far))
    returned = lax.all_to_all(
        mixed_term.transpose(1, 0, 2), SEQ, split_axis=0, concat_axis=0, tiled=True
    )
    gain = lax.dynamic_slice_in_dim(
        norm_gain, lax.axis_index(TP) * local_width, local_width, 0
    )
    hyena, payload = make_payload(query, returned.reshape(local_width, block_len), gain, members)
    payload, near = lax.optimization_barrier((payload, near))
    pieces = (own_near, own_far, near, swap(near, "core"))
    sent = lax.all_to_all(payload, TP, split_axis=0, concat_axis=0, tiled=True)
    partial_sum = feed_forward(sent, gate_up, pieces, core.reshape(1), gate_weight.shape[0])
    shares = lax.all_to_all(partial_sum, TP, split_axis=0, concat_axis=0, tiled=True)
    feed_out = jnp.sum(shares.astype(jnp.float32), axis=0).T
    return (hyena.astype(jnp.float32) + feed_out).astype(jnp.bfloat16)


def solution(mesh):
    fine = Mesh(mesh.devices.reshape(2, 8, 2, 4, 2), SEQ + TP)
    placed = (
        P(None, TP, SEQ),
        P(TP, SEQ),
        P(None, TP, None),
        P(TP),
        P(),
        P(SEQ + TP, None),
        P(SEQ + TP, None),
        P(SEQ + TP, None),
    )
    return jax.shard_map(
        per_device, mesh=fine, in_specs=placed, out_specs=P(TP, SEQ), check_vma=False
    )
```

```python
import functools

import jax
import jax.numpy as jnp
from jax import lax
from jax.experimental import pallas as pl
from jax.experimental.pallas import tpu as pltpu
from jax.sharding import Mesh
from jax.sharding import PartitionSpec as P

EPSILON = 1e-06
LANES = 128
SEQ = ("xh", "z", "core")
TP = ("y", "xl")


def gate_kernel(projected_ref, taps_ref, weight_ref, edge_ref, sent_ref, query_ref):
    rows, width = taps_ref.shape
    groups = sent_ref.shape[0]
    weights = weight_ref[...].T
    edges = edge_ref[...].astype(jnp.float32).T
    lane = lax.broadcasted_iota(jnp.int32, (rows, width), 1)
    shorts = []
    for index in range(3):
        value = projected_ref[index].astype(jnp.float32)
        far, near = edges[:, 2 * index : 2 * index + 1], edges[:, 2 * index + 1 : 2 * index + 2]
        once = jnp.where(lane == 0, near, pltpu.roll(value, 1, 1))
        twice = jnp.where(lane == 0, far, jnp.where(lane == 1, near, pltpu.roll(value, 2, 1)))
        taps = [weights[:, 3 * index + tap : 3 * index + tap + 1] for tap in range(3)]
        shorts.append(taps[0] * value + taps[1] * once + taps[2] * twice)
    query_ref[...] = shorts[0]
    gated = (shorts[1] * shorts[2]).astype(jnp.bfloat16)
    sent_ref[:, 0] = gated.reshape(groups, rows // groups, width)
    sent_ref[:, 1] = taps_ref[...].reshape(groups, rows // groups, width)


def make_gated(projected, taps, short_weight, edge, groups):
    count, rows, width = projected.shape
    weights = short_weight.transpose(0, 2, 1).reshape(9, rows)
    return pl.pallas_call(
        gate_kernel,
        out_shape=(
            jax.ShapeDtypeStruct((groups, 2, rows // groups, width), jnp.bfloat16),
            jax.ShapeDtypeStruct((rows, width), jnp.float32),
        ),
        name="make_gated",
    )(projected, taps, jnp.pad(weights, ((0, 7), (0, 0))), edge)


def pack_first_kernel(split, gate_ref, up_ref, down_ref, first_ref, pair_ref):
    gate, up = gate_ref[...].astype(jnp.float32), up_ref[...].astype(jnp.float32)
    down = down_ref[...].astype(jnp.float32)
    first = jnp.concatenate([down, gate[split:], up[split:]], axis=0)
    first_ref[...] = first.astype(jnp.bfloat16)
    pair_ref[...] = jnp.concatenate([gate[:split], up[:split]], axis=0).astype(jnp.bfloat16)


def pack_first(gate, up, down):
    rows, width = gate.shape
    split = rows - (-rows % 16) // 2
    return pl.pallas_call(
        functools.partial(pack_first_kernel, split),
        out_shape=(
            jax.ShapeDtypeStruct((rows + 2 * (rows - split), width), gate.dtype),
            jax.ShapeDtypeStruct((2 * split, width), gate.dtype),
        ),
        name="pack_first",
    )(gate, up, down)


def pack_second_kernel(pair_ref, other_ref, out_ref):
    pair, other = pair_ref[...].astype(jnp.float32), other_ref[...].astype(jnp.float32)
    blank = jnp.zeros((out_ref.shape[0] - 2 * pair.shape[0], pair.shape[1]), jnp.float32)
    out_ref[...] = jnp.concatenate([pair, other, blank], axis=0).astype(jnp.bfloat16)


def pack_second(pair, other):
    rows = 2 * pair.shape[0]
    return pl.pallas_call(
        pack_second_kernel,
        out_shape=jax.ShapeDtypeStruct((rows + -rows % 8, pair.shape[1]), pair.dtype),
        name="pack_second",
    )(pair, other)


def build_table(taps_ref, channel, table_ref):
    seq_len = taps_ref.shape[2]
    taps = jnp.broadcast_to(taps_ref[channel].astype(jnp.float32), (8, seq_len))
    base = jnp.concatenate([taps, jnp.zeros((8, LANES), jnp.float32)], axis=1)
    base = pltpu.roll(base, 0, 1, stride=1, stride_axis=0)
    base = jnp.concatenate([base, pltpu.roll(base, 8, 1)], axis=0).astype(jnp.bfloat16)
    for shift in range(0, LANES, 16):
        moved = pltpu.roll(base, shift, 1) if shift else base
        table_ref[shift : shift + 16, :] = moved[:, :seq_len]


def apply_table(gated_ref, bias_ref, channel, table_ref, out_ref):
    rows = gated_ref.shape[1]
    gated = gated_ref[channel].astype(jnp.float32)
    tiles = rows // 8
    left = []
    for skip in range(tiles):
        keep = rows - 8 * skip
        left.append(jnp.concatenate([gated[:keep, :LANES], gated[:keep, LANES:]], axis=0).astype(jnp.bfloat16))
    zero = jnp.zeros((8, LANES), jnp.float32)
    total = [[zero] * tiles, [zero] * tiles]
    row = lax.broadcasted_iota(jnp.int32, (rows, LANES), 0)
    carried = [zero] * tiles
    for rho in range(8):
        sums = [carried, [zero] * tiles]
        carried = [zero] * tiles
        for skip in range(tiles):
            step = 8 * skip + rho
            keep = rows - 8 * skip
            part = jnp.dot(left[skip], table_ref[:, 2 * LANES * step : 2 * LANES * (step + 1)], preferred_element_type=jnp.float32)
            for lane_half in range(2):
                for row_half in range(2):
                    move = (2 * step + lane_half + row_half) // 2
                    if move >= rows: continue
                    side = (lane_half + row_half) % 2
                    target = sums[side] if move == step else carried
                    first = move // 8
                    for tile in range(tiles - first):
                        start = row_half * keep + 8 * tile
                        target[tile + first] = target[tile + first] + part[start:start + 8, lane_half * LANES:(lane_half + 1) * LANES]
        for side in range(2):
            if rho == 0:
                moved = sums[side]
            else:
                moved = jnp.concatenate(sums[side], axis=0)
                moved = jnp.where(row >= rho, pltpu.roll(moved, rho, 0), 0.0)
                moved = [moved[8*t:8*t+8] for t in range(tiles)]
            total[side] = [a + b for a, b in zip(total[side], moved)]
    total[0] = [a + b for a, b in zip(total[0], carried)]
    whole = jnp.concatenate([jnp.concatenate(total[0], axis=0), jnp.concatenate(total[1], axis=0)], axis=1)
    out_ref[channel] = (whole + bias_ref[channel] * gated).astype(jnp.bfloat16)

def conv_kernel(bias_ref, gated_ref, taps_ref, out_ref, even_ref, odd_ref):
    channels = gated_ref.shape[0]
    build_table(taps_ref, 0, even_ref)
    def body(step, carry):
        channel = 2 * step
        build_table(taps_ref, channel + 1, odd_ref)
        apply_table(gated_ref, bias_ref, channel, even_ref, out_ref)
        build_table(taps_ref, lax.rem(channel + 2, channels), even_ref)
        apply_table(gated_ref, bias_ref, channel + 1, odd_ref, out_ref)
        return carry
    lax.fori_loop(0, channels // 2, body, 0)

def long_mixing(gated, taps, bias):
    channels, rows, width = gated.shape
    seq_len = rows * width
    return pl.pallas_call(conv_kernel,
        out_shape=jax.ShapeDtypeStruct(gated.shape, jnp.bfloat16),
        in_specs=[pl.BlockSpec(memory_space=pltpu.SMEM), pl.BlockSpec(memory_space=pltpu.VMEM), pl.BlockSpec(memory_space=pltpu.VMEM)],
        out_specs=pl.BlockSpec(memory_space=pltpu.VMEM),
        scratch_shapes=[pltpu.VMEM((LANES, seq_len), jnp.bfloat16)]*2,
        compiler_params=pltpu.CompilerParams(vmem_limit_bytes=24*1024*1024),
        cost_estimate=pl.CostEstimate(flops=8 * channels * seq_len * seq_len, bytes_accessed=6*channels*seq_len, transcendentals=0),
        name="long_mixing")(bias, gated, taps.reshape(channels, 1, seq_len))


def payload_kernel(query_ref, mixed_ref, gain_ref, hyena_ref, out_ref):
    rows = query_ref.shape[0]
    hyena = (query_ref[...] * mixed_ref[...].astype(jnp.float32)).astype(jnp.bfloat16)
    hyena_ref[...] = hyena
    wide = hyena.astype(jnp.float32)
    scaled = (wide * gain_ref[...]).astype(jnp.bfloat16)
    rest = jnp.sum(wide * wide, axis=0, keepdims=True)
    place = lax.broadcasted_iota(jnp.int32, (out_ref.shape[1] - rows, wide.shape[1]), 0)
    extra = jnp.zeros(place.shape, jnp.float32)
    for index in range(3):
        part = rest.astype(jnp.bfloat16).astype(jnp.float32)
        extra = jnp.where(place == index, part, extra)
        rest = rest - part
    for member in range(out_ref.shape[0]):
        out_ref[member, :rows, :] = scaled
        out_ref[member, rows:, :] = extra.astype(jnp.bfloat16)


def make_payload(query, mixed, gain, members):
    rows, width = query.shape
    return pl.pallas_call(
        payload_kernel,
        out_shape=(
            jax.ShapeDtypeStruct((rows, width), jnp.bfloat16),
            jax.ShapeDtypeStruct((members, rows + 16, width), jnp.bfloat16),
        ),
        name="make_payload",
    )(query, mixed, gain.reshape(rows, 1))


def gated_product(gate, up):
    return gate / (1.0 + jnp.exp(-gate)) * up


def feed_kernel(
    sizes, core_ref, sent_ref, weight_ref, p0_ref, p1_ref, p2_ref, p3_ref, out_ref,
    x_ref, scale_ref, hidden_ref, flat_ref, piece_ref, piece_sem,
):
    units, split, block, per_step, first_steps = sizes
    step = pl.program_id(0)
    members, rows = sent_ref.shape[0], out_ref.shape[2]
    core = core_ref[0]
    length = p0_ref.shape[0]
    copies = []
    for index, ref in enumerate((p0_ref, p1_ref, p2_ref, p3_ref)):
        slot = 2 * (index // 2) + (core if index % 2 == 0 else 1 - core)
        target = piece_ref.at[pl.ds(pl.multiple_of(slot * length, 16), length), :]
        copies.append(pltpu.make_async_copy(ref, target, piece_sem.at[index]))

    @pl.when(step == 0)
    def _():
        for copy in copies:
            copy.start()
        squares = jnp.zeros((1, x_ref.shape[1]), jnp.float32)
        for member in range(members):
            x_ref[member * rows : (member + 1) * rows, :] = sent_ref[member, :rows, :]
            extra = sent_ref[member, rows:, :].astype(jnp.float32)
            squares = squares + (extra[0:1] + extra[1:2] + extra[2:3])
        scale = lax.rsqrt(squares / (members * rows) + EPSILON)
        scale_ref[...] = jnp.broadcast_to(scale, scale_ref.shape)

    @pl.when(step < first_steps)
    def _():
        scale = scale_ref[0:1, :]
        sums = jnp.dot(weight_ref[...], x_ref[...], preferred_element_type=jnp.float32) * scale
        height = weight_ref.shape[0] // per_step
        for index in range(per_step):
            part = sums[index * height : (index + 1) * height]
            for side in range(2):
                base = 2 * side * split
                value = gated_product(
                    part[base : base + split], part[base + split : base + 2 * split]
                )
                blank = jnp.zeros((block - split, value.shape[1]), jnp.float32)
                start = (2 * side + index % 2) * length
                start += (step * (per_step // 2) + index // 2) * block
                hidden_ref[pl.ds(pl.multiple_of(start, 8), block), :] = jnp.concatenate(
                    [value, blank], axis=0
                )

    @pl.when(step == first_steps)
    def _():
        for copy in copies:
            copy.wait()
        tails = [
            piece_ref[start + block // 2 : start + block, :]
            for start in range(0, piece_ref.shape[0], block)
        ]
        sums = jnp.dot(
            jnp.concatenate(tails, axis=0), x_ref[...], preferred_element_type=jnp.float32
        )
        sums = sums * scale_ref[0:1, :]
        for index in range(len(tails)):
            gate_at = index * (block // 2) + units - block // 2
            up_at = gate_at + units - split
            value = gated_product(sums[gate_at:up_at], sums[up_at : up_at + units - split])
            hidden_ref[index * block + split : index * block + units, :] = value
        flat_ref[...] = hidden_ref[...].T.astype(jnp.bfloat16)

    @pl.when(step >= first_steps)
    def _():
        wide = out_ref.shape[0] * rows
        start = pl.multiple_of((step - first_steps) * wide, LANES)
        total = jnp.dot(
            flat_ref[...], piece_ref[:, pl.ds(start, wide)], preferred_element_type=jnp.float32
        )
        for member in range(out_ref.shape[0]):
            out_ref[member] = total[:, member * rows : (member + 1) * rows].astype(jnp.bfloat16)


def feed_forward(sent, weights, pieces, core, units, split):
    members, padded, width = sent.shape
    channels = weights.shape[1]
    rows = channels // members
    length = pieces[0].shape[0]
    block = 3 * units - 2 * split
    blocks = 2 * length // block
    per_step, out_step = 8, 4
    first_steps = blocks // per_step
    anywhere = pl.BlockSpec(memory_space=pl.ANY)
    return pl.pallas_call(
        functools.partial(feed_kernel, (units, split, block, per_step, first_steps)),
        grid=(first_steps + members // out_step,),
        out_shape=jax.ShapeDtypeStruct((members, width, rows), jnp.bfloat16),
        in_specs=[
            pl.BlockSpec(memory_space=pltpu.SMEM),
            pl.BlockSpec(memory_space=pltpu.VMEM),
            pl.BlockSpec(
                (weights.shape[0] // first_steps, channels),
                lambda i: (jnp.minimum(i, first_steps - 1), 0),
            ),
            anywhere,
            anywhere,
            anywhere,
            anywhere,
        ],
        out_specs=pl.BlockSpec(
            (out_step, width, rows), lambda i: (jnp.maximum(i - first_steps, 0), 0, 0)
        ),
        scratch_shapes=[
            pltpu.VMEM((channels, width), jnp.bfloat16),
            pltpu.VMEM((8, width), jnp.float32),
            pltpu.VMEM((4 * length, width), jnp.float32),
            pltpu.VMEM((width, 4 * length), jnp.bfloat16),
            pltpu.VMEM((4 * length, channels), jnp.bfloat16),
            pltpu.SemaphoreType.DMA((4,)),
        ],
        compiler_params=pltpu.CompilerParams(vmem_limit_bytes=48 * 1024 * 1024),
        cost_estimate=pl.CostEstimate(flops=10**10, bytes_accessed=3 * 10**7, transcendentals=0),
        name="feed_forward",
    )(core, sent, weights, *pieces)


def swap(values, axis):
    return lax.ppermute(values, axis, [(0, 1), (1, 0)])


def per_device(
    projected, filter_taps, short_weight, skip_bias, norm_gain, gate_weight, up_weight, down_weight
):
    groups = lax.axis_size(SEQ)
    members = lax.axis_size(TP)
    local_width, block_len = filter_taps.shape
    per_group = local_width // groups
    seq_len = groups * block_len
    offset = lax.axis_index(SEQ) * per_group
    bias_part = lax.dynamic_slice_in_dim(skip_bias, offset, per_group, 0)

    first, pair = pack_first(gate_weight, up_weight, down_weight)
    other_pair = swap(pair, "xh")
    own_near = lax.all_gather(first, "z", axis=0, tiled=True)
    edge = projected[:, :, block_len - 2 :].transpose(0, 2, 1).reshape(6, local_width)
    edge = lax.ppermute(
        jnp.pad(edge, ((0, 2), (0, 0))), SEQ, [(i, i + 1) for i in range(groups - 1)]
    )
    sent, query = make_gated(projected, filter_taps, short_weight, edge, groups)
    second = pack_second(pair, other_pair)
    sent, second = lax.optimization_barrier((sent, second))
    here = lax.all_to_all(sent, SEQ, split_axis=0, concat_axis=0, tiled=True)

    core = lax.axis_index("core")
    gate_up = lax.all_gather(second, ("z", "core"), axis=0, tiled=True)

    here, own_near = lax.optimization_barrier((here, own_near))
    own_far = swap(own_near, "core")
    near = swap(own_near, "xh")
    here = here.transpose(1, 2, 0, 3)
    mixed_term = long_mixing(here[0], here[1].reshape(per_group, seq_len), bias_part)
    mixed_term, own_far = lax.optimization_barrier((mixed_term, own_far))
    returned = lax.all_to_all(
        mixed_term.transpose(1, 0, 2), SEQ, split_axis=0, concat_axis=0, tiled=True
    )
    gain = lax.dynamic_slice_in_dim(
        norm_gain, lax.axis_index(TP) * local_width, local_width, 0
    )
    hyena, payload = make_payload(query, returned.reshape(local_width, block_len), gain, members)
    payload, near = lax.optimization_barrier((payload, near))
    pieces = (own_near, own_far, near, swap(near, "core"))
    sent = lax.all_to_all(payload, TP, split_axis=0, concat_axis=0, tiled=True)
    units, split = gate_weight.shape[0], pair.shape[0] // 2
    partial_sum = feed_forward(sent, gate_up, pieces, core.reshape(1), units, split)
    shares = lax.all_to_all(partial_sum, TP, split_axis=0, concat_axis=0, tiled=True)
    feed_out = jnp.sum(shares.astype(jnp.float32), axis=0).T
    return (hyena.astype(jnp.float32) + feed_out).astype(jnp.bfloat16)


def solution(mesh):
    fine = Mesh(mesh.devices.reshape(2, 8, 2, 4, 2), SEQ + TP)
    placed = (
        P(None, TP, SEQ),
        P(TP, SEQ),
        P(None, TP, None),
        P(TP),
        P(),
        P(SEQ + TP, None),
        P(SEQ + TP, None),
        P(SEQ + TP, None),
    )
    return jax.shard_map(
        per_device, mesh=fine, in_specs=placed, out_specs=P(TP, SEQ), check_vma=False
    )
```

```python
import functools

import jax
import jax.numpy as jnp
from jax import lax
from jax.experimental import pallas as pl
from jax.experimental.pallas import tpu as pltpu
from jax.sharding import Mesh
from jax.sharding import PartitionSpec as P

EPSILON = 1e-06
LANES = 128
SEQ = ("xh", "z", "core")
TP = ("y", "xl")


def gate_kernel(projected_ref, weight_ref, edge_ref, gated_ref, query_ref):
    rows, width = query_ref.shape
    weights = weight_ref[...].T
    edges = edge_ref[...].astype(jnp.float32).T
    lane = lax.broadcasted_iota(jnp.int32, (rows, width), 1)
    shorts = []
    for index in range(3):
        value = projected_ref[index].astype(jnp.float32)
        far, near = edges[:, 2 * index : 2 * index + 1], edges[:, 2 * index + 1 : 2 * index + 2]
        once = jnp.where(lane == 0, near, pltpu.roll(value, 1, 1))
        twice = jnp.where(lane == 0, far, jnp.where(lane == 1, near, pltpu.roll(value, 2, 1)))
        taps = [weights[:, 3 * index + tap : 3 * index + tap + 1] for tap in range(3)]
        shorts.append(taps[0] * value + taps[1] * once + taps[2] * twice)
    query_ref[...] = shorts[0]
    gated_ref[...] = (shorts[1] * shorts[2]).astype(jnp.bfloat16)


def make_gated(projected, short_weight, edge):
    count, rows, width = projected.shape
    weights = short_weight.transpose(0, 2, 1).reshape(9, rows)
    return pl.pallas_call(
        gate_kernel,
        out_shape=(
            jax.ShapeDtypeStruct((rows, width), jnp.bfloat16),
            jax.ShapeDtypeStruct((rows, width), jnp.float32),
        ),
        name="make_gated",
    )(projected, jnp.pad(weights, ((0, 7), (0, 0))), edge)


def pack_first_kernel(gate_ref, up_ref, down_ref, first_ref, pair_ref):
    gate, up = gate_ref[...].astype(jnp.float32), up_ref[...].astype(jnp.float32)
    down = down_ref[...].astype(jnp.float32)
    blank = jnp.zeros((first_ref.shape[0] - down.shape[0], down.shape[1]), jnp.float32)
    first_ref[...] = jnp.concatenate([down, blank], axis=0).astype(jnp.bfloat16)
    pair_ref[...] = jnp.concatenate([gate, up], axis=0).astype(jnp.bfloat16)


def pack_first(gate, up, down):
    rows, width = gate.shape
    return pl.pallas_call(
        pack_first_kernel,
        out_shape=(
            jax.ShapeDtypeStruct((rows + -rows % 8, width), gate.dtype),
            jax.ShapeDtypeStruct((2 * rows, width), gate.dtype),
        ),
        name="pack_first",
    )(gate, up, down)


def pack_second_kernel(pair_ref, other_ref, out_ref):
    pair, other = pair_ref[...].astype(jnp.float32), other_ref[...].astype(jnp.float32)
    out_ref[...] = jnp.concatenate([pair, other], axis=0).astype(jnp.bfloat16)


def pack_second(pair, other):
    return pl.pallas_call(
        pack_second_kernel,
        out_shape=jax.ShapeDtypeStruct((2 * pair.shape[0], pair.shape[1]), pair.dtype),
        name="pack_second",
    )(pair, other)


def build_table(taps_ref, channel, table_ref):
    seq_len = taps_ref.shape[2]
    taps = jnp.broadcast_to(taps_ref[channel].astype(jnp.float32), (8, seq_len))
    base = jnp.concatenate([taps, jnp.zeros((8, LANES), jnp.float32)], axis=1)
    base = pltpu.roll(base, 0, 1, stride=1, stride_axis=0)
    base = jnp.concatenate([base, pltpu.roll(base, 8, 1)], axis=0).astype(jnp.bfloat16)
    for shift in range(0, LANES, 16):
        moved = pltpu.roll(base, shift, 1) if shift else base
        table_ref[shift : shift + 16, :] = moved[:, :seq_len]


def apply_table(gated_ref, bias_ref, channel, table_ref, out_ref):
    rows = gated_ref.shape[1]
    gated = gated_ref[channel].astype(jnp.float32)
    tiles = rows // 8
    left = []
    for skip in range(tiles):
        keep = rows - 8 * skip
        left.append(jnp.concatenate([gated[:keep, :LANES], gated[:keep, LANES:]], axis=0).astype(jnp.bfloat16))
    zero = jnp.zeros((8, LANES), jnp.float32)
    total = [[zero] * tiles, [zero] * tiles]
    row = lax.broadcasted_iota(jnp.int32, (rows, LANES), 0)
    carried = [zero] * tiles
    for rho in range(8):
        sums = [carried, [zero] * tiles]
        carried = [zero] * tiles
        for skip in range(tiles):
            step = 8 * skip + rho
            keep = rows - 8 * skip
            part = jnp.dot(left[skip], table_ref[:, 2 * LANES * step : 2 * LANES * (step + 1)], preferred_element_type=jnp.float32)
            for lane_half in range(2):
                for row_half in range(2):
                    move = (2 * step + lane_half + row_half) // 2
                    if move >= rows: continue
                    side = (lane_half + row_half) % 2
                    target = sums[side] if move == step else carried
                    first = move // 8
                    for tile in range(tiles - first):
                        start = row_half * keep + 8 * tile
                        target[tile + first] = target[tile + first] + part[start:start + 8, lane_half * LANES:(lane_half + 1) * LANES]
        for side in range(2):
            if rho == 0:
                moved = sums[side]
            else:
                moved = jnp.concatenate(sums[side], axis=0)
                moved = jnp.where(row >= rho, pltpu.roll(moved, rho, 0), 0.0)
                moved = [moved[8*t:8*t+8] for t in range(tiles)]
            total[side] = [a + b for a, b in zip(total[side], moved)]
    total[0] = [a + b for a, b in zip(total[0], carried)]
    whole = jnp.concatenate([jnp.concatenate(total[0], axis=0), jnp.concatenate(total[1], axis=0)], axis=1)
    out_ref[channel] = (whole + bias_ref[channel] * gated).astype(jnp.bfloat16)

def conv_kernel(bias_ref, gated_ref, taps_ref, out_ref, even_ref, odd_ref):
    channels = gated_ref.shape[0]
    build_table(taps_ref, 0, even_ref)
    def body(step, carry):
        channel = 2 * step
        build_table(taps_ref, channel + 1, odd_ref)
        apply_table(gated_ref, bias_ref, channel, even_ref, out_ref)
        build_table(taps_ref, lax.rem(channel + 2, channels), even_ref)
        apply_table(gated_ref, bias_ref, channel + 1, odd_ref, out_ref)
        return carry
    lax.fori_loop(0, channels // 2, body, 0)

def long_mixing(gated, taps, bias):
    channels, rows, width = gated.shape
    seq_len = rows * width
    return pl.pallas_call(conv_kernel,
        out_shape=jax.ShapeDtypeStruct(gated.shape, jnp.bfloat16),
        in_specs=[pl.BlockSpec(memory_space=pltpu.SMEM), pl.BlockSpec(memory_space=pltpu.VMEM), pl.BlockSpec(memory_space=pltpu.VMEM)],
        out_specs=pl.BlockSpec(memory_space=pltpu.VMEM),
        scratch_shapes=[pltpu.VMEM((LANES, seq_len), jnp.bfloat16)]*2,
        compiler_params=pltpu.CompilerParams(vmem_limit_bytes=24*1024*1024),
        cost_estimate=pl.CostEstimate(flops=8 * channels * seq_len * seq_len, bytes_accessed=6*channels*seq_len, transcendentals=0),
        name="long_mixing")(bias, gated, taps.reshape(channels, 1, seq_len))


def payload_kernel(query_ref, mixed_ref, gain_ref, hyena_ref, out_ref):
    rows = query_ref.shape[0]
    hyena = (query_ref[...] * mixed_ref[...].astype(jnp.float32)).astype(jnp.bfloat16)
    hyena_ref[...] = hyena
    wide = hyena.astype(jnp.float32)
    scaled = (wide * gain_ref[...]).astype(jnp.bfloat16)
    rest = jnp.sum(wide * wide, axis=0, keepdims=True)
    place = lax.broadcasted_iota(jnp.int32, (out_ref.shape[1] - rows, wide.shape[1]), 0)
    extra = jnp.zeros(place.shape, jnp.float32)
    for index in range(3):
        part = rest.astype(jnp.bfloat16).astype(jnp.float32)
        extra = jnp.where(place == index, part, extra)
        rest = rest - part
    for member in range(out_ref.shape[0]):
        out_ref[member, :rows, :] = scaled
        out_ref[member, rows:, :] = extra.astype(jnp.bfloat16)


def make_payload(query, mixed, gain, members):
    rows, width = query.shape
    return pl.pallas_call(
        payload_kernel,
        out_shape=(
            jax.ShapeDtypeStruct((rows, width), jnp.bfloat16),
            jax.ShapeDtypeStruct((members, rows + 16, width), jnp.bfloat16),
        ),
        name="make_payload",
    )(query, mixed, gain.reshape(rows, 1))


def feed_kernel(
    sizes, core_ref, sent_ref, weight_ref, p0_ref, p1_ref, p2_ref, p3_ref, out_ref,
    x_ref, scale_ref, hidden_ref, flat_ref, piece_ref, piece_sem,
):
    units, block, per_step, first_steps = sizes
    step = pl.program_id(0)
    members, rows = sent_ref.shape[0], out_ref.shape[2]
    core = core_ref[0]
    length = p0_ref.shape[0]
    copies = []
    for index, ref in enumerate((p0_ref, p1_ref, p2_ref, p3_ref)):
        slot = 2 * (index // 2) + (core if index % 2 == 0 else 1 - core)
        target = piece_ref.at[pl.ds(pl.multiple_of(slot * length, 16), length), :]
        copies.append(pltpu.make_async_copy(ref, target, piece_sem.at[index]))

    @pl.when(step == 0)
    def _():
        for copy in copies:
            copy.start()
        squares = jnp.zeros((1, x_ref.shape[1]), jnp.float32)
        for member in range(members):
            x_ref[member * rows : (member + 1) * rows, :] = sent_ref[member, :rows, :]
            extra = sent_ref[member, rows:, :].astype(jnp.float32)
            squares = squares + (extra[0:1] + extra[1:2] + extra[2:3])
        scale = lax.rsqrt(squares / (members * rows) + EPSILON)
        scale_ref[...] = jnp.broadcast_to(scale, scale_ref.shape)

    @pl.when(step < first_steps)
    def _():
        scale = scale_ref[0:1, :]
        sums = jnp.dot(weight_ref[...], x_ref[...], preferred_element_type=jnp.float32) * scale
        height = weight_ref.shape[0] // per_step
        for index in range(per_step):
            part = sums[index * height : (index + 1) * height]
            for side in range(2):
                base = 2 * side * units
                gate, up = part[base : base + units], part[base + units : base + 2 * units]
                value = gate / (1.0 + jnp.exp(-gate)) * up
                blank = jnp.zeros((block - units, value.shape[1]), jnp.float32)
                start = (2 * side + index % 2) * length
                start += (step * (per_step // 2) + index // 2) * block
                hidden_ref[pl.ds(pl.multiple_of(start, 8), block), :] = jnp.concatenate(
                    [value, blank], axis=0
                )

    @pl.when(step == first_steps)
    def _():
        for copy in copies:
            copy.wait()
        flat_ref[...] = hidden_ref[...].T.astype(jnp.bfloat16)

    @pl.when(step >= first_steps)
    def _():
        wide = out_ref.shape[0] * rows
        start = pl.multiple_of((step - first_steps) * wide, LANES)
        total = jnp.dot(
            flat_ref[...], piece_ref[:, pl.ds(start, wide)], preferred_element_type=jnp.float32
        )
        for member in range(out_ref.shape[0]):
            out_ref[member] = total[:, member * rows : (member + 1) * rows].astype(jnp.bfloat16)


def feed_forward(sent, weights, pieces, core, units):
    members, padded, width = sent.shape
    channels = weights.shape[1]
    rows = channels // members
    length = pieces[0].shape[0]
    block = units + -units % 8
    blocks = 2 * length // block
    per_step, out_step = 8, 4
    first_steps = blocks // per_step
    anywhere = pl.BlockSpec(memory_space=pl.ANY)
    return pl.pallas_call(
        functools.partial(feed_kernel, (units, block, per_step, first_steps)),
        grid=(first_steps + members // out_step,),
        out_shape=jax.ShapeDtypeStruct((members, width, rows), jnp.bfloat16),
        in_specs=[
            pl.BlockSpec(memory_space=pltpu.SMEM),
            pl.BlockSpec(memory_space=pltpu.VMEM),
            pl.BlockSpec(
                (weights.shape[0] // first_steps, channels),
                lambda i: (jnp.minimum(i, first_steps - 1), 0),
            ),
            anywhere,
            anywhere,
            anywhere,
            anywhere,
        ],
        out_specs=pl.BlockSpec(
            (out_step, width, rows), lambda i: (jnp.maximum(i - first_steps, 0), 0, 0)
        ),
        scratch_shapes=[
            pltpu.VMEM((channels, width), jnp.bfloat16),
            pltpu.VMEM((8, width), jnp.float32),
            pltpu.VMEM((4 * length, width), jnp.float32),
            pltpu.VMEM((width, 4 * length), jnp.bfloat16),
            pltpu.VMEM((4 * length, channels), jnp.bfloat16),
            pltpu.SemaphoreType.DMA((4,)),
        ],
        compiler_params=pltpu.CompilerParams(vmem_limit_bytes=48 * 1024 * 1024),
        cost_estimate=pl.CostEstimate(flops=10**10, bytes_accessed=3 * 10**7, transcendentals=0),
        name="feed_forward",
    )(core, sent, weights, *pieces)


def swap(values, axis):
    return lax.ppermute(values, axis, [(0, 1), (1, 0)])


def per_device(
    projected, filter_taps, short_weight, skip_bias, norm_gain, gate_weight, up_weight, down_weight
):
    groups = lax.axis_size(SEQ)
    members = lax.axis_size(TP)
    local_width, block_len = filter_taps.shape
    per_group = local_width // groups
    seq_len = groups * block_len
    offset = lax.axis_index(SEQ) * per_group
    bias_part = lax.dynamic_slice_in_dim(skip_bias, offset, per_group, 0)

    first, pair = pack_first(gate_weight, up_weight, down_weight)
    own_near = lax.all_gather(first, "z", axis=0, tiled=True)
    edge = projected[:, :, block_len - 2 :].transpose(0, 2, 1).reshape(6, local_width)
    edge = lax.ppermute(
        jnp.pad(edge, ((0, 2), (0, 0))), SEQ, [(i, i + 1) for i in range(groups - 1)]
    )
    taps = lax.all_to_all(
        filter_taps.reshape(groups, per_group, block_len),
        SEQ,
        split_axis=0,
        concat_axis=0,
        tiled=True,
    )
    gated, query = make_gated(projected, short_weight, edge)
    other_pair = swap(pair, "xh")
    second = pack_second(pair, other_pair)
    gated, taps, second = lax.optimization_barrier((gated, taps, second))
    here = lax.all_to_all(
        gated.reshape(groups, per_group, block_len), SEQ, split_axis=0, concat_axis=0, tiled=True
    )

    core = lax.axis_index("core")
    gate_up = lax.all_gather(second, ("z", "core"), axis=0, tiled=True)

    here, own_near = lax.optimization_barrier((here, own_near))
    own_far = swap(own_near, "core")
    near = swap(own_near, "xh")
    taps = taps.transpose(1, 0, 2).reshape(per_group, seq_len)
    mixed_term = long_mixing(here.transpose(1, 0, 2), taps, bias_part)
    mixed_term, own_far = lax.optimization_barrier((mixed_term, own_far))
    returned = lax.all_to_all(
        mixed_term.transpose(1, 0, 2), SEQ, split_axis=0, concat_axis=0, tiled=True
    )
    gain = lax.dynamic_slice_in_dim(
        norm_gain, lax.axis_index(TP) * local_width, local_width, 0
    )
    hyena, payload = make_payload(query, returned.reshape(local_width, block_len), gain, members)
    payload, near = lax.optimization_barrier((payload, near))
    pieces = (own_near, own_far, near, swap(near, "core"))
    sent = lax.all_to_all(payload, TP, split_axis=0, concat_axis=0, tiled=True)
    partial_sum = feed_forward(sent, gate_up, pieces, core.reshape(1), gate_weight.shape[0])
    shares = lax.all_to_all(partial_sum, TP, split_axis=0, concat_axis=0, tiled=True)
    feed_out = jnp.sum(shares.astype(jnp.float32), axis=0).T
    return (hyena.astype(jnp.float32) + feed_out).astype(jnp.bfloat16)


def solution(mesh):
    fine = Mesh(mesh.devices.reshape(2, 8, 2, 4, 2), SEQ + TP)
    placed = (
        P(None, TP, SEQ),
        P(TP, SEQ),
        P(None, TP, None),
        P(TP),
        P(),
        P(SEQ + TP, None),
        P(SEQ + TP, None),
        P(SEQ + TP, None),
    )
    return jax.shard_map(
        per_device, mesh=fine, in_specs=placed, out_specs=P(TP, SEQ), check_vma=False
    )
```

```python
import functools

import jax
import jax.numpy as jnp
from jax import lax
from jax.experimental import pallas as pl
from jax.experimental.pallas import tpu as pltpu
from jax.sharding import Mesh
from jax.sharding import PartitionSpec as P

EPSILON = 1e-06
LANES = 128
SEQ = ("xh", "z", "core")
TP = ("y", "xl")


def gate_kernel(projected_ref, weight_ref, edge_ref, gated_ref, query_ref):
    rows, width = query_ref.shape
    weights = weight_ref[...].T
    edges = edge_ref[...].astype(jnp.float32).T
    lane = lax.broadcasted_iota(jnp.int32, (rows, width), 1)
    shorts = []
    for index in range(3):
        value = projected_ref[index].astype(jnp.float32)
        far, near = edges[:, 2 * index : 2 * index + 1], edges[:, 2 * index + 1 : 2 * index + 2]
        once = jnp.where(lane == 0, near, pltpu.roll(value, 1, 1))
        twice = jnp.where(lane == 0, far, jnp.where(lane == 1, near, pltpu.roll(value, 2, 1)))
        taps = [weights[:, 3 * index + tap : 3 * index + tap + 1] for tap in range(3)]
        shorts.append(taps[0] * value + taps[1] * once + taps[2] * twice)
    query_ref[...] = shorts[0]
    gated_ref[...] = (shorts[1] * shorts[2]).astype(jnp.bfloat16)


def make_gated(projected, short_weight, edge):
    count, rows, width = projected.shape
    weights = short_weight.transpose(0, 2, 1).reshape(9, rows)
    return pl.pallas_call(
        gate_kernel,
        out_shape=(
            jax.ShapeDtypeStruct((rows, width), jnp.bfloat16),
            jax.ShapeDtypeStruct((rows, width), jnp.float32),
        ),
        name="make_gated",
    )(projected, jnp.pad(weights, ((0, 7), (0, 0))), edge)


def pack_first_kernel(gate_ref, up_ref, down_ref, first_ref, pair_ref):
    gate, up = gate_ref[...].astype(jnp.float32), up_ref[...].astype(jnp.float32)
    down = down_ref[...].astype(jnp.float32)
    blank = jnp.zeros((first_ref.shape[0] - down.shape[0], down.shape[1]), jnp.float32)
    first_ref[...] = jnp.concatenate([down, blank], axis=0).astype(jnp.bfloat16)
    pair_ref[...] = jnp.concatenate([gate, up], axis=0).astype(jnp.bfloat16)


def pack_first(gate, up, down):
    rows, width = gate.shape
    return pl.pallas_call(
        pack_first_kernel,
        out_shape=(
            jax.ShapeDtypeStruct((rows + -rows % 8, width), gate.dtype),
            jax.ShapeDtypeStruct((2 * rows, width), gate.dtype),
        ),
        name="pack_first",
    )(gate, up, down)


def pack_second_kernel(pair_ref, other_ref, out_ref):
    pair, other = pair_ref[...].astype(jnp.float32), other_ref[...].astype(jnp.float32)
    out_ref[...] = jnp.concatenate([pair, other], axis=0).astype(jnp.bfloat16)


def pack_second(pair, other):
    return pl.pallas_call(
        pack_second_kernel,
        out_shape=jax.ShapeDtypeStruct((2 * pair.shape[0], pair.shape[1]), pair.dtype),
        name="pack_second",
    )(pair, other)


def build_table(taps_ref, channel, table_ref):
    seq_len = taps_ref.shape[2]
    taps = jnp.broadcast_to(taps_ref[channel].astype(jnp.float32), (8, seq_len))
    base = jnp.concatenate([taps, jnp.zeros((8, LANES), jnp.float32)], axis=1)
    base = pltpu.roll(base, 0, 1, stride=1, stride_axis=0)
    base = jnp.concatenate([base, pltpu.roll(base, 8, 1)], axis=0).astype(jnp.bfloat16)
    for shift in range(0, LANES, 16):
        moved = pltpu.roll(base, shift, 1) if shift else base
        table_ref[shift : shift + 16, :] = moved[:, :seq_len]


def apply_table(gated_ref, bias_ref, channel, table_ref, out_ref):
    rows = gated_ref.shape[1]
    gated = gated_ref[channel].astype(jnp.float32)
    tiles = rows // 8
    left = []
    for skip in range(tiles):
        keep = rows - 8 * skip
        left.append(jnp.concatenate([gated[:keep, :LANES], gated[:keep, LANES:]], axis=0).astype(jnp.bfloat16))
    zero = jnp.zeros((8, LANES), jnp.float32)
    total = [[zero] * tiles, [zero] * tiles]
    row = lax.broadcasted_iota(jnp.int32, (rows, LANES), 0)
    carried = [zero] * tiles
    for rho in range(8):
        sums = [carried, [zero] * tiles]
        carried = [zero] * tiles
        for skip in range(tiles):
            step = 8 * skip + rho
            keep = rows - 8 * skip
            part = jnp.dot(left[skip], table_ref[:, 2 * LANES * step : 2 * LANES * (step + 1)], preferred_element_type=jnp.float32)
            for lane_half in range(2):
                for row_half in range(2):
                    move = (2 * step + lane_half + row_half) // 2
                    if move >= rows: continue
                    side = (lane_half + row_half) % 2
                    target = sums[side] if move == step else carried
                    first = move // 8
                    for tile in range(tiles - first):
                        start = row_half * keep + 8 * tile
                        target[tile + first] = target[tile + first] + part[start:start + 8, lane_half * LANES:(lane_half + 1) * LANES]
        for side in range(2):
            if rho == 0:
                moved = sums[side]
            else:
                moved = jnp.concatenate(sums[side], axis=0)
                moved = jnp.where(row >= rho, pltpu.roll(moved, rho, 0), 0.0)
                moved = [moved[8*t:8*t+8] for t in range(tiles)]
            total[side] = [a + b for a, b in zip(total[side], moved)]
    total[0] = [a + b for a, b in zip(total[0], carried)]
    whole = jnp.concatenate([jnp.concatenate(total[0], axis=0), jnp.concatenate(total[1], axis=0)], axis=1)
    out_ref[channel] = (whole + bias_ref[channel] * gated).astype(jnp.bfloat16)

def conv_kernel(bias_ref, gated_ref, taps_ref, out_ref, even_ref, odd_ref):
    channels = gated_ref.shape[0]
    build_table(taps_ref, 0, even_ref)
    def body(step, carry):
        channel = 2 * step
        build_table(taps_ref, channel + 1, odd_ref)
        apply_table(gated_ref, bias_ref, channel, even_ref, out_ref)
        build_table(taps_ref, lax.rem(channel + 2, channels), even_ref)
        apply_table(gated_ref, bias_ref, channel + 1, odd_ref, out_ref)
        return carry
    lax.fori_loop(0, channels // 2, body, 0)

def long_mixing(gated, taps, bias):
    channels, rows, width = gated.shape
    seq_len = rows * width
    return pl.pallas_call(conv_kernel,
        out_shape=jax.ShapeDtypeStruct(gated.shape, jnp.bfloat16),
        in_specs=[pl.BlockSpec(memory_space=pltpu.SMEM), pl.BlockSpec(memory_space=pltpu.VMEM), pl.BlockSpec(memory_space=pltpu.VMEM)],
        out_specs=pl.BlockSpec(memory_space=pltpu.VMEM),
        scratch_shapes=[pltpu.VMEM((LANES, seq_len), jnp.bfloat16)]*2,
        compiler_params=pltpu.CompilerParams(vmem_limit_bytes=24*1024*1024),
        cost_estimate=pl.CostEstimate(flops=8 * channels * seq_len * seq_len, bytes_accessed=6*channels*seq_len, transcendentals=0),
        name="long_mixing")(bias, gated, taps.reshape(channels, 1, seq_len))


def payload_kernel(query_ref, mixed_ref, gain_ref, hyena_ref, out_ref):
    rows = query_ref.shape[0]
    hyena = (query_ref[...] * mixed_ref[...].astype(jnp.float32)).astype(jnp.bfloat16)
    hyena_ref[...] = hyena
    wide = hyena.astype(jnp.float32)
    scaled = (wide * gain_ref[...]).astype(jnp.bfloat16)
    rest = jnp.sum(wide * wide, axis=0, keepdims=True)
    place = lax.broadcasted_iota(jnp.int32, (out_ref.shape[1] - rows, wide.shape[1]), 0)
    extra = jnp.zeros(place.shape, jnp.float32)
    for index in range(3):
        part = rest.astype(jnp.bfloat16).astype(jnp.float32)
        extra = jnp.where(place == index, part, extra)
        rest = rest - part
    for member in range(out_ref.shape[0]):
        out_ref[member, :rows, :] = scaled
        out_ref[member, rows:, :] = extra.astype(jnp.bfloat16)


def make_payload(query, mixed, gain, members):
    rows, width = query.shape
    return pl.pallas_call(
        payload_kernel,
        out_shape=(
            jax.ShapeDtypeStruct((rows, width), jnp.bfloat16),
            jax.ShapeDtypeStruct((members, rows + 16, width), jnp.bfloat16),
        ),
        name="make_payload",
    )(query, mixed, gain.reshape(rows, 1))


def feed_kernel(
    sizes, core_ref, sent_ref, weight_ref, p0_ref, p1_ref, p2_ref, p3_ref, out_ref,
    x_ref, scale_ref, hidden_ref, flat_ref, piece_ref, piece_sem,
):
    units, block, per_step, first_steps = sizes
    step = pl.program_id(0)
    members, rows = sent_ref.shape[0], out_ref.shape[2]
    core = core_ref[0]
    length = p0_ref.shape[0]
    copies = []
    for index, ref in enumerate((p0_ref, p1_ref, p2_ref, p3_ref)):
        slot = 2 * (index // 2) + (core if index % 2 == 0 else 1 - core)
        target = piece_ref.at[pl.ds(pl.multiple_of(slot * length, 16), length), :]
        copies.append(pltpu.make_async_copy(ref, target, piece_sem.at[index]))

    @pl.when(step == 0)
    def _():
        for copy in copies:
            copy.start()
        squares = jnp.zeros((1, x_ref.shape[1]), jnp.float32)
        for member in range(members):
            x_ref[member * rows : (member + 1) * rows, :] = sent_ref[member, :rows, :]
            extra = sent_ref[member, rows:, :].astype(jnp.float32)
            squares = squares + (extra[0:1] + extra[1:2] + extra[2:3])
        scale = lax.rsqrt(squares / (members * rows) + EPSILON)
        scale_ref[...] = jnp.broadcast_to(scale, scale_ref.shape)

    @pl.when(step < first_steps)
    def _():
        scale = scale_ref[0:1, :]
        sums = jnp.dot(weight_ref[...], x_ref[...], preferred_element_type=jnp.float32) * scale
        height = weight_ref.shape[0] // per_step
        for index in range(per_step):
            part = sums[index * height : (index + 1) * height]
            for side in range(2):
                base = 2 * side * units
                gate, up = part[base : base + units], part[base + units : base + 2 * units]
                value = gate / (1.0 + jnp.exp(-gate)) * up
                blank = jnp.zeros((block - units, value.shape[1]), jnp.float32)
                start = (2 * side + index % 2) * length
                start += (step * (per_step // 2) + index // 2) * block
                hidden_ref[pl.ds(pl.multiple_of(start, 8), block), :] = jnp.concatenate(
                    [value, blank], axis=0
                )

    @pl.when(step == first_steps)
    def _():
        for copy in copies:
            copy.wait()
        flat_ref[...] = hidden_ref[...].T.astype(jnp.bfloat16)

    @pl.when(step >= first_steps)
    def _():
        wide = out_ref.shape[0] * rows
        start = pl.multiple_of((step - first_steps) * wide, LANES)
        total = jnp.dot(
            flat_ref[...], piece_ref[:, pl.ds(start, wide)], preferred_element_type=jnp.float32
        )
        for member in range(out_ref.shape[0]):
            out_ref[member] = total[:, member * rows : (member + 1) * rows].astype(jnp.bfloat16)


def feed_forward(sent, weights, pieces, core, units):
    members, padded, width = sent.shape
    channels = weights.shape[1]
    rows = channels // members
    length = pieces[0].shape[0]
    block = units + -units % 8
    blocks = 2 * length // block
    per_step, out_step = 8, 4
    first_steps = blocks // per_step
    anywhere = pl.BlockSpec(memory_space=pl.ANY)
    return pl.pallas_call(
        functools.partial(feed_kernel, (units, block, per_step, first_steps)),
        grid=(first_steps + members // out_step,),
        out_shape=jax.ShapeDtypeStruct((members, width, rows), jnp.bfloat16),
        in_specs=[
            pl.BlockSpec(memory_space=pltpu.SMEM),
            pl.BlockSpec(memory_space=pltpu.VMEM),
            pl.BlockSpec(
                (weights.shape[0] // first_steps, channels),
                lambda i: (jnp.minimum(i, first_steps - 1), 0),
            ),
            anywhere,
            anywhere,
            anywhere,
            anywhere,
        ],
        out_specs=pl.BlockSpec(
            (out_step, width, rows), lambda i: (jnp.maximum(i - first_steps, 0), 0, 0)
        ),
        scratch_shapes=[
            pltpu.VMEM((channels, width), jnp.bfloat16),
            pltpu.VMEM((8, width), jnp.float32),
            pltpu.VMEM((4 * length, width), jnp.float32),
            pltpu.VMEM((width, 4 * length), jnp.bfloat16),
            pltpu.VMEM((4 * length, channels), jnp.bfloat16),
            pltpu.SemaphoreType.DMA((4,)),
        ],
        compiler_params=pltpu.CompilerParams(vmem_limit_bytes=48 * 1024 * 1024),
        cost_estimate=pl.CostEstimate(flops=10**10, bytes_accessed=3 * 10**7, transcendentals=0),
        name="feed_forward",
    )(core, sent, weights, *pieces)


def swap(values, axis):
    return lax.ppermute(values, axis, [(0, 1), (1, 0)])


def per_device(
    projected, filter_taps, short_weight, skip_bias, norm_gain, gate_weight, up_weight, down_weight
):
    groups = lax.axis_size(SEQ)
    members = lax.axis_size(TP)
    local_width, block_len = filter_taps.shape
    per_group = local_width // groups
    seq_len = groups * block_len
    offset = lax.axis_index(SEQ) * per_group
    bias_part = lax.dynamic_slice_in_dim(skip_bias, offset, per_group, 0)

    first, pair = pack_first(gate_weight, up_weight, down_weight)
    own_near = lax.all_gather(first, "z", axis=0, tiled=True)
    edge = projected[:, :, block_len - 2 :].transpose(0, 2, 1).reshape(6, local_width)
    edge = lax.ppermute(
        jnp.pad(edge, ((0, 2), (0, 0))), SEQ, [(i, i + 1) for i in range(groups - 1)]
    )
    taps = lax.all_to_all(
        filter_taps.reshape(groups, per_group, block_len),
        SEQ,
        split_axis=0,
        concat_axis=0,
        tiled=True,
    )
    gated, query = make_gated(projected, short_weight, edge)
    other_pair = swap(pair, "xh")
    gated, taps = lax.optimization_barrier((gated, taps))
    here = lax.all_to_all(
        gated.reshape(groups, per_group, block_len), SEQ, split_axis=0, concat_axis=0, tiled=True
    )

    core = lax.axis_index("core")
    here, other_pair = lax.optimization_barrier((here, other_pair))
    second = pack_second(pair, other_pair)
    gate_up = lax.all_gather(second, ("z", "core"), axis=0, tiled=True)

    here, own_near = lax.optimization_barrier((here, own_near))
    own_far = swap(own_near, "core")
    near = swap(own_near, "xh")
    taps = taps.transpose(1, 0, 2).reshape(per_group, seq_len)
    mixed_term = long_mixing(here.transpose(1, 0, 2), taps, bias_part)
    mixed_term, own_far = lax.optimization_barrier((mixed_term, own_far))
    returned = lax.all_to_all(
        mixed_term.transpose(1, 0, 2), SEQ, split_axis=0, concat_axis=0, tiled=True
    )
    gain = lax.dynamic_slice_in_dim(
        norm_gain, lax.axis_index(TP) * local_width, local_width, 0
    )
    hyena, payload = make_payload(query, returned.reshape(local_width, block_len), gain, members)
    payload, near = lax.optimization_barrier((payload, near))
    pieces = (own_near, own_far, near, swap(near, "core"))
    sent = lax.all_to_all(payload, TP, split_axis=0, concat_axis=0, tiled=True)
    partial_sum = feed_forward(sent, gate_up, pieces, core.reshape(1), gate_weight.shape[0])
    shares = lax.all_to_all(partial_sum, TP, split_axis=0, concat_axis=0, tiled=True)
    feed_out = jnp.sum(shares.astype(jnp.float32), axis=0).T
    return (hyena.astype(jnp.float32) + feed_out).astype(jnp.bfloat16)


def solution(mesh):
    fine = Mesh(mesh.devices.reshape(2, 8, 2, 4, 2), SEQ + TP)
    placed = (
        P(None, TP, SEQ),
        P(TP, SEQ),
        P(None, TP, None),
        P(TP),
        P(),
        P(SEQ + TP, None),
        P(SEQ + TP, None),
        P(SEQ + TP, None),
    )
    return jax.shard_map(
        per_device, mesh=fine, in_specs=placed, out_specs=P(TP, SEQ), check_vma=False
    )
```

```python
import functools

import jax
import jax.numpy as jnp
from jax import lax
from jax.experimental import pallas as pl
from jax.experimental.pallas import tpu as pltpu
from jax.sharding import Mesh
from jax.sharding import PartitionSpec as P

EPSILON = 1e-06
LANES = 128
SEQ = ("xh", "z", "core")
TP = ("y", "xl")
SMALL = pltpu.CompilerParams(vmem_limit_bytes=12 * 1024 * 1024)


def gate_kernel(projected_ref, weight_ref, edge_ref, gated_ref, query_ref):
    rows, width = query_ref.shape
    weights = weight_ref[...].T
    edges = edge_ref[...].astype(jnp.float32).T
    lane = lax.broadcasted_iota(jnp.int32, (rows, width), 1)
    shorts = []
    for index in range(3):
        value = projected_ref[index].astype(jnp.float32)
        far, near = edges[:, 2 * index : 2 * index + 1], edges[:, 2 * index + 1 : 2 * index + 2]
        once = jnp.where(lane == 0, near, pltpu.roll(value, 1, 1))
        twice = jnp.where(lane == 0, far, jnp.where(lane == 1, near, pltpu.roll(value, 2, 1)))
        taps = [weights[:, 3 * index + tap : 3 * index + tap + 1] for tap in range(3)]
        shorts.append(taps[0] * value + taps[1] * once + taps[2] * twice)
    query_ref[...] = shorts[0]
    gated_ref[...] = (shorts[1] * shorts[2]).astype(jnp.bfloat16)


def make_gated(projected, short_weight, edge):
    count, rows, width = projected.shape
    weights = short_weight.transpose(0, 2, 1).reshape(9, rows)
    return pl.pallas_call(
        gate_kernel,
        out_shape=(
            jax.ShapeDtypeStruct((rows, width), jnp.bfloat16),
            jax.ShapeDtypeStruct((rows, width), jnp.float32),
        ),
        compiler_params=SMALL,
        name="make_gated",
    )(projected, jnp.pad(weights, ((0, 7), (0, 0))), edge)


def pack_first_kernel(gate_ref, up_ref, down_ref, first_ref, pair_ref):
    gate, up = gate_ref[...].astype(jnp.float32), up_ref[...].astype(jnp.float32)
    down = down_ref[...].astype(jnp.float32)
    blank = jnp.zeros((first_ref.shape[0] - down.shape[0], down.shape[1]), jnp.float32)
    first_ref[...] = jnp.concatenate([down, blank], axis=0).astype(jnp.bfloat16)
    pair_ref[...] = jnp.concatenate([gate, up], axis=0).astype(jnp.bfloat16)


def pack_first(gate, up, down):
    rows, width = gate.shape
    return pl.pallas_call(
        pack_first_kernel,
        out_shape=(
            jax.ShapeDtypeStruct((rows + -rows % 8, width), gate.dtype),
            jax.ShapeDtypeStruct((2 * rows, width), gate.dtype),
        ),
        name="pack_first",
    )(gate, up, down)


def pack_second_kernel(pair_ref, other_ref, out_ref):
    pair, other = pair_ref[...].astype(jnp.float32), other_ref[...].astype(jnp.float32)
    out_ref[...] = jnp.concatenate([pair, other], axis=0).astype(jnp.bfloat16)


def pack_second(pair, other):
    return pl.pallas_call(
        pack_second_kernel,
        out_shape=jax.ShapeDtypeStruct((2 * pair.shape[0], pair.shape[1]), pair.dtype),
        compiler_params=SMALL,
        name="pack_second",
    )(pair, other)


def build_table(taps_ref, channel, table_ref):
    seq_len = taps_ref.shape[2]
    taps = jnp.broadcast_to(taps_ref[channel].astype(jnp.float32), (8, seq_len))
    base = jnp.concatenate([taps, jnp.zeros((8, LANES), jnp.float32)], axis=1)
    base = pltpu.roll(base, 0, 1, stride=1, stride_axis=0)
    base = jnp.concatenate([base, pltpu.roll(base, 8, 1)], axis=0).astype(jnp.bfloat16)
    for shift in range(0, LANES, 16):
        moved = pltpu.roll(base, shift, 1) if shift else base
        table_ref[shift : shift + 16, :] = moved[:, :seq_len]


def apply_table(gated_ref, bias_ref, channel, table_ref, out_ref):
    rows = gated_ref.shape[1]
    gated = gated_ref[channel].astype(jnp.float32)
    tiles = rows // 8
    left = []
    for skip in range(tiles):
        keep = rows - 8 * skip
        left.append(jnp.concatenate([gated[:keep, :LANES], gated[:keep, LANES:]], axis=0).astype(jnp.bfloat16))
    zero = jnp.zeros((8, LANES), jnp.float32)
    total = [[zero] * tiles, [zero] * tiles]
    row = lax.broadcasted_iota(jnp.int32, (rows, LANES), 0)
    carried = [zero] * tiles
    for rho in range(8):
        sums = [carried, [zero] * tiles]
        carried = [zero] * tiles
        for skip in range(tiles):
            step = 8 * skip + rho
            keep = rows - 8 * skip
            part = jnp.dot(left[skip], table_ref[:, 2 * LANES * step : 2 * LANES * (step + 1)], preferred_element_type=jnp.float32)
            for lane_half in range(2):
                for row_half in range(2):
                    move = (2 * step + lane_half + row_half) // 2
                    if move >= rows: continue
                    side = (lane_half + row_half) % 2
                    target = sums[side] if move == step else carried
                    first = move // 8
                    for tile in range(tiles - first):
                        start = row_half * keep + 8 * tile
                        target[tile + first] = target[tile + first] + part[start:start + 8, lane_half * LANES:(lane_half + 1) * LANES]
        for side in range(2):
            if rho == 0:
                moved = sums[side]
            else:
                moved = jnp.concatenate(sums[side], axis=0)
                moved = jnp.where(row >= rho, pltpu.roll(moved, rho, 0), 0.0)
                moved = [moved[8*t:8*t+8] for t in range(tiles)]
            total[side] = [a + b for a, b in zip(total[side], moved)]
    total[0] = [a + b for a, b in zip(total[0], carried)]
    whole = jnp.concatenate([jnp.concatenate(total[0], axis=0), jnp.concatenate(total[1], axis=0)], axis=1)
    out_ref[channel] = (whole + bias_ref[channel] * gated).astype(jnp.bfloat16)

def conv_kernel(bias_ref, gated_ref, taps_ref, out_ref, even_ref, odd_ref):
    channels = gated_ref.shape[0]
    build_table(taps_ref, 0, even_ref)
    def body(step, carry):
        channel = 2 * step
        build_table(taps_ref, channel + 1, odd_ref)
        apply_table(gated_ref, bias_ref, channel, even_ref, out_ref)
        build_table(taps_ref, lax.rem(channel + 2, channels), even_ref)
        apply_table(gated_ref, bias_ref, channel + 1, odd_ref, out_ref)
        return carry
    lax.fori_loop(0, channels // 2, body, 0)

def long_mixing(gated, taps, bias):
    channels, rows, width = gated.shape
    seq_len = rows * width
    return pl.pallas_call(conv_kernel,
        out_shape=jax.ShapeDtypeStruct(gated.shape, jnp.bfloat16),
        in_specs=[pl.BlockSpec(memory_space=pltpu.SMEM), pl.BlockSpec(memory_space=pltpu.VMEM), pl.BlockSpec(memory_space=pltpu.VMEM)],
        out_specs=pl.BlockSpec(memory_space=pltpu.VMEM),
        scratch_shapes=[pltpu.VMEM((LANES, seq_len), jnp.bfloat16)]*2,
        compiler_params=pltpu.CompilerParams(vmem_limit_bytes=24*1024*1024),
        cost_estimate=pl.CostEstimate(flops=8 * channels * seq_len * seq_len, bytes_accessed=6*channels*seq_len, transcendentals=0),
        name="long_mixing")(bias, gated, taps.reshape(channels, 1, seq_len))


def payload_kernel(query_ref, mixed_ref, gain_ref, hyena_ref, out_ref):
    rows = query_ref.shape[0]
    hyena = (query_ref[...] * mixed_ref[...].astype(jnp.float32)).astype(jnp.bfloat16)
    hyena_ref[...] = hyena
    wide = hyena.astype(jnp.float32)
    scaled = (wide * gain_ref[...]).astype(jnp.bfloat16)
    rest = jnp.sum(wide * wide, axis=0, keepdims=True)
    place = lax.broadcasted_iota(jnp.int32, (out_ref.shape[1] - rows, wide.shape[1]), 0)
    extra = jnp.zeros(place.shape, jnp.float32)
    for index in range(3):
        part = rest.astype(jnp.bfloat16).astype(jnp.float32)
        extra = jnp.where(place == index, part, extra)
        rest = rest - part
    for member in range(out_ref.shape[0]):
        out_ref[member, :rows, :] = scaled
        out_ref[member, rows:, :] = extra.astype(jnp.bfloat16)


def make_payload(query, mixed, gain, members):
    rows, width = query.shape
    return pl.pallas_call(
        payload_kernel,
        out_shape=(
            jax.ShapeDtypeStruct((rows, width), jnp.bfloat16),
            jax.ShapeDtypeStruct((members, rows + 16, width), jnp.bfloat16),
        ),
        compiler_params=SMALL,
        name="make_payload",
    )(query, mixed, gain.reshape(rows, 1))


def feed_kernel(
    sizes, core_ref, sent_ref, weight_ref, p0_ref, p1_ref, p2_ref, p3_ref, out_ref,
    x_ref, scale_ref, hidden_ref, flat_ref, piece_ref, piece_sem,
):
    units, block, per_step, first_steps = sizes
    step = pl.program_id(0)
    members, rows = sent_ref.shape[0], out_ref.shape[2]
    core = core_ref[0]
    length = p0_ref.shape[0]
    copies = []
    for index, ref in enumerate((p0_ref, p1_ref, p2_ref, p3_ref)):
        slot = 2 * (index // 2) + (core if index % 2 == 0 else 1 - core)
        target = piece_ref.at[pl.ds(pl.multiple_of(slot * length, 16), length), :]
        copies.append(pltpu.make_async_copy(ref, target, piece_sem.at[index]))

    @pl.when(step == 0)
    def _():
        for copy in copies:
            copy.start()
        squares = jnp.zeros((1, x_ref.shape[1]), jnp.float32)
        for member in range(members):
            x_ref[member * rows : (member + 1) * rows, :] = sent_ref[member, :rows, :]
            extra = sent_ref[member, rows:, :].astype(jnp.float32)
            squares = squares + (extra[0:1] + extra[1:2] + extra[2:3])
        scale = lax.rsqrt(squares / (members * rows) + EPSILON)
        scale_ref[...] = jnp.broadcast_to(scale, scale_ref.shape)

    @pl.when(step < first_steps)
    def _():
        scale = scale_ref[0:1, :]
        sums = jnp.dot(weight_ref[...], x_ref[...], preferred_element_type=jnp.float32) * scale
        height = weight_ref.shape[0] // per_step
        for index in range(per_step):
            part = sums[index * height : (index + 1) * height]
            for side in range(2):
                base = 2 * side * units
                gate, up = part[base : base + units], part[base + units : base + 2 * units]
                value = gate / (1.0 + jnp.exp(-gate)) * up
                blank = jnp.zeros((block - units, value.shape[1]), jnp.float32)
                start = (2 * side + index % 2) * length
                start += (step * (per_step // 2) + index // 2) * block
                hidden_ref[pl.ds(pl.multiple_of(start, 8), block), :] = jnp.concatenate(
                    [value, blank], axis=0
                )

    @pl.when(step == first_steps)
    def _():
        for copy in copies:
            copy.wait()
        flat_ref[...] = hidden_ref[...].T.astype(jnp.bfloat16)

    @pl.when(step >= first_steps)
    def _():
        wide = out_ref.shape[0] * rows
        start = pl.multiple_of((step - first_steps) * wide, LANES)
        total = jnp.dot(
            flat_ref[...], piece_ref[:, pl.ds(start, wide)], preferred_element_type=jnp.float32
        )
        for member in range(out_ref.shape[0]):
            out_ref[member] = total[:, member * rows : (member + 1) * rows].astype(jnp.bfloat16)


def feed_forward(sent, weights, pieces, core, units):
    members, padded, width = sent.shape
    channels = weights.shape[1]
    rows = channels // members
    length = pieces[0].shape[0]
    block = units + -units % 8
    blocks = 2 * length // block
    per_step, out_step = 8, 4
    first_steps = blocks // per_step
    anywhere = pl.BlockSpec(memory_space=pl.ANY)
    return pl.pallas_call(
        functools.partial(feed_kernel, (units, block, per_step, first_steps)),
        grid=(first_steps + members // out_step,),
        out_shape=jax.ShapeDtypeStruct((members, width, rows), jnp.bfloat16),
        in_specs=[
            pl.BlockSpec(memory_space=pltpu.SMEM),
            pl.BlockSpec(memory_space=pltpu.VMEM),
            pl.BlockSpec(
                (weights.shape[0] // first_steps, channels),
                lambda i: (jnp.minimum(i, first_steps - 1), 0),
            ),
            anywhere,
            anywhere,
            anywhere,
            anywhere,
        ],
        out_specs=pl.BlockSpec(
            (out_step, width, rows), lambda i: (jnp.maximum(i - first_steps, 0), 0, 0)
        ),
        scratch_shapes=[
            pltpu.VMEM((channels, width), jnp.bfloat16),
            pltpu.VMEM((8, width), jnp.float32),
            pltpu.VMEM((4 * length, width), jnp.float32),
            pltpu.VMEM((width, 4 * length), jnp.bfloat16),
            pltpu.VMEM((4 * length, channels), jnp.bfloat16),
            pltpu.SemaphoreType.DMA((4,)),
        ],
        compiler_params=pltpu.CompilerParams(vmem_limit_bytes=52 * 1024 * 1024),
        cost_estimate=pl.CostEstimate(flops=10**10, bytes_accessed=3 * 10**7, transcendentals=0),
        name="feed_forward",
    )(core, sent, weights, *pieces)


def finish_kernel(shares_ref, hyena_ref, out_ref):
    total = shares_ref[0].astype(jnp.float32)
    for member in range(1, shares_ref.shape[0]):
        total = total + shares_ref[member].astype(jnp.float32)
    out_ref[...] = (hyena_ref[...].astype(jnp.float32) + total.T).astype(jnp.bfloat16)


def finish(shares, hyena):
    return pl.pallas_call(
        finish_kernel,
        out_shape=jax.ShapeDtypeStruct(hyena.shape, jnp.bfloat16),
        compiler_params=SMALL,
        name="finish",
    )(shares, hyena)


def swap(values, axis):
    return lax.ppermute(values, axis, [(0, 1), (1, 0)])


def per_device(
    projected, filter_taps, short_weight, skip_bias, norm_gain, gate_weight, up_weight, down_weight
):
    groups = lax.axis_size(SEQ)
    members = lax.axis_size(TP)
    local_width, block_len = filter_taps.shape
    per_group = local_width // groups
    seq_len = groups * block_len
    offset = lax.axis_index(SEQ) * per_group
    bias_part = lax.dynamic_slice_in_dim(skip_bias, offset, per_group, 0)

    first, pair = pack_first(gate_weight, up_weight, down_weight)
    own_near = lax.all_gather(first, "z", axis=0, tiled=True)
    edge = projected[:, :, block_len - 2 :].transpose(0, 2, 1).reshape(6, local_width)
    edge = lax.ppermute(
        jnp.pad(edge, ((0, 2), (0, 0))), SEQ, [(i, i + 1) for i in range(groups - 1)]
    )
    taps = lax.all_to_all(
        filter_taps.reshape(groups, per_group, block_len),
        SEQ,
        split_axis=0,
        concat_axis=0,
        tiled=True,
    )
    gated, query = make_gated(projected, short_weight, edge)
    other_pair = swap(pair, "xh")
    second = pack_second(pair, other_pair)
    gated, taps, second, bias_part = lax.optimization_barrier((gated, taps, second, bias_part))
    here = lax.all_to_all(
        gated.reshape(groups, per_group, block_len), SEQ, split_axis=0, concat_axis=0, tiled=True
    )

    core = lax.axis_index("core")
    gate_up = lax.all_gather(second, ("z", "core"), axis=0, tiled=True)

    here, own_near = lax.optimization_barrier((here, own_near))
    own_far = swap(own_near, "core")
    near = swap(own_near, "xh")
    taps = taps.transpose(1, 0, 2).reshape(per_group, seq_len)
    mixed_term = long_mixing(here.transpose(1, 0, 2), taps, bias_part)
    mixed_term, own_far = lax.optimization_barrier((mixed_term, own_far))
    returned = lax.all_to_all(
        mixed_term.transpose(1, 0, 2), SEQ, split_axis=0, concat_axis=0, tiled=True
    )
    gain = lax.dynamic_slice_in_dim(
        norm_gain, lax.axis_index(TP) * local_width, local_width, 0
    )
    hyena, payload = make_payload(query, returned.reshape(local_width, block_len), gain, members)
    payload, near = lax.optimization_barrier((payload, near))
    pieces = (own_near, own_far, near, swap(near, "core"))
    sent = lax.all_to_all(payload, TP, split_axis=0, concat_axis=0, tiled=True)
    partial_sum = feed_forward(sent, gate_up, pieces, core.reshape(1), gate_weight.shape[0])
    shares = lax.all_to_all(partial_sum, TP, split_axis=0, concat_axis=0, tiled=True)
    return finish(shares, hyena)


def solution(mesh):
    fine = Mesh(mesh.devices.reshape(2, 8, 2, 4, 2), SEQ + TP)
    placed = (
        P(None, TP, SEQ),
        P(TP, SEQ),
        P(None, TP, None),
        P(TP),
        P(),
        P(SEQ + TP, None),
        P(SEQ + TP, None),
        P(SEQ + TP, None),
    )
    return jax.shard_map(
        per_device, mesh=fine, in_specs=placed, out_specs=P(TP, SEQ), check_vma=False
    )
```

```python
import functools

import jax
import jax.numpy as jnp
from jax import lax
from jax.experimental import pallas as pl
from jax.experimental.pallas import tpu as pltpu
from jax.sharding import Mesh
from jax.sharding import PartitionSpec as P

EPSILON = 1e-06
LANES = 128
SEQ = ("xh", "z", "core")
TP = ("y", "xl")
SMALL = pltpu.CompilerParams(vmem_limit_bytes=12 * 1024 * 1024)


def gate_kernel(projected_ref, taps_ref, weight_ref, edge_ref, sent_ref, query_ref):
    rows, width = taps_ref.shape
    groups = sent_ref.shape[0]
    weights = weight_ref[...].T
    edges = edge_ref[...].astype(jnp.float32).T
    lane = lax.broadcasted_iota(jnp.int32, (rows, width), 1)
    shorts = []
    for index in range(3):
        value = projected_ref[index].astype(jnp.float32)
        far, near = edges[:, 2 * index : 2 * index + 1], edges[:, 2 * index + 1 : 2 * index + 2]
        once = jnp.where(lane == 0, near, pltpu.roll(value, 1, 1))
        twice = jnp.where(lane == 0, far, jnp.where(lane == 1, near, pltpu.roll(value, 2, 1)))
        taps = [weights[:, 3 * index + tap : 3 * index + tap + 1] for tap in range(3)]
        shorts.append(taps[0] * value + taps[1] * once + taps[2] * twice)
    query_ref[...] = shorts[0]
    gated = (shorts[1] * shorts[2]).astype(jnp.bfloat16)
    sent_ref[:, 0] = gated.reshape(groups, rows // groups, width)
    sent_ref[:, 1] = taps_ref[...].reshape(groups, rows // groups, width)


def make_gated(projected, taps, short_weight, edge, groups):
    count, rows, width = projected.shape
    weights = short_weight.transpose(0, 2, 1).reshape(9, rows)
    return pl.pallas_call(
        gate_kernel,
        out_shape=(
            jax.ShapeDtypeStruct((groups, 2, rows // groups, width), jnp.bfloat16),
            jax.ShapeDtypeStruct((rows, width), jnp.float32),
        ),
        compiler_params=SMALL,
        name="make_gated",
    )(projected, taps, jnp.pad(weights, ((0, 7), (0, 0))), edge)


def pack_first_kernel(gate_ref, up_ref, down_ref, first_ref, pair_ref):
    gate, up = gate_ref[...].astype(jnp.float32), up_ref[...].astype(jnp.float32)
    down = down_ref[...].astype(jnp.float32)
    blank = jnp.zeros((first_ref.shape[0] - down.shape[0], down.shape[1]), jnp.float32)
    first_ref[...] = jnp.concatenate([down, blank], axis=0).astype(jnp.bfloat16)
    pair_ref[...] = jnp.concatenate([gate, up], axis=0).astype(jnp.bfloat16)


def pack_first(gate, up, down):
    rows, width = gate.shape
    return pl.pallas_call(
        pack_first_kernel,
        out_shape=(
            jax.ShapeDtypeStruct((rows + -rows % 8, width), gate.dtype),
            jax.ShapeDtypeStruct((2 * rows, width), gate.dtype),
        ),
        name="pack_first",
    )(gate, up, down)


def pack_second_kernel(pair_ref, other_ref, out_ref):
    pair, other = pair_ref[...].astype(jnp.float32), other_ref[...].astype(jnp.float32)
    out_ref[...] = jnp.concatenate([pair, other], axis=0).astype(jnp.bfloat16)


def pack_second(pair, other):
    return pl.pallas_call(
        pack_second_kernel,
        out_shape=jax.ShapeDtypeStruct((2 * pair.shape[0], pair.shape[1]), pair.dtype),
        compiler_params=SMALL,
        name="pack_second",
    )(pair, other)


def build_table(taps_ref, channel, table_ref):
    seq_len = taps_ref.shape[2]
    taps = jnp.broadcast_to(taps_ref[channel].astype(jnp.float32), (8, seq_len))
    base = jnp.concatenate([taps, jnp.zeros((8, LANES), jnp.float32)], axis=1)
    base = pltpu.roll(base, 0, 1, stride=1, stride_axis=0)
    for pair in range(LANES // 16):
        parts = []
        for shift in (16 * pair, 16 * pair + 8):
            moved = pltpu.roll(base, shift, 1) if shift else base
            parts.append(moved[:, :seq_len])
        table_ref[16 * pair : 16 * pair + 16, :] = jnp.concatenate(parts, axis=0).astype(
            jnp.bfloat16
        )


def apply_table(gated_ref, bias_ref, channel, table_ref, out_ref):
    rows = gated_ref.shape[1]
    gated = gated_ref[channel].astype(jnp.float32)
    tiles = rows // 8
    left = []
    for skip in range(tiles):
        keep = rows - 8 * skip
        left.append(jnp.concatenate([gated[:keep, :LANES], gated[:keep, LANES:]], axis=0).astype(jnp.bfloat16))
    zero = jnp.zeros((8, LANES), jnp.float32)
    total = [[zero] * tiles, [zero] * tiles]
    row = lax.broadcasted_iota(jnp.int32, (rows, LANES), 0)
    carried = [zero] * tiles
    for rho in range(8):
        sums = [carried, [zero] * tiles]
        carried = [zero] * tiles
        for skip in range(tiles):
            step = 8 * skip + rho
            keep = rows - 8 * skip
            part = jnp.dot(left[skip], table_ref[:, 2 * LANES * step : 2 * LANES * (step + 1)], preferred_element_type=jnp.float32)
            for lane_half in range(2):
                for row_half in range(2):
                    move = (2 * step + lane_half + row_half) // 2
                    if move >= rows: continue
                    side = (lane_half + row_half) % 2
                    target = sums[side] if move == step else carried
                    first = move // 8
                    for tile in range(tiles - first):
                        start = row_half * keep + 8 * tile
                        target[tile + first] = target[tile + first] + part[start:start + 8, lane_half * LANES:(lane_half + 1) * LANES]
        for side in range(2):
            if rho == 0:
                moved = sums[side]
            else:
                moved = jnp.concatenate(sums[side], axis=0)
                moved = jnp.where(row >= rho, pltpu.roll(moved, rho, 0), 0.0)
                moved = [moved[8*t:8*t+8] for t in range(tiles)]
            total[side] = [a + b for a, b in zip(total[side], moved)]
    total[0] = [a + b for a, b in zip(total[0], carried)]
    whole = jnp.concatenate([jnp.concatenate(total[0], axis=0), jnp.concatenate(total[1], axis=0)], axis=1)
    out_ref[channel] = (whole + bias_ref[channel] * gated).astype(jnp.bfloat16)

def conv_kernel(bias_ref, gated_ref, taps_ref, out_ref, even_ref, odd_ref):
    channels = gated_ref.shape[0]
    build_table(taps_ref, 0, even_ref)
    def body(step, carry):
        channel = 2 * step
        build_table(taps_ref, channel + 1, odd_ref)
        apply_table(gated_ref, bias_ref, channel, even_ref, out_ref)
        build_table(taps_ref, lax.rem(channel + 2, channels), even_ref)
        apply_table(gated_ref, bias_ref, channel + 1, odd_ref, out_ref)
        return carry
    lax.fori_loop(0, channels // 2, body, 0)

def long_mixing(gated, taps, bias):
    channels, rows, width = gated.shape
    seq_len = rows * width
    return pl.pallas_call(conv_kernel,
        out_shape=jax.ShapeDtypeStruct(gated.shape, jnp.bfloat16),
        in_specs=[pl.BlockSpec(memory_space=pltpu.SMEM), pl.BlockSpec(memory_space=pltpu.VMEM), pl.BlockSpec(memory_space=pltpu.VMEM)],
        out_specs=pl.BlockSpec(memory_space=pltpu.VMEM),
        scratch_shapes=[pltpu.VMEM((LANES, seq_len), jnp.bfloat16)]*2,
        compiler_params=pltpu.CompilerParams(vmem_limit_bytes=24*1024*1024),
        cost_estimate=pl.CostEstimate(flops=8 * channels * seq_len * seq_len, bytes_accessed=6*channels*seq_len, transcendentals=0),
        name="long_mixing")(bias, gated, taps.reshape(channels, 1, seq_len))


def payload_kernel(query_ref, mixed_ref, gain_ref, hyena_ref, out_ref):
    rows = query_ref.shape[0]
    hyena = (query_ref[...] * mixed_ref[...].astype(jnp.float32)).astype(jnp.bfloat16)
    hyena_ref[...] = hyena
    wide = hyena.astype(jnp.float32)
    scaled = (wide * gain_ref[...]).astype(jnp.bfloat16)
    rest = jnp.sum(wide * wide, axis=0, keepdims=True)
    place = lax.broadcasted_iota(jnp.int32, (out_ref.shape[1] - rows, wide.shape[1]), 0)
    extra = jnp.zeros(place.shape, jnp.float32)
    for index in range(3):
        part = rest.astype(jnp.bfloat16).astype(jnp.float32)
        extra = jnp.where(place == index, part, extra)
        rest = rest - part
    for member in range(out_ref.shape[0]):
        out_ref[member, :rows, :] = scaled
        out_ref[member, rows:, :] = extra.astype(jnp.bfloat16)


def make_payload(query, mixed, gain, members):
    rows, width = query.shape
    return pl.pallas_call(
        payload_kernel,
        out_shape=(
            jax.ShapeDtypeStruct((rows, width), jnp.bfloat16),
            jax.ShapeDtypeStruct((members, rows + 16, width), jnp.bfloat16),
        ),
        compiler_params=SMALL,
        name="make_payload",
    )(query, mixed, gain.reshape(rows, 1))


def feed_kernel(
    sizes, core_ref, sent_ref, weight_ref, p0_ref, p1_ref, p2_ref, p3_ref, out_ref,
    x_ref, scale_ref, hidden_ref, flat_ref, piece_ref, piece_sem,
):
    units, block, per_step, first_steps = sizes
    step = pl.program_id(0)
    members, rows = sent_ref.shape[0], out_ref.shape[2]
    core = core_ref[0]
    length = p0_ref.shape[0]
    copies = []
    for index, ref in enumerate((p0_ref, p1_ref, p2_ref, p3_ref)):
        slot = 2 * (index // 2) + (core if index % 2 == 0 else 1 - core)
        target = piece_ref.at[pl.ds(pl.multiple_of(slot * length, 16), length), :]
        copies.append(pltpu.make_async_copy(ref, target, piece_sem.at[index]))

    @pl.when(step == 0)
    def _():
        for copy in copies:
            copy.start()
        squares = jnp.zeros((1, x_ref.shape[1]), jnp.float32)
        for member in range(members):
            x_ref[member * rows : (member + 1) * rows, :] = sent_ref[member, :rows, :]
            extra = sent_ref[member, rows:, :].astype(jnp.float32)
            squares = squares + (extra[0:1] + extra[1:2] + extra[2:3])
        scale = lax.rsqrt(squares / (members * rows) + EPSILON)
        scale_ref[...] = jnp.broadcast_to(scale, scale_ref.shape)

    @pl.when(step < first_steps)
    def _():
        scale = scale_ref[0:1, :]
        sums = jnp.dot(weight_ref[...], x_ref[...], preferred_element_type=jnp.float32) * scale
        height = weight_ref.shape[0] // per_step
        for index in range(per_step):
            part = sums[index * height : (index + 1) * height]
            for side in range(2):
                base = 2 * side * units
                gate, up = part[base : base + units], part[base + units : base + 2 * units]
                value = gate / (1.0 + jnp.exp(-gate)) * up
                blank = jnp.zeros((block - units, value.shape[1]), jnp.float32)
                start = (2 * side + index % 2) * length
                start += (step * (per_step // 2) + index // 2) * block
                hidden_ref[pl.ds(pl.multiple_of(start, 8), block), :] = jnp.concatenate(
                    [value, blank], axis=0
                )

    @pl.when(step == first_steps)
    def _():
        for copy in copies:
            copy.wait()
        flat_ref[...] = hidden_ref[...].T.astype(jnp.bfloat16)

    @pl.when(step >= first_steps)
    def _():
        wide = out_ref.shape[0] * rows
        start = pl.multiple_of((step - first_steps) * wide, LANES)
        total = jnp.dot(
            flat_ref[...], piece_ref[:, pl.ds(start, wide)], preferred_element_type=jnp.float32
        )
        for member in range(out_ref.shape[0]):
            out_ref[member] = total[:, member * rows : (member + 1) * rows].astype(jnp.bfloat16)


def feed_forward(sent, weights, pieces, core, units):
    members, padded, width = sent.shape
    channels = weights.shape[1]
    rows = channels // members
    length = pieces[0].shape[0]
    block = units + -units % 8
    blocks = 2 * length // block
    per_step, out_step = 8, 4
    first_steps = blocks // per_step
    anywhere = pl.BlockSpec(memory_space=pl.ANY)
    return pl.pallas_call(
        functools.partial(feed_kernel, (units, block, per_step, first_steps)),
        grid=(first_steps + members // out_step,),
        out_shape=jax.ShapeDtypeStruct((members, width, rows), jnp.bfloat16),
        in_specs=[
            pl.BlockSpec(memory_space=pltpu.SMEM),
            pl.BlockSpec(memory_space=pltpu.VMEM),
            pl.BlockSpec(
                (weights.shape[0] // first_steps, channels),
                lambda i: (jnp.minimum(i, first_steps - 1), 0),
            ),
            anywhere,
            anywhere,
            anywhere,
            anywhere,
        ],
        out_specs=pl.BlockSpec(
            (out_step, width, rows), lambda i: (jnp.maximum(i - first_steps, 0), 0, 0)
        ),
        scratch_shapes=[
            pltpu.VMEM((channels, width), jnp.bfloat16),
            pltpu.VMEM((8, width), jnp.float32),
            pltpu.VMEM((4 * length, width), jnp.float32),
            pltpu.VMEM((width, 4 * length), jnp.bfloat16),
            pltpu.VMEM((4 * length, channels), jnp.bfloat16),
            pltpu.SemaphoreType.DMA((4,)),
        ],
        compiler_params=pltpu.CompilerParams(vmem_limit_bytes=52 * 1024 * 1024),
        cost_estimate=pl.CostEstimate(flops=10**10, bytes_accessed=3 * 10**7, transcendentals=0),
        name="feed_forward",
    )(core, sent, weights, *pieces)


def finish_kernel(shares_ref, hyena_ref, out_ref):
    total = shares_ref[0].astype(jnp.float32)
    for member in range(1, shares_ref.shape[0]):
        total = total + shares_ref[member].astype(jnp.float32)
    out_ref[...] = (hyena_ref[...].astype(jnp.float32) + total.T).astype(jnp.bfloat16)


def finish(shares, hyena):
    return pl.pallas_call(
        finish_kernel,
        out_shape=jax.ShapeDtypeStruct(hyena.shape, jnp.bfloat16),
        compiler_params=SMALL,
        name="finish",
    )(shares, hyena)


def swap(values, axis):
    return lax.ppermute(values, axis, [(0, 1), (1, 0)])


def per_device(
    projected, filter_taps, short_weight, skip_bias, norm_gain, gate_weight, up_weight, down_weight
):
    groups = lax.axis_size(SEQ)
    members = lax.axis_size(TP)
    local_width, block_len = filter_taps.shape
    per_group = local_width // groups
    seq_len = groups * block_len
    offset = lax.axis_index(SEQ) * per_group
    bias_part = lax.dynamic_slice_in_dim(skip_bias, offset, per_group, 0)

    first, pair = pack_first(gate_weight, up_weight, down_weight)
    own_near = lax.all_gather(first, "z", axis=0, tiled=True)
    edge = projected[:, :, block_len - 2 :].transpose(0, 2, 1).reshape(6, local_width)
    edge = lax.ppermute(
        jnp.pad(edge, ((0, 2), (0, 0))), SEQ, [(i, i + 1) for i in range(groups - 1)]
    )
    sent, query = make_gated(projected, filter_taps, short_weight, edge, groups)
    sent, bias_part = lax.optimization_barrier((sent, bias_part))
    here = lax.all_to_all(sent, SEQ, split_axis=0, concat_axis=0, tiled=True)

    core = lax.axis_index("core")
    other_pair = swap(pair, "xh")
    here, other_pair = lax.optimization_barrier((here, other_pair))
    gate_up = lax.all_gather(pack_second(pair, other_pair), ("z", "core"), axis=0, tiled=True)

    here, own_near = lax.optimization_barrier((here, own_near))
    own_far = swap(own_near, "core")
    near = swap(own_near, "xh")
    here = here.transpose(1, 2, 0, 3)
    mixed_term = long_mixing(here[0], here[1].reshape(per_group, seq_len), bias_part)
    mixed_term, own_far = lax.optimization_barrier((mixed_term, own_far))
    returned = lax.all_to_all(
        mixed_term.transpose(1, 0, 2), SEQ, split_axis=0, concat_axis=0, tiled=True
    )
    gain = lax.dynamic_slice_in_dim(
        norm_gain, lax.axis_index(TP) * local_width, local_width, 0
    )
    hyena, payload = make_payload(query, returned.reshape(local_width, block_len), gain, members)
    payload, near = lax.optimization_barrier((payload, near))
    pieces = (own_near, own_far, near, swap(near, "core"))
    sent = lax.all_to_all(payload, TP, split_axis=0, concat_axis=0, tiled=True)
    partial_sum = feed_forward(sent, gate_up, pieces, core.reshape(1), gate_weight.shape[0])
    shares = lax.all_to_all(partial_sum, TP, split_axis=0, concat_axis=0, tiled=True)
    return finish(shares, hyena)


def solution(mesh):
    fine = Mesh(mesh.devices.reshape(2, 8, 2, 4, 2), SEQ + TP)
    placed = (
        P(None, TP, SEQ),
        P(TP, SEQ),
        P(None, TP, None),
        P(TP),
        P(),
        P(SEQ + TP, None),
        P(SEQ + TP, None),
        P(SEQ + TP, None),
    )
    return jax.shard_map(
        per_device, mesh=fine, in_specs=placed, out_specs=P(TP, SEQ), check_vma=False
    )
```

```python
import functools

import jax
import jax.numpy as jnp
from jax import lax
from jax.experimental import pallas as pl
from jax.experimental.pallas import tpu as pltpu
from jax.sharding import Mesh
from jax.sharding import PartitionSpec as P

EPSILON = 1e-06
LANES = 128
SEQ = ("xh", "z", "core")
TP = ("y", "xl")
SMALL = pltpu.CompilerParams(vmem_limit_bytes=12 * 1024 * 1024)


def gate_kernel(projected_ref, weight_ref, edge_ref, gated_ref, query_ref):
    rows, width = query_ref.shape
    weights = weight_ref[...].T
    edges = edge_ref[...].astype(jnp.float32).T
    lane = lax.broadcasted_iota(jnp.int32, (rows, width), 1)
    shorts = []
    for index in range(3):
        value = projected_ref[index].astype(jnp.float32)
        far, near = edges[:, 2 * index : 2 * index + 1], edges[:, 2 * index + 1 : 2 * index + 2]
        once = jnp.where(lane == 0, near, pltpu.roll(value, 1, 1))
        twice = jnp.where(lane == 0, far, jnp.where(lane == 1, near, pltpu.roll(value, 2, 1)))
        taps = [weights[:, 3 * index + tap : 3 * index + tap + 1] for tap in range(3)]
        shorts.append(taps[0] * value + taps[1] * once + taps[2] * twice)
    query_ref[...] = shorts[0]
    gated_ref[...] = (shorts[1] * shorts[2]).astype(jnp.bfloat16)


def make_gated(projected, short_weight, edge):
    count, rows, width = projected.shape
    weights = short_weight.transpose(0, 2, 1).reshape(9, rows)
    return pl.pallas_call(
        gate_kernel,
        out_shape=(
            jax.ShapeDtypeStruct((rows, width), jnp.bfloat16),
            jax.ShapeDtypeStruct((rows, width), jnp.float32),
        ),
        compiler_params=SMALL,
        name="make_gated",
    )(projected, jnp.pad(weights, ((0, 7), (0, 0))), edge)


def pad_kernel(rows_ref, out_ref):
    rows = rows_ref[...].astype(jnp.float32)
    blank = jnp.zeros((out_ref.shape[0] - rows.shape[0], rows.shape[1]), jnp.float32)
    out_ref[...] = jnp.concatenate([rows, blank], axis=0).astype(jnp.bfloat16)


def pad_rows(rows):
    count, width = rows.shape
    return pl.pallas_call(
        pad_kernel,
        out_shape=jax.ShapeDtypeStruct((count + -count % 8, width), rows.dtype),
        name="pad_rows",
    )(rows)


def pack_kernel(pair_ref, other_ref, out_ref):
    pair, other = pair_ref[...].astype(jnp.float32), other_ref[...].astype(jnp.float32)
    out_ref[...] = jnp.concatenate([pair, other], axis=0).astype(jnp.bfloat16)


def pack_rows(pair, other):
    return pl.pallas_call(
        pack_kernel,
        out_shape=jax.ShapeDtypeStruct((2 * pair.shape[0], pair.shape[1]), pair.dtype),
        compiler_params=SMALL,
        name="pack_rows",
    )(pair, other)


def build_table(taps_ref, channel, table_ref):
    seq_len = taps_ref.shape[2]
    taps = jnp.broadcast_to(taps_ref[channel].astype(jnp.float32), (8, seq_len))
    base = jnp.concatenate([taps, jnp.zeros((8, LANES), jnp.float32)], axis=1)
    base = pltpu.roll(base, 0, 1, stride=1, stride_axis=0)
    base = jnp.concatenate([base, pltpu.roll(base, 8, 1)], axis=0).astype(jnp.bfloat16)
    for shift in range(0, LANES, 16):
        moved = pltpu.roll(base, shift, 1) if shift else base
        table_ref[shift : shift + 16, :] = moved[:, :seq_len]


def apply_table(gated_ref, bias_ref, channel, table_ref, out_ref):
    rows = gated_ref.shape[1]
    gated = gated_ref[channel].astype(jnp.float32)
    tiles = rows // 8
    left = []
    for skip in range(tiles):
        keep = rows - 8 * skip
        left.append(jnp.concatenate([gated[:keep, :LANES], gated[:keep, LANES:]], axis=0).astype(jnp.bfloat16))
    zero = jnp.zeros((8, LANES), jnp.float32)
    total = [[zero] * tiles, [zero] * tiles]
    row = lax.broadcasted_iota(jnp.int32, (rows, LANES), 0)
    carried = [zero] * tiles
    for rho in range(8):
        sums = [carried, [zero] * tiles]
        carried = [zero] * tiles
        for skip in range(tiles):
            step = 8 * skip + rho
            keep = rows - 8 * skip
            part = jnp.dot(left[skip], table_ref[:, 2 * LANES * step : 2 * LANES * (step + 1)], preferred_element_type=jnp.float32)
            for lane_half in range(2):
                for row_half in range(2):
                    move = (2 * step + lane_half + row_half) // 2
                    if move >= rows: continue
                    side = (lane_half + row_half) % 2
                    target = sums[side] if move == step else carried
                    first = move // 8
                    for tile in range(tiles - first):
                        start = row_half * keep + 8 * tile
                        target[tile + first] = target[tile + first] + part[start:start + 8, lane_half * LANES:(lane_half + 1) * LANES]
        for side in range(2):
            if rho == 0:
                moved = sums[side]
            else:
                moved = jnp.concatenate(sums[side], axis=0)
                moved = jnp.where(row >= rho, pltpu.roll(moved, rho, 0), 0.0)
                moved = [moved[8*t:8*t+8] for t in range(tiles)]
            total[side] = [a + b for a, b in zip(total[side], moved)]
    total[0] = [a + b for a, b in zip(total[0], carried)]
    whole = jnp.concatenate([jnp.concatenate(total[0], axis=0), jnp.concatenate(total[1], axis=0)], axis=1)
    out_ref[channel] = (whole + bias_ref[channel] * gated).astype(jnp.bfloat16)

def conv_kernel(bias_ref, gated_ref, taps_ref, out_ref, even_ref, odd_ref):
    channels = gated_ref.shape[0]
    build_table(taps_ref, 0, even_ref)
    def body(step, carry):
        channel = 2 * step
        build_table(taps_ref, channel + 1, odd_ref)
        apply_table(gated_ref, bias_ref, channel, even_ref, out_ref)
        build_table(taps_ref, lax.rem(channel + 2, channels), even_ref)
        apply_table(gated_ref, bias_ref, channel + 1, odd_ref, out_ref)
        return carry
    lax.fori_loop(0, channels // 2, body, 0)

def long_mixing(gated, taps, bias):
    channels, rows, width = gated.shape
    seq_len = rows * width
    return pl.pallas_call(conv_kernel,
        out_shape=jax.ShapeDtypeStruct(gated.shape, jnp.bfloat16),
        in_specs=[pl.BlockSpec(memory_space=pltpu.SMEM), pl.BlockSpec(memory_space=pltpu.VMEM), pl.BlockSpec(memory_space=pltpu.VMEM)],
        out_specs=pl.BlockSpec(memory_space=pltpu.VMEM),
        scratch_shapes=[pltpu.VMEM((LANES, seq_len), jnp.bfloat16)]*2,
        compiler_params=pltpu.CompilerParams(vmem_limit_bytes=24*1024*1024),
        cost_estimate=pl.CostEstimate(flops=8 * channels * seq_len * seq_len, bytes_accessed=6*channels*seq_len, transcendentals=0),
        name="long_mixing")(bias, gated, taps.reshape(channels, 1, seq_len))


def payload_kernel(query_ref, mixed_ref, gain_ref, hyena_ref, out_ref):
    rows = query_ref.shape[0]
    hyena = (query_ref[...] * mixed_ref[...].astype(jnp.float32)).astype(jnp.bfloat16)
    hyena_ref[...] = hyena
    wide = hyena.astype(jnp.float32)
    scaled = (wide * gain_ref[...]).astype(jnp.bfloat16)
    rest = jnp.sum(wide * wide, axis=0, keepdims=True)
    place = lax.broadcasted_iota(jnp.int32, (out_ref.shape[1] - rows, wide.shape[1]), 0)
    extra = jnp.zeros(place.shape, jnp.float32)
    for index in range(3):
        part = rest.astype(jnp.bfloat16).astype(jnp.float32)
        extra = jnp.where(place == index, part, extra)
        rest = rest - part
    for member in range(out_ref.shape[0]):
        out_ref[member, :rows, :] = scaled
        out_ref[member, rows:, :] = extra.astype(jnp.bfloat16)


def make_payload(query, mixed, gain, members):
    rows, width = query.shape
    return pl.pallas_call(
        payload_kernel,
        out_shape=(
            jax.ShapeDtypeStruct((rows, width), jnp.bfloat16),
            jax.ShapeDtypeStruct((members, rows + 16, width), jnp.bfloat16),
        ),
        compiler_params=SMALL,
        name="make_payload",
    )(query, mixed, gain.reshape(rows, 1))


def feed_kernel(
    sizes, core_ref, sent_ref, weight_ref, p0_ref, p1_ref, p2_ref, p3_ref, out_ref,
    x_ref, scale_ref, hidden_ref, flat_ref, piece_ref, piece_sem,
):
    units, block, per_step, first_steps = sizes
    step = pl.program_id(0)
    members, rows = sent_ref.shape[0], out_ref.shape[2]
    core = core_ref[0]
    length = p0_ref.shape[0]
    copies = []
    for index, ref in enumerate((p0_ref, p1_ref, p2_ref, p3_ref)):
        slot = 2 * (index // 2) + (core if index % 2 == 0 else 1 - core)
        target = piece_ref.at[pl.ds(pl.multiple_of(slot * length, 16), length), :]
        copies.append(pltpu.make_async_copy(ref, target, piece_sem.at[index]))

    @pl.when(step == 0)
    def _():
        for copy in copies:
            copy.start()
        squares = jnp.zeros((1, x_ref.shape[1]), jnp.float32)
        for member in range(members):
            x_ref[member * rows : (member + 1) * rows, :] = sent_ref[member, :rows, :]
            extra = sent_ref[member, rows:, :].astype(jnp.float32)
            squares = squares + (extra[0:1] + extra[1:2] + extra[2:3])
        scale = lax.rsqrt(squares / (members * rows) + EPSILON)
        scale_ref[...] = jnp.broadcast_to(scale, scale_ref.shape)

    @pl.when(step < first_steps)
    def _():
        scale = scale_ref[0:1, :]
        sums = jnp.dot(weight_ref[...], x_ref[...], preferred_element_type=jnp.float32) * scale
        height = weight_ref.shape[0] // per_step
        for index in range(per_step):
            part = sums[index * height : (index + 1) * height]
            for side in range(2):
                base = 2 * side * units
                gate, up = part[base : base + units], part[base + units : base + 2 * units]
                value = gate / (1.0 + jnp.exp(-gate)) * up
                blank = jnp.zeros((block - units, value.shape[1]), jnp.float32)
                start = (2 * side + index % 2) * length
                start += (step * (per_step // 2) + index // 2) * block
                hidden_ref[pl.ds(pl.multiple_of(start, 8), block), :] = jnp.concatenate(
                    [value, blank], axis=0
                )

    @pl.when(step == first_steps)
    def _():
        for copy in copies:
            copy.wait()
        flat_ref[...] = hidden_ref[...].T.astype(jnp.bfloat16)

    @pl.when(step >= first_steps)
    def _():
        wide = out_ref.shape[0] * rows
        start = pl.multiple_of((step - first_steps) * wide, LANES)
        total = jnp.dot(
            flat_ref[...], piece_ref[:, pl.ds(start, wide)], preferred_element_type=jnp.float32
        )
        for member in range(out_ref.shape[0]):
            out_ref[member] = total[:, member * rows : (member + 1) * rows].astype(jnp.bfloat16)


def feed_forward(sent, weights, pieces, core, units):
    members, padded, width = sent.shape
    channels = weights.shape[1]
    rows = channels // members
    length = pieces[0].shape[0]
    block = units + -units % 8
    blocks = 2 * length // block
    per_step, out_step = 8, 4
    first_steps = blocks // per_step
    anywhere = pl.BlockSpec(memory_space=pl.ANY)
    return pl.pallas_call(
        functools.partial(feed_kernel, (units, block, per_step, first_steps)),
        grid=(first_steps + members // out_step,),
        out_shape=jax.ShapeDtypeStruct((members, width, rows), jnp.bfloat16),
        in_specs=[
            pl.BlockSpec(memory_space=pltpu.SMEM),
            pl.BlockSpec(memory_space=pltpu.VMEM),
            pl.BlockSpec(
                (weights.shape[0] // first_steps, channels),
                lambda i: (jnp.minimum(i, first_steps - 1), 0),
            ),
            anywhere,
            anywhere,
            anywhere,
            anywhere,
        ],
        out_specs=pl.BlockSpec(
            (out_step, width, rows), lambda i: (jnp.maximum(i - first_steps, 0), 0, 0)
        ),
        scratch_shapes=[
            pltpu.VMEM((channels, width), jnp.bfloat16),
            pltpu.VMEM((8, width), jnp.float32),
            pltpu.VMEM((4 * length, width), jnp.float32),
            pltpu.VMEM((width, 4 * length), jnp.bfloat16),
            pltpu.VMEM((4 * length, channels), jnp.bfloat16),
            pltpu.SemaphoreType.DMA((4,)),
        ],
        compiler_params=pltpu.CompilerParams(vmem_limit_bytes=52 * 1024 * 1024),
        cost_estimate=pl.CostEstimate(flops=10**10, bytes_accessed=3 * 10**7, transcendentals=0),
        name="feed_forward",
    )(core, sent, weights, *pieces)


def finish_kernel(shares_ref, hyena_ref, out_ref):
    total = shares_ref[0].astype(jnp.float32)
    for member in range(1, shares_ref.shape[0]):
        total = total + shares_ref[member].astype(jnp.float32)
    out_ref[...] = (hyena_ref[...].astype(jnp.float32) + total.T).astype(jnp.bfloat16)


def finish(shares, hyena):
    return pl.pallas_call(
        finish_kernel,
        out_shape=jax.ShapeDtypeStruct(hyena.shape, jnp.bfloat16),
        compiler_params=SMALL,
        name="finish",
    )(shares, hyena)


def swap(values, axis):
    return lax.ppermute(values, axis, [(0, 1), (1, 0)])


def per_device(
    projected, filter_taps, short_weight, skip_bias, norm_gain, gate_weight, up_weight, down_weight
):
    groups = lax.axis_size(SEQ)
    members = lax.axis_size(TP)
    local_width, block_len = filter_taps.shape
    per_group = local_width // groups
    seq_len = groups * block_len
    offset = lax.axis_index(SEQ) * per_group
    bias_part = lax.dynamic_slice_in_dim(skip_bias, offset, per_group, 0)

    pair = pack_rows(gate_weight, up_weight)
    own_near = lax.all_gather(pad_rows(down_weight), "z", axis=0, tiled=True)
    edge = projected[:, :, block_len - 2 :].transpose(0, 2, 1).reshape(6, local_width)
    edge = lax.ppermute(
        jnp.pad(edge, ((0, 2), (0, 0))), SEQ, [(i, i + 1) for i in range(groups - 1)]
    )
    taps = lax.all_to_all(
        filter_taps.reshape(groups, per_group, block_len),
        SEQ,
        split_axis=0,
        concat_axis=0,
        tiled=True,
    )
    gated, query = make_gated(projected, short_weight, edge)
    other_pair = swap(pair, "xh")
    second = pack_rows(pair, other_pair)
    gated, taps, second, bias_part = lax.optimization_barrier((gated, taps, second, bias_part))
    here = lax.all_to_all(
        gated.reshape(groups, per_group, block_len), SEQ, split_axis=0, concat_axis=0, tiled=True
    )

    core = lax.axis_index("core")
    gate_up = lax.all_gather(second, ("z", "core"), axis=0, tiled=True)

    here, own_near = lax.optimization_barrier((here, own_near))
    own_far = swap(own_near, "core")
    near = swap(own_near, "xh")
    taps = taps.transpose(1, 0, 2).reshape(per_group, seq_len)
    mixed_term = long_mixing(here.transpose(1, 0, 2), taps, bias_part)
    mixed_term, own_far = lax.optimization_barrier((mixed_term, own_far))
    returned = lax.all_to_all(
        mixed_term.transpose(1, 0, 2), SEQ, split_axis=0, concat_axis=0, tiled=True
    )
    gain = lax.dynamic_slice_in_dim(
        norm_gain, lax.axis_index(TP) * local_width, local_width, 0
    )
    hyena, payload = make_payload(query, returned.reshape(local_width, block_len), gain, members)
    payload, near = lax.optimization_barrier((payload, near))
    pieces = (own_near, own_far, near, swap(near, "core"))
    sent = lax.all_to_all(payload, TP, split_axis=0, concat_axis=0, tiled=True)
    partial_sum = feed_forward(sent, gate_up, pieces, core.reshape(1), gate_weight.shape[0])
    shares = lax.all_to_all(partial_sum, TP, split_axis=0, concat_axis=0, tiled=True)
    return finish(shares, hyena)


def solution(mesh):
    fine = Mesh(mesh.devices.reshape(2, 8, 2, 4, 2), SEQ + TP)
    placed = (
        P(None, TP, SEQ),
        P(TP, SEQ),
        P(None, TP, None),
        P(TP),
        P(),
        P(SEQ + TP, None),
        P(SEQ + TP, None),
        P(SEQ + TP, None),
    )
    return jax.shard_map(
        per_device, mesh=fine, in_specs=placed, out_specs=P(TP, SEQ), check_vma=False
    )
```

```python
import functools

import jax
import jax.numpy as jnp
from jax import lax
from jax.experimental import pallas as pl
from jax.experimental.pallas import tpu as pltpu
from jax.sharding import Mesh
from jax.sharding import PartitionSpec as P

EPSILON = 1e-06
LANES = 128
SEQ = ("xh", "z", "core")
TP = ("y", "xl")
SMALL = pltpu.CompilerParams(vmem_limit_bytes=12 * 1024 * 1024)


def gate_kernel(projected_ref, weight_ref, edge_ref, gated_ref, query_ref):
    rows, width = query_ref.shape
    weights = weight_ref[...].T
    edges = edge_ref[...].astype(jnp.float32).T
    lane = lax.broadcasted_iota(jnp.int32, (rows, width), 1)
    shorts = []
    for index in range(3):
        value = projected_ref[index].astype(jnp.float32)
        far, near = edges[:, 2 * index : 2 * index + 1], edges[:, 2 * index + 1 : 2 * index + 2]
        once = jnp.where(lane == 0, near, pltpu.roll(value, 1, 1))
        twice = jnp.where(lane == 0, far, jnp.where(lane == 1, near, pltpu.roll(value, 2, 1)))
        taps = [weights[:, 3 * index + tap : 3 * index + tap + 1] for tap in range(3)]
        shorts.append(taps[0] * value + taps[1] * once + taps[2] * twice)
    query_ref[...] = shorts[0]
    gated_ref[...] = (shorts[1] * shorts[2]).astype(jnp.bfloat16)


def make_gated(projected, short_weight, edge):
    count, rows, width = projected.shape
    weights = short_weight.transpose(0, 2, 1).reshape(9, rows)
    return pl.pallas_call(
        gate_kernel,
        out_shape=(
            jax.ShapeDtypeStruct((rows, width), jnp.bfloat16),
            jax.ShapeDtypeStruct((rows, width), jnp.float32),
        ),
        compiler_params=SMALL,
        name="make_gated",
    )(projected, jnp.pad(weights, ((0, 7), (0, 0))), edge)


def pack_first_kernel(gate_ref, up_ref, down_ref, first_ref, pair_ref):
    gate, up = gate_ref[...].astype(jnp.float32), up_ref[...].astype(jnp.float32)
    down = down_ref[...].astype(jnp.float32)
    blank = jnp.zeros((first_ref.shape[0] - down.shape[0], down.shape[1]), jnp.float32)
    first_ref[...] = jnp.concatenate([down, blank], axis=0).astype(jnp.bfloat16)
    pair_ref[...] = jnp.concatenate([gate, up], axis=0).astype(jnp.bfloat16)


def pack_first(gate, up, down):
    rows, width = gate.shape
    return pl.pallas_call(
        pack_first_kernel,
        out_shape=(
            jax.ShapeDtypeStruct((rows + -rows % 8, width), gate.dtype),
            jax.ShapeDtypeStruct((2 * rows, width), gate.dtype),
        ),
        name="pack_first",
    )(gate, up, down)


def pack_second_kernel(pair_ref, other_ref, out_ref):
    pair, other = pair_ref[...].astype(jnp.float32), other_ref[...].astype(jnp.float32)
    out_ref[...] = jnp.concatenate([pair, other], axis=0).astype(jnp.bfloat16)


def pack_second(pair, other):
    return pl.pallas_call(
        pack_second_kernel,
        out_shape=jax.ShapeDtypeStruct((2 * pair.shape[0], pair.shape[1]), pair.dtype),
        compiler_params=SMALL,
        name="pack_second",
    )(pair, other)


def build_table(taps_ref, channel, table_ref):
    seq_len = taps_ref.shape[2]
    taps = jnp.broadcast_to(taps_ref[channel].astype(jnp.float32), (8, seq_len))
    base = jnp.concatenate([taps, jnp.zeros((8, LANES), jnp.float32)], axis=1)
    base = pltpu.roll(base, 0, 1, stride=1, stride_axis=0)
    base = jnp.concatenate([base, pltpu.roll(base, 8, 1)], axis=0).astype(jnp.bfloat16)
    for shift in range(0, LANES, 16):
        moved = pltpu.roll(base, shift, 1) if shift else base
        table_ref[shift : shift + 16, :] = moved[:, :seq_len]


def apply_table(gated_ref, bias_ref, channel, table_ref, out_ref):
    rows = gated_ref.shape[1]
    gated = gated_ref[channel].astype(jnp.float32)
    tiles = rows // 8
    left = []
    for skip in range(tiles):
        keep = rows - 8 * skip
        left.append(jnp.concatenate([gated[:keep, :LANES], gated[:keep, LANES:]], axis=0).astype(jnp.bfloat16))
    zero = jnp.zeros((8, LANES), jnp.float32)
    total = [[zero] * tiles, [zero] * tiles]
    row = lax.broadcasted_iota(jnp.int32, (rows, LANES), 0)
    carried = [zero] * tiles
    for rho in range(8):
        sums = [carried, [zero] * tiles]
        carried = [zero] * tiles
        for skip in range(tiles):
            step = 8 * skip + rho
            keep = rows - 8 * skip
            part = jnp.dot(left[skip], table_ref[:, 2 * LANES * step : 2 * LANES * (step + 1)], preferred_element_type=jnp.float32)
            for lane_half in range(2):
                for row_half in range(2):
                    move = (2 * step + lane_half + row_half) // 2
                    if move >= rows: continue
                    side = (lane_half + row_half) % 2
                    target = sums[side] if move == step else carried
                    first = move // 8
                    for tile in range(tiles - first):
                        start = row_half * keep + 8 * tile
                        target[tile + first] = target[tile + first] + part[start:start + 8, lane_half * LANES:(lane_half + 1) * LANES]
        for side in range(2):
            if rho == 0:
                moved = sums[side]
            else:
                moved = jnp.concatenate(sums[side], axis=0)
                moved = jnp.where(row >= rho, pltpu.roll(moved, rho, 0), 0.0)
                moved = [moved[8*t:8*t+8] for t in range(tiles)]
            total[side] = [a + b for a, b in zip(total[side], moved)]
    total[0] = [a + b for a, b in zip(total[0], carried)]
    whole = jnp.concatenate([jnp.concatenate(total[0], axis=0), jnp.concatenate(total[1], axis=0)], axis=1)
    out_ref[channel] = (whole + bias_ref[channel] * gated).astype(jnp.bfloat16)

def conv_kernel(bias_ref, gated_ref, taps_ref, out_ref, even_ref, odd_ref):
    channels = gated_ref.shape[0]
    build_table(taps_ref, 0, even_ref)
    def body(step, carry):
        channel = 2 * step
        build_table(taps_ref, channel + 1, odd_ref)
        apply_table(gated_ref, bias_ref, channel, even_ref, out_ref)
        build_table(taps_ref, lax.rem(channel + 2, channels), even_ref)
        apply_table(gated_ref, bias_ref, channel + 1, odd_ref, out_ref)
        return carry
    lax.fori_loop(0, channels // 2, body, 0)

def long_mixing(gated, taps, bias):
    channels, rows, width = gated.shape
    seq_len = rows * width
    return pl.pallas_call(conv_kernel,
        out_shape=jax.ShapeDtypeStruct(gated.shape, jnp.bfloat16),
        in_specs=[pl.BlockSpec(memory_space=pltpu.SMEM), pl.BlockSpec(memory_space=pltpu.VMEM), pl.BlockSpec(memory_space=pltpu.VMEM)],
        out_specs=pl.BlockSpec(memory_space=pltpu.VMEM),
        scratch_shapes=[pltpu.VMEM((LANES, seq_len), jnp.bfloat16)]*2,
        compiler_params=pltpu.CompilerParams(vmem_limit_bytes=24*1024*1024),
        cost_estimate=pl.CostEstimate(flops=8 * channels * seq_len * seq_len, bytes_accessed=6*channels*seq_len, transcendentals=0),
        name="long_mixing")(bias, gated, taps.reshape(channels, 1, seq_len))


def payload_kernel(query_ref, mixed_ref, gain_ref, hyena_ref, out_ref):
    rows = query_ref.shape[0]
    hyena = (query_ref[...] * mixed_ref[...].astype(jnp.float32)).astype(jnp.bfloat16)
    hyena_ref[...] = hyena
    wide = hyena.astype(jnp.float32)
    scaled = (wide * gain_ref[...]).astype(jnp.bfloat16)
    rest = jnp.sum(wide * wide, axis=0, keepdims=True)
    place = lax.broadcasted_iota(jnp.int32, (out_ref.shape[1] - rows, wide.shape[1]), 0)
    extra = jnp.zeros(place.shape, jnp.float32)
    for index in range(3):
        part = rest.astype(jnp.bfloat16).astype(jnp.float32)
        extra = jnp.where(place == index, part, extra)
        rest = rest - part
    for member in range(out_ref.shape[0]):
        out_ref[member, :rows, :] = scaled
        out_ref[member, rows:, :] = extra.astype(jnp.bfloat16)


def make_payload(query, mixed, gain, members):
    rows, width = query.shape
    return pl.pallas_call(
        payload_kernel,
        out_shape=(
            jax.ShapeDtypeStruct((rows, width), jnp.bfloat16),
            jax.ShapeDtypeStruct((members, rows + 16, width), jnp.bfloat16),
        ),
        compiler_params=SMALL,
        name="make_payload",
    )(query, mixed, gain.reshape(rows, 1))


def feed_kernel(
    sizes, core_ref, sent_ref, weight_ref, p0_ref, p1_ref, p2_ref, p3_ref, out_ref,
    x_ref, scale_ref, hidden_ref, flat_ref, piece_ref, piece_sem,
):
    units, block, per_step, first_steps = sizes
    step = pl.program_id(0)
    members, rows = sent_ref.shape[0], out_ref.shape[2]
    core = core_ref[0]
    length = p0_ref.shape[0]
    copies = []
    for index, ref in enumerate((p0_ref, p1_ref, p2_ref, p3_ref)):
        slot = 2 * (index // 2) + (core if index % 2 == 0 else 1 - core)
        target = piece_ref.at[pl.ds(pl.multiple_of(slot * length, 16), length), :]
        copies.append(pltpu.make_async_copy(ref, target, piece_sem.at[index]))

    @pl.when(step == 0)
    def _():
        for copy in copies:
            copy.start()
        squares = jnp.zeros((1, x_ref.shape[1]), jnp.float32)
        for member in range(members):
            x_ref[member * rows : (member + 1) * rows, :] = sent_ref[member, :rows, :]
            extra = sent_ref[member, rows:, :].astype(jnp.float32)
            squares = squares + (extra[0:1] + extra[1:2] + extra[2:3])
        scale = lax.rsqrt(squares / (members * rows) + EPSILON)
        scale_ref[...] = jnp.broadcast_to(scale, scale_ref.shape)

    @pl.when(step < first_steps)
    def _():
        scale = scale_ref[0:1, :]
        sums = jnp.dot(weight_ref[...], x_ref[...], preferred_element_type=jnp.float32) * scale
        height = weight_ref.shape[0] // per_step
        for index in range(per_step):
            part = sums[index * height : (index + 1) * height]
            for side in range(2):
                base = 2 * side * units
                gate, up = part[base : base + units], part[base + units : base + 2 * units]
                value = gate / (1.0 + jnp.exp(-gate)) * up
                blank = jnp.zeros((block - units, value.shape[1]), jnp.float32)
                start = (2 * side + index % 2) * length
                start += (step * (per_step // 2) + index // 2) * block
                hidden_ref[pl.ds(pl.multiple_of(start, 8), block), :] = jnp.concatenate(
                    [value, blank], axis=0
                )

    @pl.when(step == first_steps)
    def _():
        for copy in copies:
            copy.wait()
        flat_ref[...] = hidden_ref[...].T.astype(jnp.bfloat16)

    @pl.when(step >= first_steps)
    def _():
        wide = out_ref.shape[0] * rows
        start = pl.multiple_of((step - first_steps) * wide, LANES)
        total = jnp.dot(
            flat_ref[...], piece_ref[:, pl.ds(start, wide)], preferred_element_type=jnp.float32
        )
        for member in range(out_ref.shape[0]):
            out_ref[member] = total[:, member * rows : (member + 1) * rows].astype(jnp.bfloat16)


def feed_forward(sent, weights, pieces, core, units):
    members, padded, width = sent.shape
    channels = weights.shape[1]
    rows = channels // members
    length = pieces[0].shape[0]
    block = units + -units % 8
    blocks = 2 * length // block
    per_step, out_step = 8, 4
    first_steps = blocks // per_step
    anywhere = pl.BlockSpec(memory_space=pl.ANY)
    return pl.pallas_call(
        functools.partial(feed_kernel, (units, block, per_step, first_steps)),
        grid=(first_steps + members // out_step,),
        out_shape=jax.ShapeDtypeStruct((members, width, rows), jnp.bfloat16),
        in_specs=[
            pl.BlockSpec(memory_space=pltpu.SMEM),
            pl.BlockSpec(memory_space=pltpu.VMEM),
            pl.BlockSpec(
                (weights.shape[0] // first_steps, channels),
                lambda i: (jnp.minimum(i, first_steps - 1), 0),
            ),
            anywhere,
            anywhere,
            anywhere,
            anywhere,
        ],
        out_specs=pl.BlockSpec(
            (out_step, width, rows), lambda i: (jnp.maximum(i - first_steps, 0), 0, 0)
        ),
        scratch_shapes=[
            pltpu.VMEM((channels, width), jnp.bfloat16),
            pltpu.VMEM((8, width), jnp.float32),
            pltpu.VMEM((4 * length, width), jnp.float32),
            pltpu.VMEM((width, 4 * length), jnp.bfloat16),
            pltpu.VMEM((4 * length, channels), jnp.bfloat16),
            pltpu.SemaphoreType.DMA((4,)),
        ],
        compiler_params=pltpu.CompilerParams(vmem_limit_bytes=52 * 1024 * 1024),
        cost_estimate=pl.CostEstimate(flops=10**10, bytes_accessed=3 * 10**7, transcendentals=0),
        name="feed_forward",
    )(core, sent, weights, *pieces)


def finish_kernel(shares_ref, hyena_ref, out_ref):
    total = shares_ref[0].astype(jnp.float32)
    for member in range(1, shares_ref.shape[0]):
        total = total + shares_ref[member].astype(jnp.float32)
    out_ref[...] = (hyena_ref[...].astype(jnp.float32) + total.T).astype(jnp.bfloat16)


def finish(shares, hyena):
    return pl.pallas_call(
        finish_kernel,
        out_shape=jax.ShapeDtypeStruct(hyena.shape, jnp.bfloat16),
        compiler_params=SMALL,
        name="finish",
    )(shares, hyena)


def swap(values, axis):
    return lax.ppermute(values, axis, [(0, 1), (1, 0)])


def per_device(
    projected, filter_taps, short_weight, skip_bias, norm_gain, gate_weight, up_weight, down_weight
):
    groups = lax.axis_size(SEQ)
    members = lax.axis_size(TP)
    local_width, block_len = filter_taps.shape
    per_group = local_width // groups
    seq_len = groups * block_len
    offset = lax.axis_index(SEQ) * per_group
    bias_part = lax.dynamic_slice_in_dim(skip_bias, offset, per_group, 0)

    first, pair = pack_first(gate_weight, up_weight, down_weight)
    own_near = lax.all_gather(first, "z", axis=0, tiled=True)
    edge = projected[:, :, block_len - 2 :].transpose(0, 2, 1).reshape(6, local_width)
    edge = lax.ppermute(
        jnp.pad(edge, ((0, 2), (0, 0))), SEQ, [(i, i + 1) for i in range(groups - 1)]
    )
    taps = lax.all_to_all(
        filter_taps.reshape(groups, per_group, block_len),
        SEQ,
        split_axis=0,
        concat_axis=0,
        tiled=True,
    )
    gated, query = make_gated(projected, short_weight, edge)
    other_pair = swap(pair, "xh")
    second = pack_second(pair, other_pair)
    gated, taps, second, bias_part = lax.optimization_barrier((gated, taps, second, bias_part))
    here = lax.all_to_all(
        gated.reshape(groups, per_group, block_len), SEQ, split_axis=0, concat_axis=0, tiled=True
    )

    core = lax.axis_index("core")
    gate_up = lax.all_gather(second, ("z", "core"), axis=0, tiled=True)

    here, own_near = lax.optimization_barrier((here, own_near))
    near = swap(own_near, "xh")
    taps = taps.transpose(1, 0, 2).reshape(per_group, seq_len)
    mixed_term = long_mixing(here.transpose(1, 0, 2), taps, bias_part)
    returned = lax.all_to_all(
        mixed_term.transpose(1, 0, 2), SEQ, split_axis=0, concat_axis=0, tiled=True
    )
    gain = lax.dynamic_slice_in_dim(
        norm_gain, lax.axis_index(TP) * local_width, local_width, 0
    )
    hyena, payload = make_payload(query, returned.reshape(local_width, block_len), gain, members)
    payload, near, own_near = lax.optimization_barrier((payload, near, own_near))
    pieces = (own_near, swap(own_near, "core"), near, swap(near, "core"))
    sent = lax.all_to_all(payload, TP, split_axis=0, concat_axis=0, tiled=True)
    partial_sum = feed_forward(sent, gate_up, pieces, core.reshape(1), gate_weight.shape[0])
    shares = lax.all_to_all(partial_sum, TP, split_axis=0, concat_axis=0, tiled=True)
    return finish(shares, hyena)


def solution(mesh):
    fine = Mesh(mesh.devices.reshape(2, 8, 2, 4, 2), SEQ + TP)
    placed = (
        P(None, TP, SEQ),
        P(TP, SEQ),
        P(None, TP, None),
        P(TP),
        P(),
        P(SEQ + TP, None),
        P(SEQ + TP, None),
        P(SEQ + TP, None),
    )
    return jax.shard_map(
        per_device, mesh=fine, in_specs=placed, out_specs=P(TP, SEQ), check_vma=False
    )
```
